32 devices in a mesh: row: 4 (over x, core), col: 8 (over z, y).
Axes of the slice: x: 2, y: 2, z: 4, core: 2. Of those that a mesh axis runs over, the one named last changes fastest.
Arguments:
- valence: bfloat16 [2, 16, 32768], replicated, may hold values from -6 to 6
- conduction: bfloat16 [2, 128, 32768], replicated, may hold values from -6 to 6
- valence_energy: float32 [16], replicated, may hold values from -8 to -1
- conduction_energy: float32 [128], replicated, may hold values from 0.5 to 6
- band_pairs: int32 [1024, 2], P(('row', 'col')), may hold values from 0 to 127, as said below
- grid_index: int32 [16384], replicated, may hold values from 0 to 32767, as said below
Outputs:
- response: float32 [2, 16384, 16384], P(None, 'row', 'col')
The draws below stay inside these ranges and needn't reach their ends.
Inputs may be any that keep to these rules, and one draw needn't show every extreme that they name: `band_pairs`: the rows are distinct combinations of a valence band below 16 and a conduction band below 128, half of all combinations. `grid_index`: the 16384 entries are distinct.
All inputs are finite; a program needn't handle non-finite values.
Results may differ from the reference program's by a relative error of at most 0.0039.
Values may be sent and summed in bfloat16 or wider, within the bound.
No kernel may reach another device: no remote copies, remote signals or barrier semaphores. Data moves between devices by JAX's collectives and lax.ppermute only.
A program may use at most 256 MiB of HBM per device.

```python
import math
import jax
import jax.numpy as jnp
from jax import lax

NG = 16384
N1 = 32
N2 = 32
N3 = 32
NVB = 16
NCB = 128
NR = 32768


def draw_band_pairs(key, part):
    combos = NVB * NCB
    target = NCB - 1
    others = jax.random.permutation(key, combos - 1).astype(jnp.int32)
    others = jnp.where(others >= target, others + 1, others)
    chosen = jnp.concatenate([jnp.array([target], dtype=jnp.int32), others[:NVB * NCB // 2 - 1]])
    chosen = jax.random.permutation(jax.random.fold_in(key, 5), chosen).astype(jnp.int32)
    return jnp.stack([chosen // NCB, chosen % NCB], axis=1).astype(jnp.int32)


def draw_grid_index(key, part):
    inner = 1 + jax.random.permutation(jax.random.fold_in(key, 11), NR - 2)[:NG - 2]
    ends = jnp.array([0, NR - 1], dtype=jnp.int32)
    joined = jnp.concatenate([ends, inner.astype(jnp.int32)])
    shuffled = jax.random.permutation(jax.random.fold_in(key, 23), joined)
    return shuffled.astype(jnp.int32)


def gaussian(stream_key, dims, spread, limit, kind=jnp.bfloat16):
    return jnp.clip(spread * jax.random.normal(stream_key, dims, jnp.float32), -limit, limit).astype(kind)


def setup_inputs(seed: int = 0) -> dict:
    seeds = jax.random.split(jax.random.key(seed), 7)
    return {
        "valence": gaussian(seeds[0], (2, NVB, NR), 0.7071, 6.0),
        "conduction": gaussian(seeds[1], (2, NCB, NR), 0.7071, 6.0),
        "valence_energy": jnp.clip(jax.random.uniform(seeds[2], (NVB,), jnp.float32, -8.0, -1.0), -8.0, -1.0),
        "conduction_energy": jnp.clip(jax.random.uniform(seeds[3], (NCB,), jnp.float32, 0.5, 6.0), 0.5, 6.0),
        "band_pairs": draw_band_pairs(jax.random.fold_in(seeds[6], 71), 0),
        "grid_index": draw_grid_index(jax.random.fold_in(seeds[6], 71), 0),
    }


def tables(length):
    position = jnp.arange(length, dtype=jnp.int32)
    phase_angle = (position[:, None] * position[None, :] % length).astype(jnp.float32) * (2.0 * math.pi / length)
    return (jnp.cos(phase_angle), jnp.sin(phase_angle))

def transform(real_part, imag_part):
    for pattern, length in (('pabr,kr->pabk', N3), ('parc,kr->pakc', N2), ('prbc,kr->pkbc', N1)):
        cosine, sine_table = tables(length)
        new_real = jnp.einsum(pattern, real_part, cosine, precision=lax.Precision.HIGHEST) + jnp.einsum(pattern, imag_part, sine_table, precision=lax.Precision.HIGHEST)
        new_imag = jnp.einsum(pattern, imag_part, cosine, precision=lax.Precision.HIGHEST) - jnp.einsum(pattern, real_part, sine_table, precision=lax.Precision.HIGHEST)
        real_part, imag_part = (new_real, new_imag)
    return (real_part, imag_part)

def pair_spectrum(valence, conduction, valence_energy, conduction_energy, band_pairs):
    pair_count = band_pairs.shape[0]
    valence_rows = jnp.take(valence, band_pairs[:, 0], axis=1).astype(jnp.float32)
    conduction_rows = jnp.take(conduction, band_pairs[:, 1], axis=1).astype(jnp.float32)
    rho_real = valence_rows[0] * conduction_rows[0] + valence_rows[1] * conduction_rows[1]
    rho_imag = valence_rows[0] * conduction_rows[1] - valence_rows[1] * conduction_rows[0]
    grid_shape = (pair_count, N1, N2, N3)
    out_real, out_imag = transform(rho_real.reshape(grid_shape), rho_imag.reshape(grid_shape))
    normalize = 1.0 / math.sqrt(N1 * N2 * N3)
    spectrum = jnp.stack([out_real.reshape(pair_count, -1), out_imag.reshape(pair_count, -1)]) * normalize
    valence_hot = band_pairs[:, 0][:, None] == jnp.arange(valence_energy.shape[0], dtype=jnp.int32)[None, :]
    conduction_hot = band_pairs[:, 1][:, None] == jnp.arange(conduction_energy.shape[0], dtype=jnp.int32)[None, :]
    energy_gap = lax.optimization_barrier(jnp.sum(jnp.where(valence_hot, valence_energy[None, :], 0.0), axis=1)) - lax.optimization_barrier(jnp.sum(jnp.where(conduction_hot, conduction_energy[None, :], 0.0), axis=1))
    weights = 2.0 / (math.sqrt(NVB * NCB // 2) * energy_gap)
    return (spectrum, weights)

def contract(weighted_part, operand, crossed):
    contract_dims = (((0, 1), (0, 1)), ((), ()))
    real_part = lax.dot_general(weighted_part, operand, contract_dims, preferred_element_type=jnp.float32)
    imag_part = lax.dot_general(weighted_part, crossed, contract_dims, preferred_element_type=jnp.float32)
    return jnp.stack([real_part, imag_part])

def reference(valence, conduction, valence_energy, conduction_energy, band_pairs, grid_index):
    spectrum, weights = pair_spectrum(valence, conduction, valence_energy, conduction_energy, band_pairs)
    selected = jnp.take(spectrum, grid_index, axis=2)
    weighted = (weights[None, :, None] * selected).astype(jnp.bfloat16)
    density = selected.astype(jnp.bfloat16)
    crossed = jnp.stack([density[1], -density[0]])
    vector_count = grid_index.shape[0]
    block_width = math.gcd(vector_count, 1024)
    pair_count = weighted.shape[1]
    pieces = weighted.reshape(2, pair_count, vector_count // block_width, block_width).transpose(2, 0, 1, 3)

    def one_block(row_block):
        return contract(row_block, density, crossed)
    result = lax.map(one_block, pieces)
    return result.transpose(1, 0, 2, 3).reshape(2, vector_count, vector_count)
```

```python
import math

import jax
import jax.numpy as jnp
import ml_dtypes
import numpy as np
from jax import lax
from jax.experimental import pallas as pl
from jax.experimental.pallas import tpu as pltpu
from jax.sharding import PartitionSpec as P

N1 = 32
N2 = 32
N3 = 32
NR = N1 * N2 * N3
LANES = 128
HI = N2 * N3 // LANES
LO = N2 // HI
ROWS = N1 * HI
VMEM_LIMIT = 58 * 1024 * 1024
CHUNKS = (2, 2, 2, 1, 1)


def split_bf16(values):
    high = values.astype(ml_dtypes.bfloat16)
    low = (values - high.astype(np.float64)).astype(ml_dtypes.bfloat16)
    return high, low


def dft_tables():
    row = np.arange(ROWS)
    left = np.exp(
        -2j
        * np.pi
        * (
            (row[:, None] // HI) * (row[None, :] // HI) / N1
            + (row[:, None] % HI) * (row[None, :] % HI) / HI
        )
    )
    lane = np.arange(LANES)
    right = np.exp(
        -2j
        * np.pi
        * (
            (lane[:, None] // N3) * (lane[None, :] // N3) / LO
            + (lane[:, None] % N3) * (lane[None, :] % N3) / N3
        )
    )
    twiddle = np.exp(-2j * np.pi * (row[:, None] % HI) * (lane[None, :] // N3) / N2)
    twiddle = twiddle / math.sqrt(NR)
    left_high, left_low = split_bf16(np.concatenate([left.real, left.imag], axis=0))
    right_full = np.concatenate(
        [
            np.concatenate([right.real, right.imag], axis=1),
            np.concatenate([-right.imag, right.real], axis=1),
        ],
        axis=0,
    )
    right_high, right_low = split_bf16(right_full)
    return (
        np.concatenate([left_high, left_low], axis=0),
        right_high,
        right_low,
        np.stack([twiddle.real, twiddle.imag]).astype(np.float32),
    )


def table_position(grid_index):
    first = grid_index // (N2 * N3)
    second = grid_index // N3 % N2
    third = grid_index % N3
    return (first * HI + second % HI) * LANES + second // HI * N3 + third


def halves(value):
    high = value.astype(jnp.bfloat16)
    low = (value - high.astype(jnp.float32)).astype(jnp.bfloat16)
    return high, low


def dot(a, b):
    return jnp.dot(a, b, preferred_element_type=jnp.float32)


def transform_kernel(
    pairs,
    load_steps,
    step_rows,
    out_rows,
    hot_c_ref,
    hot_v_ref,
    cond_ref,
    val_ref,
    left_ref,
    right_high_ref,
    right_low_ref,
    twiddle_ref,
    out_ref,
    rho_r,
    rho_i,
    spec,
):
    step = pl.program_id(0)
    features = 2 * pairs

    @pl.when(step < load_steps)
    def _():
        cond = dot(hot_c_ref[...], cond_ref[...])
        val = dot(hot_v_ref[...], val_ref[...])
        cr, ci = cond[:pairs], cond[pairs:]
        vr, vi = val[:pairs], val[pairs:]
        real = vr * cr + vi * ci
        imag = vr * ci - vi * cr
        for a in range(step_rows):
            row = pl.multiple_of((step * step_rows + a) * pairs, pairs)
            rho_r[pl.ds(row, pairs), :] = real[:, a * LANES : (a + 1) * LANES]
            rho_i[pl.ds(row, pairs), :] = imag[:, a * LANES : (a + 1) * LANES]

    @pl.when(step == load_steps)
    def _():
        def one_pair(p, carry):
            data = jnp.concatenate(
                [
                    rho_r[pl.ds(p, ROWS, stride=pairs), :],
                    rho_i[pl.ds(p, ROWS, stride=pairs), :],
                ],
                axis=1,
            )
            high, low = halves(data)
            by_high = dot(left_ref[...], high)
            by_low = dot(left_ref[0 : 2 * ROWS, :], low)
            mixed = by_high[: 2 * ROWS] + (by_high[2 * ROWS :] + by_low)
            mid_r = mixed[:ROWS, :LANES] - mixed[ROWS:, LANES:]
            mid_i = mixed[:ROWS, LANES:] + mixed[ROWS:, :LANES]
            tr, ti = twiddle_ref[0], twiddle_ref[1]
            turned = jnp.concatenate([mid_r * tr - mid_i * ti, mid_r * ti + mid_i * tr], axis=1)
            high, low = halves(turned)
            out = dot(high, right_high_ref[...]) + (
                dot(low, right_high_ref[...]) + dot(high, right_low_ref[...])
            )
            spec[pl.ds(p, ROWS, stride=features), :] = out[:, :LANES]
            spec[pl.ds(pairs + p, ROWS, stride=features), :] = out[:, LANES:]
            return carry

        lax.fori_loop(0, pairs, one_pair, 0, unroll=2)

    @pl.when(step >= load_steps)
    def _():
        block = step - load_steps

        def one_row(k, carry):
            start = pl.multiple_of((block * out_rows + k) * features, features)
            tile = spec[pl.ds(start, features), :]
            tile = jnp.concatenate([tile] * (LANES // features), axis=0)
            out_ref[pl.ds(pl.multiple_of(k * LANES, LANES), LANES), :] = tile.T
            return carry

        lax.fori_loop(0, out_rows, one_row, 0, unroll=4)


def transform(valence, conduction, band_pairs):
    pairs = band_pairs.shape[0]
    nvb, ncb = valence.shape[1], conduction.shape[1]
    load_steps, out_steps = 8, 8
    step_rows = ROWS // load_steps
    out_rows = ROWS // out_steps
    chunk = step_rows * LANES

    def hot(band, count):
        one = (band[:, None] == jnp.arange(count, dtype=jnp.int32)[None, :]).astype(jnp.bfloat16)
        return jnp.kron(jnp.eye(2, dtype=jnp.bfloat16), one)

    left, right_high, right_low, twiddle = dft_tables()
    whole = lambda shape: pl.BlockSpec(shape, lambda i: (0,) * len(shape))
    loaded = lambda i: (0, jnp.minimum(i, load_steps - 1))
    flops = 2 * pairs * (6 * ROWS * ROWS * 2 * LANES + 3 * ROWS * 4 * LANES * LANES)
    return pl.pallas_call(
        lambda *refs: transform_kernel(pairs, load_steps, step_rows, out_rows, *refs),
        grid=(load_steps + out_steps,),
        in_specs=[
            whole((2 * pairs, 2 * ncb)),
            whole((2 * pairs, 2 * nvb)),
            pl.BlockSpec((2 * ncb, chunk), loaded),
            pl.BlockSpec((2 * nvb, chunk), loaded),
            whole(left.shape),
            whole(right_high.shape),
            whole(right_low.shape),
            whole(twiddle.shape),
        ],
        out_specs=pl.BlockSpec(
            (out_rows * LANES, LANES), lambda i: (jnp.maximum(i - load_steps, 0), 0)
        ),
        out_shape=jax.ShapeDtypeStruct((NR, LANES), jnp.float32),
        scratch_shapes=[
            pltpu.VMEM((ROWS * pairs, LANES), jnp.float32),
            pltpu.VMEM((ROWS * pairs, LANES), jnp.float32),
            pltpu.VMEM((ROWS * 2 * pairs, LANES), jnp.float32),
        ],
        compiler_params=pltpu.CompilerParams(vmem_limit_bytes=VMEM_LIMIT),
        cost_estimate=pl.CostEstimate(flops=flops, bytes_accessed=40_000_000, transcendentals=0),
        name="transform",
    )(
        hot(band_pairs[:, 1], ncb),
        hot(band_pairs[:, 0], nvb),
        conduction.reshape(2 * ncb, NR),
        valence.reshape(2 * nvb, NR),
        jnp.asarray(left),
        jnp.asarray(right_high),
        jnp.asarray(right_low),
        jnp.asarray(twiddle),
    )


def select_kernel(row_count, features, count, position_ref, me_ref, table_ref, *rest):
    outs, rows = rest[:row_count], rest[row_count]
    pack = LANES // features
    part = count // pack
    lane = lax.broadcasted_iota(jnp.int32, (part, LANES), 1)
    unroll = 32
    for s in range(row_count):
        base = (me_ref[0] ^ s) * count

        def some_rows(step, carry):
            start = step * unroll
            for j in range(unroll):
                index = position_ref[base + start + j]
                rows[pl.ds(start + j, 1), :] = table_ref[pl.ds(index, 1), :]
            return carry

        lax.fori_loop(0, count // unroll, some_rows, 0)
        packed = rows[0:part, :]
        for k in range(1, pack):
            packed = jnp.where(lane >= k * features, rows[k * part : (k + 1) * part, :], packed)
        outs[s][...] = packed.astype(jnp.bfloat16)


def select(table, position, me, row_count, features):
    count = position.shape[0] // row_count
    pack = LANES // features
    shape = (count // pack, LANES)
    return pl.pallas_call(
        lambda *refs: select_kernel(row_count, features, count, *refs),
        grid_spec=pltpu.PrefetchScalarGridSpec(
            num_scalar_prefetch=2,
            grid=(),
            in_specs=[pl.BlockSpec(memory_space=pltpu.VMEM)],
            out_specs=[pl.BlockSpec(memory_space=pltpu.VMEM)] * row_count,
            scratch_shapes=[pltpu.VMEM((count, LANES), jnp.float32)],
        ),
        out_shape=[jax.ShapeDtypeStruct(shape, jnp.bfloat16)] * row_count,
        compiler_params=pltpu.CompilerParams(vmem_limit_bytes=VMEM_LIMIT),
        cost_estimate=pl.CostEstimate(flops=0, bytes_accessed=20_000_000, transcendentals=0),
        name="select",
    )(position, me, table)


def assemble_kernel(row_count, features, me_ref, *rest):
    parts, out_ref, held = rest[:row_count], rest[row_count], rest[row_count + 1]
    pack = LANES // features
    part = parts[0].shape[0]
    lane = lax.broadcasted_iota(jnp.int32, (part, LANES), 1)
    for s in range(row_count):
        held[s] = parts[s][...].astype(jnp.float32)
    for b in range(row_count // pack):
        for k in range(pack):
            block = None
            for q in range(pack):
                piece = held[(b * pack + q) ^ me_ref[0]]
                if q != k:
                    piece = pltpu.roll(piece, (q - k) * features % LANES, 1)
                block = piece if block is None else jnp.where(lane >= q * features, piece, block)
            out_ref[k * part : (k + 1) * part, b * LANES : (b + 1) * LANES] = block.astype(
                jnp.bfloat16
            )


def assemble(parts, me, features):
    row_count = len(parts)
    pack = LANES // features
    part = parts[0].shape[0]
    return pl.pallas_call(
        lambda *refs: assemble_kernel(row_count, features, *refs),
        grid_spec=pltpu.PrefetchScalarGridSpec(
            num_scalar_prefetch=1,
            grid=(),
            in_specs=[pl.BlockSpec(memory_space=pltpu.VMEM)] * row_count,
            out_specs=pl.BlockSpec(memory_space=pltpu.VMEM),
            scratch_shapes=[pltpu.VMEM((row_count, part, LANES), jnp.float32)],
        ),
        out_shape=jax.ShapeDtypeStruct((part * pack, row_count * features), jnp.bfloat16),
        compiler_params=pltpu.CompilerParams(vmem_limit_bytes=VMEM_LIMIT),
        cost_estimate=pl.CostEstimate(flops=0, bytes_accessed=2_000_000, transcendentals=0),
        name="assemble",
    )(me, *parts)


def flip_kernel(slot_count, part_ref, *rest):
    slots, out_ref = rest[:slot_count], rest[slot_count]
    width = slots[0].shape[1]
    for s in range(slot_count):
        out_ref[s * width : (s + 1) * width, :] = (
            slots[s][...].astype(jnp.float32).T.astype(jnp.bfloat16)
        )


def flip(slots, part, depth):
    slot_count = len(slots)
    width = slots[0].shape[1]
    tile = min(256, depth)
    steps = depth // tile
    pick = lambda t, part_ref: (part_ref[0] * steps + t, 0)
    return pl.pallas_call(
        lambda *refs: flip_kernel(slot_count, *refs),
        grid_spec=pltpu.PrefetchScalarGridSpec(
            num_scalar_prefetch=1,
            grid=(steps,),
            in_specs=[pl.BlockSpec((tile, width), pick)] * slot_count,
            out_specs=pl.BlockSpec((slot_count * width, tile), lambda t, part_ref: (0, t)),
        ),
        out_shape=jax.ShapeDtypeStruct((slot_count * width, depth), jnp.bfloat16),
        compiler_params=pltpu.CompilerParams(vmem_limit_bytes=VMEM_LIMIT),
        cost_estimate=pl.CostEstimate(
            flops=0, bytes_accessed=8 * slot_count * width * depth, transcendentals=0
        ),
        name="flip",
    )(part, *slots)


def contract_kernel(slot_count, pairs, aliased, *refs):
    slots = refs[:slot_count]
    weight_ref, column_ref = refs[slot_count : slot_count + 2]
    out_ref, weighted, crossed = refs[slot_count + 2 + aliased :]
    width = slots[0].shape[1]

    @pl.when(pl.program_id(0) == 0)
    def _():
        for s in range(slot_count):
            rows = slice(s * width, (s + 1) * width)
            values = column_ref[rows, :].astype(jnp.float32)
            values = values.reshape(width // (2 * pairs), 2, pairs, values.shape[1])
            turned = jnp.stack([values[:, 1], -values[:, 0]], axis=1)
            crossed[rows, :] = turned.reshape(width, values.shape[3]).astype(jnp.bfloat16)

    for s in range(slot_count):
        weighted[:, s * width : (s + 1) * width] = (
            slots[s][...].astype(jnp.float32) * weight_ref[s : s + 1, :]
        ).astype(jnp.bfloat16)
    out_ref[0, 0] = dot(weighted[...], column_ref[...])
    out_ref[1, 0] = dot(weighted[...], crossed[...])


def contract(result, slots, weights, column, pairs, parts, block, row_start, column_start):
    slot_count = len(slots)
    width = slots[0].shape[1]
    depth = slots[0].shape[0] // parts
    across = column.shape[1]
    shape = (2, parts, block, block)
    aliased = 0 if result is None else 1
    place = (row_start // depth, column_start // across)
    whole = lambda shape: pl.BlockSpec(shape, lambda h: (0, 0))
    return pl.pallas_call(
        lambda *refs: contract_kernel(slot_count, pairs, aliased, *refs),
        grid=(parts,),
        in_specs=[pl.BlockSpec((depth, width), lambda h: (h, 0))] * slot_count
        + [whole(weights.shape), whole(column.shape)]
        + [pl.BlockSpec(memory_space=pl.ANY)] * aliased,
        out_specs=pl.BlockSpec((2, 1, depth, across), lambda h: (0, h) + place),
        out_shape=jax.ShapeDtypeStruct(shape, jnp.float32),
        scratch_shapes=[
            pltpu.VMEM((depth, slot_count * width), jnp.bfloat16),
            pltpu.VMEM(column.shape, jnp.bfloat16),
        ],
        input_output_aliases={slot_count + 2: 0} if aliased else {},
        compiler_params=pltpu.CompilerParams(vmem_limit_bytes=VMEM_LIMIT),
        cost_estimate=pl.CostEstimate(
            flops=4 * parts * depth * across * slot_count * width,
            bytes_accessed=8 * parts * depth * across + 2 * parts * depth * slot_count * width,
            transcendentals=0,
        ),
        name="contract",
    )(*slots, weights, column, *([result] if aliased else []))


def pair_weights(valence_energy, conduction_energy, band_pairs):
    valence_hot = (
        band_pairs[:, 0][:, None] == jnp.arange(valence_energy.shape[0], dtype=jnp.int32)[None, :]
    )
    conduction_hot = (
        band_pairs[:, 1][:, None]
        == jnp.arange(conduction_energy.shape[0], dtype=jnp.int32)[None, :]
    )
    energy_gap = jnp.sum(jnp.where(valence_hot, valence_energy[None, :], 0.0), axis=1) - jnp.sum(
        jnp.where(conduction_hot, conduction_energy[None, :], 0.0), axis=1
    )
    return energy_gap


def body(valence, conduction, valence_energy, conduction_energy, band_pairs, grid_index):
    rows, cols = lax.axis_size("row"), lax.axis_size("col")
    row, col = lax.axis_index("row"), lax.axis_index("col")
    pairs = band_pairs.shape[0]
    features = 2 * pairs
    total = grid_index.shape[0]
    block = total // cols
    parts = cols // rows
    me = row.astype(jnp.int32).reshape(1)
    my_part = (col % parts).astype(jnp.int32).reshape(1)
    owner = col // parts

    order = list(range(0, cols, 2)) + list(range(1, cols, 2))[::-1]
    ring_up = [(order[q], order[(q + 1) % cols]) for q in range(cols)]
    ring_down = [(b, a) for a, b in ring_up]
    place = np.argsort(np.array(order))
    my_place = jnp.asarray(place, jnp.int32)[col]
    half = cols // 2
    offsets = [0]
    for t in range(1, half):
        offsets += [-t, t]
    offsets.append(half)
    sources = jnp.asarray(np.array(order), jnp.int32)[
        (my_place + jnp.asarray(np.array(offsets), jnp.int32)) % cols
    ]

    gap = pair_weights(valence_energy, conduction_energy, band_pairs)
    weight = 2.0 / (math.sqrt(pairs * rows * cols) * gap)
    weights = lax.all_gather(weight, ("row", "col"), axis=0, tiled=True)
    weights = jnp.take(weights.reshape(rows, cols, pairs).transpose(1, 0, 2), sources, axis=0)
    weights = jnp.broadcast_to(weights[:, :, None, :], (cols, rows, 2, pairs))
    weights = weights.reshape(cols, rows * features)

    position = table_position(grid_index).reshape(rows, parts, block)
    table = transform(valence, conduction, band_pairs)

    unit = block // sum(CHUNKS)
    starts = [sum(CHUNKS[:i]) * unit for i in range(len(CHUNKS))]
    chunks, columns = [], []
    result = None
    for start, share in zip(starts, CHUNKS):
        depth = share * unit
        wanted = position[:, :, start : start + depth].reshape(-1)
        sent = select(table, wanted, me, rows, features)
        got = [sent[0]] + [
            lax.ppermute(sent[s], "row", [(r, r ^ s) for r in range(rows)])
            for s in range(1, rows)
        ]
        own = assemble(got, me, features)
        slots = [own]
        up = down = own
        for _ in range(1, half):
            up = lax.ppermute(up, "col", ring_up)
            down = lax.ppermute(down, "col", ring_down)
            slots += [up, down]
        cut = own.shape[0] // 2
        slots.append(
            jnp.concatenate(
                [
                    lax.ppermute(up[:cut], "col", ring_up),
                    lax.ppermute(down[cut:], "col", ring_down),
                ],
                axis=0,
            )
        )
        column = flip(slots, my_part, depth)
        holders = [0]
        step = rows // 2
        while step:
            perm = [
                ((c // parts ^ h) * cols + c, (c // parts ^ h ^ step) * cols + c)
                for c in range(cols)
                for h in holders
            ]
            arrived = lax.ppermute(column, ("row", "col"), perm)
            column = jnp.where((row ^ owner) & step != 0, arrived, column)
            holders += [h ^ step for h in holders]
            step //= 2
        i = len(chunks)
        chunks.append(slots)
        columns.append(column)
        tiles = [(i, j) for j in range(i)] + [(j, i) for j in range(i + 1)]
        for a, b in tiles:
            result = contract(
                result, chunks[a], weights, columns[b], pairs, parts, block, starts[a], starts[b]
            )
    return result.reshape(2, parts * block, block)


def solution(mesh):
    return jax.shard_map(
        body,
        mesh=mesh,
        in_specs=(P(), P(), P(), P(), P(("row", "col"), None), P()),
        out_specs=P(None, "row", "col"),
        check_vma=False,
    )
```

```python
import math

import jax
import jax.numpy as jnp
import ml_dtypes
import numpy as np
from jax import lax
from jax.experimental import pallas as pl
from jax.experimental.pallas import tpu as pltpu
from jax.sharding import PartitionSpec as P

N1 = 32
N2 = 32
N3 = 32
NR = N1 * N2 * N3
LANES = 128
HI = N2 * N3 // LANES
LO = N2 // HI
ROWS = N1 * HI
VMEM_LIMIT = 58 * 1024 * 1024
CHUNKS = ((3, 1), (4, 4), (0, 3))
EIGHTHS = 8


def split_bf16(values):
    high = values.astype(ml_dtypes.bfloat16)
    low = (values - high.astype(np.float64)).astype(ml_dtypes.bfloat16)
    return high, low


def dft_tables():
    row = np.arange(ROWS)
    left = np.exp(
        -2j
        * np.pi
        * (
            (row[:, None] // HI) * (row[None, :] // HI) / N1
            + (row[:, None] % HI) * (row[None, :] % HI) / HI
        )
    )
    lane = np.arange(LANES)
    right = np.exp(
        -2j
        * np.pi
        * (
            (lane[:, None] // N3) * (lane[None, :] // N3) / LO
            + (lane[:, None] % N3) * (lane[None, :] % N3) / N3
        )
    )
    twiddle = np.exp(-2j * np.pi * (row[:, None] % HI) * (lane[None, :] // N3) / N2)
    twiddle = twiddle / math.sqrt(NR)
    left_full = np.block([[left.real, -left.imag], [left.imag, left.real]])
    right_full = np.block([[right.real, right.imag], [-right.imag, right.real]])
    left_high, left_low = split_bf16(left_full)
    right_high, right_low = split_bf16(right_full)
    twiddle = np.concatenate([twiddle, twiddle], axis=1)
    return (
        np.concatenate([left_high, left_low, left_high], axis=1),
        np.concatenate([right_high, right_high, right_low], axis=0),
        np.stack([twiddle.real, twiddle.imag]).astype(np.float32),
    )


def table_position(grid_index):
    first = grid_index // (N2 * N3)
    second = grid_index // N3 % N2
    third = grid_index % N3
    return (first * HI + second % HI) * LANES + second // HI * N3 + third


def halves(value):
    high = value.astype(jnp.bfloat16)
    low = (value - high.astype(jnp.float32)).astype(jnp.bfloat16)
    return high, low


def dot(a, b):
    return jnp.dot(a, b, preferred_element_type=jnp.float32)


def select_rows(shapes, row_count, features, position_ref, me_ref, table, rows, outs):
    pack = LANES // features
    unroll = 32
    start = 0
    for i, count in enumerate(shapes):
        part = count // pack
        lane = lax.broadcasted_iota(jnp.int32, (part, LANES), 1)
        for s in range(row_count):
            base = start + (me_ref[0] ^ s) * count

            def some_rows(step, carry):
                first = step * unroll
                for j in range(unroll):
                    index = position_ref[base + first + j]
                    rows[pl.ds(first + j, 1), :] = table[pl.ds(index, 1), :]
                return carry

            lax.fori_loop(0, count // unroll, some_rows, 0)
            packed = rows[0:part, :]
            for k in range(1, pack):
                packed = jnp.where(lane >= k * features, rows[k * part : (k + 1) * part, :], packed)
            outs[i * row_count + s][...] = packed.astype(jnp.bfloat16)
        start += row_count * count


def transform_kernel(pairs, load_steps, step_rows, shapes, row_count, *refs):
    position_ref, me_ref, hot_c_ref, hot_v_ref, cond_ref, val_ref = refs[:6]
    left_ref, right_ref, twiddle_ref = refs[6:9]
    outs = refs[9 : 9 + len(shapes) * row_count]
    rho_r, rho_i, spec, table, middle, rows = refs[9 + len(shapes) * row_count :]
    step = pl.program_id(0)
    features = 2 * pairs

    cond = dot(hot_c_ref[...], cond_ref[...])
    val = dot(hot_v_ref[...], val_ref[...])
    cr, ci = cond[:pairs], cond[pairs:]
    vr, vi = val[:pairs], val[pairs:]
    real = vr * cr + vi * ci
    imag = vr * ci - vi * cr
    for a in range(step_rows):
        row = pl.multiple_of((step * step_rows + a) * pairs, pairs)
        rho_r[pl.ds(row, pairs), :] = real[:, a * LANES : (a + 1) * LANES]
        rho_i[pl.ds(row, pairs), :] = imag[:, a * LANES : (a + 1) * LANES]

    def left_half(group, slot):
        one, two = 2 * group, 2 * group + 1
        data = jnp.concatenate(
            [
                jnp.concatenate([ref[pl.ds(p, ROWS, stride=pairs), :] for p in (one, two)], axis=1)
                for ref in (rho_r, rho_i)
            ],
            axis=0,
        )
        high, low = halves(data)
        mixed = dot(left_ref[...], jnp.concatenate([high, high, low], axis=0))
        mid_r, mid_i = mixed[:ROWS], mixed[ROWS:]
        tr, ti = twiddle_ref[0], twiddle_ref[1]
        turn_r = mid_r * tr - mid_i * ti
        turn_i = mid_r * ti + mid_i * tr
        turned = jnp.concatenate(
            [
                jnp.concatenate([turn_r[:, :LANES], turn_i[:, :LANES]], axis=1),
                jnp.concatenate([turn_r[:, LANES:], turn_i[:, LANES:]], axis=1),
            ],
            axis=0,
        )
        high, low = halves(turned)
        middle[slot, :, : 2 * LANES] = high
        middle[slot, :, 2 * LANES :] = low

    def right_half(group, slot):
        high = middle[slot, :, : 2 * LANES]
        low = middle[slot, :, 2 * LANES :]
        out = dot(jnp.concatenate([high, low, high], axis=1), right_ref[...])
        for k in range(2):
            p = 2 * group + k
            part = out[k * ROWS : (k + 1) * ROWS]
            spec[pl.ds(p, ROWS, stride=features), :] = part[:, :LANES]
            spec[pl.ds(pairs + p, ROWS, stride=features), :] = part[:, LANES:]

    @pl.when(step == load_steps - 1)
    def _():
        groups = pairs // 2
        left_half(0, 0)

        def two_groups(k, carry):
            right_half(2 * k, 0)
            left_half(2 * k + 1, 1)
            right_half(2 * k + 1, 1)
            left_half(jnp.minimum(2 * k + 2, groups - 1), 0)
            return carry

        lax.fori_loop(0, groups // 2, two_groups, 0)

        def one_row(k, carry):
            start = pl.multiple_of(k * features, features)
            tile = spec[pl.ds(start, features), :].astype(jnp.bfloat16)
            tile = jnp.concatenate([tile] * (LANES // features), axis=0)
            table[pl.ds(pl.multiple_of(k * LANES, LANES), LANES), :] = tile.T.astype(jnp.float32)
            return carry

        lax.fori_loop(0, ROWS, one_row, 0, unroll=8)
        select_rows(shapes, row_count, features, position_ref, me_ref, table, rows, outs)


def transform(valence, conduction, band_pairs, position, me, shapes, row_count):
    pairs = band_pairs.shape[0]
    features = 2 * pairs
    pack = LANES // features
    nvb, ncb = valence.shape[1], conduction.shape[1]
    load_steps = 8
    step_rows = ROWS // load_steps
    chunk = step_rows * LANES

    def hot(band, count):
        one = (band[:, None] == jnp.arange(count, dtype=jnp.int32)[None, :]).astype(jnp.bfloat16)
        none = jnp.zeros_like(one)
        return jnp.concatenate(
            [jnp.concatenate([one, none], axis=1), jnp.concatenate([none, one], axis=1)], axis=0
        )

    left, right, twiddle = dft_tables()
    whole = lambda shape: pl.BlockSpec(shape, lambda i, *_: (0,) * len(shape))
    loaded = lambda i, *_: (0, i)
    flops = 2 * pairs * (6 * ROWS * ROWS * 2 * LANES + 3 * ROWS * 4 * LANES * LANES)
    out_shapes = [(count // pack, LANES) for count in shapes for _ in range(row_count)]
    outs = pl.pallas_call(
        lambda *refs: transform_kernel(pairs, load_steps, step_rows, shapes, row_count, *refs),
        grid_spec=pltpu.PrefetchScalarGridSpec(
            num_scalar_prefetch=2,
            grid=(load_steps,),
            in_specs=[
                whole((2 * pairs, 2 * ncb)),
                whole((2 * pairs, 2 * nvb)),
                pl.BlockSpec((2 * ncb, chunk), loaded),
                pl.BlockSpec((2 * nvb, chunk), loaded),
                whole(left.shape),
                whole(right.shape),
                whole(twiddle.shape),
            ],
            out_specs=[whole(shape) for shape in out_shapes],
            scratch_shapes=[
                pltpu.VMEM((ROWS * pairs, LANES), jnp.float32),
                pltpu.VMEM((ROWS * pairs, LANES), jnp.float32),
                pltpu.VMEM((ROWS * features, LANES), jnp.float32),
                pltpu.VMEM((NR, LANES), jnp.float32),
                pltpu.VMEM((2, 2 * ROWS, 4 * LANES), jnp.bfloat16),
                pltpu.VMEM((max(shapes), LANES), jnp.float32),
            ],
        ),
        out_shape=[jax.ShapeDtypeStruct(shape, jnp.bfloat16) for shape in out_shapes],
        compiler_params=pltpu.CompilerParams(vmem_limit_bytes=VMEM_LIMIT),
        cost_estimate=pl.CostEstimate(flops=flops, bytes_accessed=40_000_000, transcendentals=0),
        name="transform",
    )(
        position,
        me,
        hot(band_pairs[:, 1], ncb),
        hot(band_pairs[:, 0], nvb),
        conduction.reshape(2 * ncb, NR),
        valence.reshape(2 * nvb, NR),
        jnp.asarray(left),
        jnp.asarray(right),
        jnp.asarray(twiddle),
    )
    return [outs[i * row_count : (i + 1) * row_count] for i in range(len(shapes))]


def assemble_kernel(row_count, features, me_ref, *rest):
    parts, out_ref, held = rest[:row_count], rest[row_count], rest[row_count + 1]
    pack = LANES // features
    part = parts[0].shape[0]
    lane = lax.broadcasted_iota(jnp.int32, (part, LANES), 1)
    for s in range(row_count):
        held[s] = parts[s][...].astype(jnp.float32)
    for b in range(row_count // pack):
        for k in range(pack):
            block = None
            for q in range(pack):
                piece = held[(b * pack + q) ^ me_ref[0]]
                if q != k:
                    piece = pltpu.roll(piece, (q - k) * features % LANES, 1)
                block = piece if block is None else jnp.where(lane >= q * features, piece, block)
            out_ref[k * part : (k + 1) * part, b * LANES : (b + 1) * LANES] = block.astype(
                jnp.bfloat16
            )


def assemble(parts, me, features):
    row_count = len(parts)
    pack = LANES // features
    part = parts[0].shape[0]
    return pl.pallas_call(
        lambda *refs: assemble_kernel(row_count, features, *refs),
        grid_spec=pltpu.PrefetchScalarGridSpec(
            num_scalar_prefetch=1,
            grid=(),
            in_specs=[pl.BlockSpec(memory_space=pltpu.VMEM)] * row_count,
            out_specs=pl.BlockSpec(memory_space=pltpu.VMEM),
            scratch_shapes=[pltpu.VMEM((row_count, part, LANES), jnp.float32)],
        ),
        out_shape=jax.ShapeDtypeStruct((part * pack, row_count * features), jnp.bfloat16),
        compiler_params=pltpu.CompilerParams(vmem_limit_bytes=VMEM_LIMIT),
        cost_estimate=pl.CostEstimate(flops=0, bytes_accessed=2_000_000, transcendentals=0),
        name="assemble",
    )(me, *parts)


def flip_kernel(slot_count, part_ref, *rest):
    slots, out_ref = rest[:slot_count], rest[slot_count]
    width = slots[0].shape[1]
    for s in range(slot_count):
        out_ref[s * width : (s + 1) * width, :] = (
            slots[s][...].astype(jnp.float32).T.astype(jnp.bfloat16)
        )


def flip(slots, part, depth):
    slot_count = len(slots)
    width = slots[0].shape[1]
    tile = min(256, depth)
    steps = depth // tile
    pick = lambda t, part_ref: (part_ref[0] * steps + t, 0)
    return pl.pallas_call(
        lambda *refs: flip_kernel(slot_count, *refs),
        grid_spec=pltpu.PrefetchScalarGridSpec(
            num_scalar_prefetch=1,
            grid=(steps,),
            in_specs=[pl.BlockSpec((tile, width), pick)] * slot_count,
            out_specs=pl.BlockSpec((slot_count * width, tile), lambda t, part_ref: (0, t)),
        ),
        out_shape=jax.ShapeDtypeStruct((slot_count * width, depth), jnp.bfloat16),
        compiler_params=pltpu.CompilerParams(vmem_limit_bytes=VMEM_LIMIT),
        cost_estimate=pl.CostEstimate(
            flops=0, bytes_accessed=8 * slot_count * width * depth, transcendentals=0
        ),
        name="flip",
    )(part, *slots)


def settle_kernel(pairs, aliased, *refs):
    take_ref, kept_ref, arrived_ref = refs[:3]
    out_ref = refs[3 + aliased]
    kept = jnp.where(take_ref[0] != 0, arrived_ref[...], kept_ref[...])
    out_ref[0] = kept
    values = kept.astype(jnp.float32)
    rows, across = values.shape
    values = values.reshape(rows // (2 * pairs), 2, pairs, across)
    turned = jnp.stack([values[:, 1], -values[:, 0]], axis=1)
    out_ref[1] = turned.reshape(rows, across).astype(jnp.bfloat16)


def settle(held, take, kept, arrived, first_row, depth, pairs):
    rows, across = kept.shape
    tile = math.gcd(math.gcd(rows, first_row), 512)
    aliased = 0 if held is None else 1
    place = first_row // tile
    return pl.pallas_call(
        lambda *refs: settle_kernel(pairs, aliased, *refs),
        grid_spec=pltpu.PrefetchScalarGridSpec(
            num_scalar_prefetch=1,
            grid=(rows // tile,),
            in_specs=[pl.BlockSpec((tile, across), lambda t, _: (t, 0))] * 2
            + [pl.BlockSpec(memory_space=pl.ANY)] * aliased,
            out_specs=pl.BlockSpec((2, tile, across), lambda t, _: (0, place + t, 0)),
        ),
        out_shape=jax.ShapeDtypeStruct((2, depth, across), jnp.bfloat16),
        input_output_aliases={3: 0} if aliased else {},
        compiler_params=pltpu.CompilerParams(vmem_limit_bytes=VMEM_LIMIT),
        cost_estimate=pl.CostEstimate(
            flops=0, bytes_accessed=8 * rows * across, transcendentals=0
        ),
        name="settle",
    )(take, kept, arrived, *([held] if aliased else []))


def weigh_kernel(slot_count, *refs):
    slots, weight_ref, out_ref = refs[:slot_count], refs[slot_count], refs[slot_count + 1]
    width = slots[0].shape[1]
    for s in range(slot_count):
        out_ref[:, s * width : (s + 1) * width] = (
            slots[s][...].astype(jnp.float32) * weight_ref[s : s + 1, :]
        ).astype(jnp.bfloat16)


def weigh(slots, weights):
    slot_count = len(slots)
    count, width = slots[0].shape
    tile = math.gcd(count, 256)
    return pl.pallas_call(
        lambda *refs: weigh_kernel(slot_count, *refs),
        grid=(count // tile,),
        in_specs=[pl.BlockSpec((tile, width), lambda t: (t, 0))] * slot_count
        + [pl.BlockSpec(weights.shape, lambda t: (0, 0))],
        out_specs=pl.BlockSpec((tile, slot_count * width), lambda t: (t, 0)),
        out_shape=jax.ShapeDtypeStruct((count, slot_count * width), jnp.bfloat16),
        compiler_params=pltpu.CompilerParams(vmem_limit_bytes=VMEM_LIMIT),
        cost_estimate=pl.CostEstimate(
            flops=0, bytes_accessed=4 * count * slot_count * width, transcendentals=0
        ),
        name="weigh",
    )(*slots, weights)


def contract_kernel(left_spans, right_spans, aliased, *refs):
    lefts = refs[: len(left_spans)]
    rights = refs[len(left_spans) : len(left_spans) + len(right_spans)]
    out_ref = refs[len(left_spans) + len(right_spans) + aliased]
    column, row = pl.program_id(0), pl.program_id(1)

    def block(left_ref, right_ref):
        parts, unit, depth = left_ref.shape
        left = left_ref[...].reshape(parts * unit, depth)
        for z in range(2):
            out_ref[z] = dot(left, right_ref[z]).reshape(out_ref.shape[1:])

    for (left_start, left_count), left_ref in zip(left_spans, lefts):
        for (right_start, right_count), right_ref in zip(right_spans, rights):
            inside = (row >= left_start) & (row < left_start + left_count)
            inside &= (column >= right_start) & (column < right_start + right_count)
            pl.when(inside)(lambda left_ref=left_ref, right_ref=right_ref: block(left_ref, right_ref))


def contract(result, lefts, rights, unit, eighths):
    parts, _, depth = lefts[0][2].shape
    one = len(rights) == 1
    wide = 1
    if one:
        wide = 2 if rights[0][1] % 2 == 0 else rights[0][1]

    def spans(chunks, step):
        found, start = [], 0
        for _, count, _ in chunks:
            found.append((start, count // step))
            start += count // step
        return found, start

    left_spans, left_steps = spans(lefts, 1)
    right_spans, right_steps = spans(rights, wide)

    def inner(span):
        return lambda i: jnp.clip(i - span[0], 0, span[1] - 1)

    def outer(chunks, found, step):
        def place(i):
            answer = chunks[0][0] // step + i
            for (first, _, _), (start, _) in list(zip(chunks, found))[1:]:
                answer = jnp.where(i >= start, first // step + i - start, answer)
            return answer

        return place

    left_in = [inner(span) for span in left_spans]
    right_in = [inner(span) for span in right_spans]
    row_out, column_out = outer(lefts, left_spans, 1), outer(rights, right_spans, wide)
    aliased = 0 if result is None else 1
    flops = 8 * parts * left_steps * unit * right_steps * wide * unit * depth
    return pl.pallas_call(
        lambda *refs: contract_kernel(left_spans, right_spans, aliased, *refs),
        grid=(right_steps, left_steps),
        in_specs=[
            pl.BlockSpec((parts, unit, depth), lambda c, r, f=f: (0, f(r), 0)) for f in left_in
        ]
        + [
            pl.BlockSpec((2, depth, wide * unit), lambda c, r, f=f: (0, 0, f(c))) for f in right_in
        ]
        + [pl.BlockSpec(memory_space=pl.ANY)] * aliased,
        out_specs=pl.BlockSpec(
            (2, parts, unit, wide * unit), lambda c, r: (0, 0, row_out(r), column_out(c))
        ),
        out_shape=jax.ShapeDtypeStruct((2, parts, eighths * unit, eighths * unit), jnp.float32),
        input_output_aliases={len(lefts) + len(rights): 0} if aliased else {},
        compiler_params=pltpu.CompilerParams(vmem_limit_bytes=VMEM_LIMIT),
        cost_estimate=pl.CostEstimate(
            flops=flops, bytes_accessed=flops // depth + 4_000_000, transcendentals=0
        ),
        name="contract",
    )(*[a for _, _, a in lefts], *[a for _, _, a in rights], *([result] if aliased else []))


def energy_gaps(valence_energy, conduction_energy, band_pairs):
    valence_hot = (
        band_pairs[:, 0][:, None] == jnp.arange(valence_energy.shape[0], dtype=jnp.int32)[None, :]
    )
    conduction_hot = (
        band_pairs[:, 1][:, None]
        == jnp.arange(conduction_energy.shape[0], dtype=jnp.int32)[None, :]
    )
    return jnp.sum(jnp.where(valence_hot, valence_energy[None, :], 0.0), axis=1) - jnp.sum(
        jnp.where(conduction_hot, conduction_energy[None, :], 0.0), axis=1
    )


def after(value, *others):
    return lax.optimization_barrier((value,) + others)[0]


def body(valence, conduction, valence_energy, conduction_energy, band_pairs, grid_index):
    rows, cols = lax.axis_size("row"), lax.axis_size("col")
    row, col = lax.axis_index("row"), lax.axis_index("col")
    pairs = band_pairs.shape[0]
    features = 2 * pairs
    width = rows * features
    block = grid_index.shape[0] // cols
    parts = cols // rows
    unit = block // EIGHTHS
    me = row.astype(jnp.int32).reshape(1)
    my_part = (col % parts).astype(jnp.int32).reshape(1)
    owner = col // parts

    order = list(range(0, cols, 2)) + list(range(1, cols, 2))[::-1]
    ring_up = [(order[q], order[(q + 1) % cols]) for q in range(cols)]
    ring_down = [(b, a) for a, b in ring_up]
    my_place = jnp.asarray(np.argsort(np.array(order)), jnp.int32)[col]
    half = cols // 2
    offsets = [0]
    for t in range(1, half):
        offsets += [-t, t]
    offsets.append(half)
    sources = jnp.asarray(np.array(order), jnp.int32)[
        (my_place + jnp.asarray(np.array(offsets), jnp.int32)) % cols
    ]

    gap = energy_gaps(valence_energy, conduction_energy, band_pairs)
    weight = 2.0 / (math.sqrt(pairs * rows * cols) * gap)
    weight = jnp.broadcast_to(jnp.pad(weight, (0, LANES - pairs))[None, :], (8, LANES))
    weights = lax.all_gather(weight, ("row", "col"), axis=0, tiled=True)
    weights = weights.reshape(rows, cols, 8, LANES)[:, :, 0, :pairs].transpose(1, 0, 2)
    weights = jnp.take(weights, sources, axis=0)
    weights = jnp.broadcast_to(weights[:, :, None, :], (cols, rows, 2, pairs))
    weights = weights.reshape(cols, width)

    position = table_position(grid_index).reshape(rows, parts, EIGHTHS, unit)
    position = jnp.concatenate(
        [position[:, :, first : first + share].reshape(-1) for first, share in CHUNKS]
    )
    counts = [parts * share * unit for _, share in CHUNKS]
    sent = transform(valence, conduction, band_pairs, after(position, weight), me, counts, rows)
    me = after(me, weights)

    owns, moved = [], None
    for i in range(len(CHUNKS)):
        parcels = [sent[i][s] if moved is None else after(sent[i][s], moved) for s in range(rows)]
        got = parcels[:1] + [
            lax.ppermute(parcels[s], "row", [(r, r ^ s) for r in range(rows)])
            for s in range(1, rows)
        ]
        moved = got[-1]
        owns.append(assemble(got, me, features))

    def send_column(held, kept, first_row):
        holders, step = [0], rows // 2
        while step:
            perm = [
                ((c // parts ^ h) * cols + c, (c // parts ^ h ^ step) * cols + c)
                for c in range(cols)
                for h in holders
            ]
            arrived = lax.ppermute(kept, ("row", "col"), perm)
            take = (row ^ owner) & step != 0
            if step > 1:
                kept = jnp.where(take, arrived, kept)
            holders += [h ^ step for h in holders]
            step //= 2
        take = take.astype(jnp.int32).reshape(1)
        return settle(held, take, kept, arrived, first_row, cols * width, pairs)

    result, lefts, rights = None, [], []
    second = None
    for (first, share), own in zip(CHUNKS, owns):
        if second is not None:
            own = after(own, *second)
        groups = [[own]]
        up = down = own
        for t in range(1, half):
            up = lax.ppermute(up, "col", ring_up)
            down = lax.ppermute(down, "col", ring_down)
            if t == min(2, half - 1):
                second = (up, down)
            if t > 1 and share > 1:
                groups.append([])
            groups[-1] += [up, down]
        cut = own.shape[0] // 2
        groups[-1].append(
            jnp.concatenate(
                [
                    lax.ppermute(up[:cut], "col", ring_up),
                    lax.ppermute(down[cut:], "col", ring_down),
                ],
                axis=0,
            )
        )
        if share == 3:
            groups = [sum(groups[:-1], []), groups[-1]]
        held, first_row = None, 0
        for group in groups:
            if result is not None and group is groups[-1]:
                group = [after(group[0], result)] + group[1:]
            held = send_column(held, flip(group, my_part, share * unit), first_row)
            first_row += len(group) * width
        left = weigh(sum(groups, []), weights).reshape(parts, share * unit, cols * width)
        lefts.append((first, share, left))
        if rights:
            result = contract(result, lefts[-1:], rights, unit, EIGHTHS)
        rights.append((first, share, held))
        result = contract(result, lefts, rights[-1:], unit, EIGHTHS)
    return result.reshape(2, parts * block, block)


def solution(mesh):
    return jax.shard_map(
        body,
        mesh=mesh,
        in_specs=(P(), P(), P(), P(), P(("row", "col"), None), P()),
        out_specs=P(None, "row", "col"),
        check_vma=False,
    )
```

```python
import math

import jax
import jax.numpy as jnp
import ml_dtypes
import numpy as np
from jax import lax
from jax.experimental import pallas as pl
from jax.experimental.pallas import tpu as pltpu
from jax.sharding import PartitionSpec as P

N1 = 32
N2 = 32
N3 = 32
NR = N1 * N2 * N3
LANES = 128
HI = N2 * N3 // LANES
LO = N2 // HI
ROWS = N1 * HI
VMEM_LIMIT = 58 * 1024 * 1024
CHUNKS = ((0, 2), (2, 6))
EIGHTHS = 8
GROUP = 4


def split_bf16(values):
    high = values.astype(ml_dtypes.bfloat16)
    low = (values - high.astype(np.float64)).astype(ml_dtypes.bfloat16)
    return high, low


def dft_tables():
    row = np.arange(ROWS)
    left = np.exp(
        -2j
        * np.pi
        * (
            (row[:, None] // HI) * (row[None, :] // HI) / N1
            + (row[:, None] % HI) * (row[None, :] % HI) / HI
        )
    )
    lane = np.arange(LANES)
    right = np.exp(
        -2j
        * np.pi
        * (
            (lane[:, None] // N3) * (lane[None, :] // N3) / LO
            + (lane[:, None] % N3) * (lane[None, :] % N3) / N3
        )
    )
    twiddle = np.exp(-2j * np.pi * (row[:, None] % HI) * (lane[None, :] // N3) / N2)
    twiddle = twiddle / math.sqrt(NR)
    left_full = np.block([[left.real, -left.imag], [left.imag, left.real]])
    right_full = np.block([[right.real, right.imag], [-right.imag, right.real]])
    left_high, left_low = split_bf16(left_full)
    right_high, right_low = split_bf16(right_full)
    twiddle = np.concatenate([twiddle] * GROUP, axis=1)
    return (
        np.concatenate([left_high, left_low, left_high], axis=1),
        np.concatenate([right_high, right_low], axis=1),
        np.stack([twiddle.real, twiddle.imag]).astype(np.float32),
    )


def table_position(grid_index):
    first = grid_index // (N2 * N3)
    second = grid_index // N3 % N2
    third = grid_index % N3
    return (first * HI + second % HI) * LANES + second // HI * N3 + third


def halves(value):
    high = value.astype(jnp.bfloat16)
    low = (value - high.astype(jnp.float32)).astype(jnp.bfloat16)
    return high, low


def dot(a, b):
    return jnp.dot(a, b, preferred_element_type=jnp.float32)


def select_rows(shapes, row_count, features, position_ref, me_ref, table, rows, outs):
    pack = LANES // features
    unroll = 32
    start = 0
    for i, count in enumerate(shapes):
        part = count // pack
        lane = lax.broadcasted_iota(jnp.int32, (part, LANES), 1)
        for s in range(row_count):
            base = start + (me_ref[0] ^ s) * count

            def some_rows(step, carry):
                first = step * unroll
                for j in range(unroll):
                    index = position_ref[base + first + j]
                    rows[pl.ds(first + j, 1), :] = table[pl.ds(index, 1), :]
                return carry

            lax.fori_loop(0, count // unroll, some_rows, 0)
            packed = rows[0:part, :]
            for k in range(1, pack):
                packed = jnp.where(lane >= k * features, rows[k * part : (k + 1) * part, :], packed)
            outs[i * row_count + s][...] = packed.astype(jnp.bfloat16)
        start += row_count * count


def transform_kernel(pairs, load_steps, step_rows, shapes, row_count, *refs):
    position_ref, me_ref, hot_c_ref, hot_v_ref, scale_ref, cond_ref, val_ref = refs[:7]
    left_ref, right_ref, twiddle_ref = refs[7:10]
    outs = refs[10 : 10 + len(shapes) * row_count]
    rho_r, rho_i, spec, table, middle, rows = refs[10 + len(shapes) * row_count :]
    step = pl.program_id(0)
    features = 2 * pairs

    cond = dot(hot_c_ref[...], cond_ref[...])
    val = dot(hot_v_ref[...], val_ref[...]) * scale_ref[...]
    cr, ci = cond[:pairs], cond[pairs:]
    vr, vi = val[:pairs], val[pairs:]
    real = vr * cr + vi * ci
    imag = vr * ci - vi * cr
    for a in range(step_rows):
        row = pl.multiple_of((step * step_rows + a) * pairs, pairs)
        rho_r[pl.ds(row, pairs), :] = real[:, a * LANES : (a + 1) * LANES]
        rho_i[pl.ds(row, pairs), :] = imag[:, a * LANES : (a + 1) * LANES]

    def left_half(group, slot):
        members = [GROUP * group + k for k in range(GROUP)]
        data = jnp.concatenate(
            [
                jnp.concatenate([ref[pl.ds(p, ROWS, stride=pairs), :] for p in members], axis=1)
                for ref in (rho_r, rho_i)
            ],
            axis=0,
        )
        high, low = halves(data)
        mixed = dot(left_ref[...], jnp.concatenate([high, high, low], axis=0))
        mid_r, mid_i = mixed[:ROWS], mixed[ROWS:]
        tr, ti = twiddle_ref[0], twiddle_ref[1]
        turn_r = mid_r * tr - mid_i * ti
        turn_i = mid_r * ti + mid_i * tr
        for k in range(GROUP):
            lanes = slice(k * LANES, (k + 1) * LANES)
            rows_k = slice(k * ROWS, (k + 1) * ROWS)
            for z, turned in enumerate((turn_r, turn_i)):
                high, low = halves(turned[:, lanes])
                middle[slot, rows_k, z * LANES : (z + 1) * LANES] = high
                middle[slot, rows_k, (2 + z) * LANES : (3 + z) * LANES] = low

    def right_half(group, slot):
        high = middle[slot, :, : 2 * LANES]
        low = middle[slot, :, 2 * LANES :]
        by_high = dot(high, right_ref[...])
        by_low = dot(low, right_ref[:, : 2 * LANES])
        out = by_high[:, : 2 * LANES] + (by_high[:, 2 * LANES :] + by_low)
        for k in range(GROUP):
            p = GROUP * group + k
            part = out[k * ROWS : (k + 1) * ROWS]
            spec[pl.ds(p, ROWS, stride=features), :] = part[:, :LANES]
            spec[pl.ds(pairs + p, ROWS, stride=features), :] = part[:, LANES:]

    @pl.when(step == load_steps - 1)
    def _():
        groups = pairs // GROUP
        left_half(0, 0)

        def two_groups(k, carry):
            right_half(2 * k, 0)
            left_half(2 * k + 1, 1)
            right_half(2 * k + 1, 1)
            left_half(jnp.minimum(2 * k + 2, groups - 1), 0)
            return carry

        lax.fori_loop(0, groups // 2, two_groups, 0)

        def one_row(k, carry):
            start = pl.multiple_of(k * features, features)
            tile = spec[pl.ds(start, features), :].astype(jnp.bfloat16)
            tile = jnp.concatenate([tile] * (LANES // features), axis=0)
            table[pl.ds(pl.multiple_of(k * LANES, LANES), LANES), :] = tile.T.astype(jnp.float32)
            return carry

        lax.fori_loop(0, ROWS, one_row, 0, unroll=8)
        select_rows(shapes, row_count, features, position_ref, me_ref, table, rows, outs)


def transform(valence, conduction, band_pairs, scale, position, me, shapes, row_count):
    pairs = band_pairs.shape[0]
    features = 2 * pairs
    pack = LANES // features
    nvb, ncb = valence.shape[1], conduction.shape[1]
    load_steps = 8
    step_rows = ROWS // load_steps
    chunk = step_rows * LANES

    def hot(band, count):
        one = (band[:, None] == jnp.arange(count, dtype=jnp.int32)[None, :]).astype(jnp.bfloat16)
        none = jnp.zeros_like(one)
        return jnp.concatenate(
            [jnp.concatenate([one, none], axis=1), jnp.concatenate([none, one], axis=1)], axis=0
        )

    left, right, twiddle = dft_tables()
    whole = lambda shape: pl.BlockSpec(shape, lambda i, *_: (0,) * len(shape))
    loaded = lambda i, *_: (0, i)
    flops = 2 * pairs * (6 * ROWS * ROWS * 2 * LANES + 3 * ROWS * 4 * LANES * LANES)
    out_shapes = [(count // pack, LANES) for count in shapes for _ in range(row_count)]
    outs = pl.pallas_call(
        lambda *refs: transform_kernel(pairs, load_steps, step_rows, shapes, row_count, *refs),
        grid_spec=pltpu.PrefetchScalarGridSpec(
            num_scalar_prefetch=2,
            grid=(load_steps,),
            in_specs=[
                whole((2 * pairs, 2 * ncb)),
                whole((2 * pairs, 2 * nvb)),
                whole((2 * pairs, 1)),
                pl.BlockSpec((2 * ncb, chunk), loaded),
                pl.BlockSpec((2 * nvb, chunk), loaded),
                whole(left.shape),
                whole(right.shape),
                whole(twiddle.shape),
            ],
            out_specs=[whole(shape) for shape in out_shapes],
            scratch_shapes=[
                pltpu.VMEM((ROWS * pairs, LANES), jnp.float32),
                pltpu.VMEM((ROWS * pairs, LANES), jnp.float32),
                pltpu.VMEM((ROWS * features, LANES), jnp.float32),
                pltpu.VMEM((NR, LANES), jnp.float32),
                pltpu.VMEM((2, GROUP * ROWS, 4 * LANES), jnp.bfloat16),
                pltpu.VMEM((max(shapes), LANES), jnp.float32),
            ],
        ),
        out_shape=[jax.ShapeDtypeStruct(shape, jnp.bfloat16) for shape in out_shapes],
        compiler_params=pltpu.CompilerParams(vmem_limit_bytes=VMEM_LIMIT),
        cost_estimate=pl.CostEstimate(flops=flops, bytes_accessed=40_000_000, transcendentals=0),
        name="transform",
    )(
        position,
        me,
        hot(band_pairs[:, 1], ncb),
        hot(band_pairs[:, 0], nvb),
        jnp.concatenate([scale, scale])[:, None],
        conduction.reshape(2 * ncb, NR),
        valence.reshape(2 * nvb, NR),
        jnp.asarray(left),
        jnp.asarray(right),
        jnp.asarray(twiddle),
    )
    return [outs[i * row_count : (i + 1) * row_count] for i in range(len(shapes))]


def assemble_kernel(row_count, features, me_ref, *rest):
    parts, out_ref, held = rest[:row_count], rest[row_count], rest[row_count + 1]
    pack = LANES // features
    part = parts[0].shape[0]
    lane = lax.broadcasted_iota(jnp.int32, (part, LANES), 1)
    for s in range(row_count):
        held[s] = parts[s][...].astype(jnp.float32)
    for b in range(row_count // pack):
        for k in range(pack):
            block = None
            for q in range(pack):
                piece = held[(b * pack + q) ^ me_ref[0]]
                if q != k:
                    piece = pltpu.roll(piece, (q - k) * features % LANES, 1)
                block = piece if block is None else jnp.where(lane >= q * features, piece, block)
            out_ref[k * part : (k + 1) * part, b * LANES : (b + 1) * LANES] = block.astype(
                jnp.bfloat16
            )


def assemble(parts, me, features):
    row_count = len(parts)
    pack = LANES // features
    part = parts[0].shape[0]
    return pl.pallas_call(
        lambda *refs: assemble_kernel(row_count, features, *refs),
        grid_spec=pltpu.PrefetchScalarGridSpec(
            num_scalar_prefetch=1,
            grid=(),
            in_specs=[pl.BlockSpec(memory_space=pltpu.VMEM)] * row_count,
            out_specs=pl.BlockSpec(memory_space=pltpu.VMEM),
            scratch_shapes=[pltpu.VMEM((row_count, part, LANES), jnp.float32)],
        ),
        out_shape=jax.ShapeDtypeStruct((part * pack, row_count * features), jnp.bfloat16),
        compiler_params=pltpu.CompilerParams(vmem_limit_bytes=VMEM_LIMIT),
        cost_estimate=pl.CostEstimate(flops=0, bytes_accessed=2_000_000, transcendentals=0),
        name="assemble",
    )(me, *parts)


def spans(shares, step):
    found, start = [], 0
    for share in shares:
        found.append((start, share // step))
        start += share // step
    return found


def clipped(span, offset=0):
    return lambda i: offset + jnp.clip(i - span[0], 0, span[1] - 1)


def flip_kernel(slot_count, found, part_ref, *refs):
    out_ref = refs[-1]
    tile = pl.program_id(0)
    for k, (start, count) in enumerate(found):

        @pl.when((tile >= start) & (tile < start + count))
        def _():
            for s in range(slot_count):
                values = refs[k * slot_count + s][...]
                width = values.shape[1]
                out_ref[s * width : (s + 1) * width, :] = (
                    values.astype(jnp.float32).T.astype(jnp.bfloat16)
                )


def flip(chunks, shares, part, unit):
    slot_count = len(chunks[0])
    width = chunks[0][0].shape[1]
    found = spans(shares, 1)
    steps = sum(shares)

    def pick(span, share):
        place = clipped(span)
        return lambda t, part_ref: (part_ref[0] * share + place(t), 0)

    return pl.pallas_call(
        lambda *refs: flip_kernel(slot_count, found, *refs),
        grid_spec=pltpu.PrefetchScalarGridSpec(
            num_scalar_prefetch=1,
            grid=(steps,),
            in_specs=[
                pl.BlockSpec((unit, width), pick(span, share))
                for span, share in zip(found, shares)
                for _ in range(slot_count)
            ],
            out_specs=pl.BlockSpec((slot_count * width, unit), lambda t, part_ref: (0, t)),
        ),
        out_shape=jax.ShapeDtypeStruct((slot_count * width, steps * unit), jnp.bfloat16),
        compiler_params=pltpu.CompilerParams(vmem_limit_bytes=VMEM_LIMIT),
        cost_estimate=pl.CostEstimate(
            flops=0, bytes_accessed=8 * slot_count * width * steps * unit, transcendentals=0
        ),
        name="flip",
    )(part, *[slot for chunk in chunks for slot in chunk])


def settle_kernel(pairs, take_ref, kept_ref, arrived_ref, out_ref):
    values = jnp.where(take_ref[0] != 0, arrived_ref[...], kept_ref[...]).astype(jnp.float32)
    rows, across = values.shape
    out_ref[0] = (-values).astype(jnp.bfloat16)
    values = values.reshape(rows // (2 * pairs), 2, pairs, across)
    turned = jnp.stack([-values[:, 1], values[:, 0]], axis=1)
    out_ref[1] = turned.reshape(rows, across).astype(jnp.bfloat16)


def settle(take, kept, arrived, pairs):
    rows, across = kept.shape
    tile = math.gcd(rows, 256)
    return pl.pallas_call(
        lambda *refs: settle_kernel(pairs, *refs),
        grid_spec=pltpu.PrefetchScalarGridSpec(
            num_scalar_prefetch=1,
            grid=(rows // tile,),
            in_specs=[pl.BlockSpec((tile, across), lambda t, _: (t, 0))] * 2,
            out_specs=pl.BlockSpec((2, tile, across), lambda t, _: (0, t, 0)),
        ),
        out_shape=jax.ShapeDtypeStruct((2, rows, across), jnp.bfloat16),
        compiler_params=pltpu.CompilerParams(vmem_limit_bytes=VMEM_LIMIT),
        cost_estimate=pl.CostEstimate(
            flops=0, bytes_accessed=8 * rows * across, transcendentals=0
        ),
        name="settle",
    )(take, kept, arrived)


def contract_kernel(slot_count, found, right_count, alias, add, *refs):
    chunks = len(found)
    rights = refs[chunks * slot_count : chunks * slot_count + right_count]
    out_ref = refs[-1]
    row = pl.program_id(1)
    for k, (start, count) in enumerate(found):

        @pl.when((row >= start) & (row < start + count))
        def _():
            slots = refs[k * slot_count : (k + 1) * slot_count]
            parts, depth, width = slots[0].shape
            left = jnp.concatenate(
                [slot[...].reshape(parts * depth, width) for slot in slots], axis=1
            )
            for z in range(2):
                right = jnp.concatenate([ref[z] for ref in rights], axis=0)
                total = dot(left, right).reshape(out_ref.shape[1:])
                out_ref[z] = total + refs[-2][z] if add else total


def contract(result, lefts, shares, rights, unit, row_units, column_units, first, steps, add):
    parts, _, width = lefts[0][0].shape
    slot_count = len(lefts[0])
    found = spans(shares, row_units)
    row_steps = sum(shares) // row_units
    depth, side = slot_count * width, sum(shares) * unit
    rows, columns = row_units * unit, column_units * unit
    alias = 0 if result is None else 1
    block = pl.BlockSpec((2, parts, rows, columns), lambda c, r: (0, 0, r, first + c))
    flops = 8 * parts * side * steps * columns * depth
    in_specs = [
        pl.BlockSpec((parts, rows, width), lambda c, r, f=clipped(span): (0, f(r), 0))
        for span in found
        for _ in range(slot_count)
    ]
    in_specs += [
        pl.BlockSpec((2, right.shape[1], columns), lambda c, r: (0, 0, first + c))
        for right in rights
    ]
    if alias:
        in_specs.append(block if add else pl.BlockSpec(memory_space=pl.ANY))
    arrays = [slot for chunk in lefts for slot in chunk] + list(rights)
    return pl.pallas_call(
        lambda *refs: contract_kernel(slot_count, found, len(rights), alias, add, *refs),
        grid=(steps, row_steps),
        in_specs=in_specs,
        out_specs=block,
        out_shape=jax.ShapeDtypeStruct((2, parts, side, side), jnp.float32),
        input_output_aliases={len(arrays): 0} if alias else {},
        compiler_params=pltpu.CompilerParams(vmem_limit_bytes=VMEM_LIMIT),
        cost_estimate=pl.CostEstimate(
            flops=flops, bytes_accessed=flops // depth * (2 if add else 1), transcendentals=0
        ),
        name="contract",
    )(*arrays, *([result] if alias else []))


def energy_gaps(valence_energy, conduction_energy, band_pairs):
    valence_hot = (
        band_pairs[:, 0][:, None] == jnp.arange(valence_energy.shape[0], dtype=jnp.int32)[None, :]
    )
    conduction_hot = (
        band_pairs[:, 1][:, None]
        == jnp.arange(conduction_energy.shape[0], dtype=jnp.int32)[None, :]
    )
    return jnp.sum(jnp.where(valence_hot, valence_energy[None, :], 0.0), axis=1) - jnp.sum(
        jnp.where(conduction_hot, conduction_energy[None, :], 0.0), axis=1
    )


def after(value, *others):
    return lax.optimization_barrier((value,) + others)[0]


def body(valence, conduction, valence_energy, conduction_energy, band_pairs, grid_index):
    rows, cols = lax.axis_size("row"), lax.axis_size("col")
    row, col = lax.axis_index("row"), lax.axis_index("col")
    pairs = band_pairs.shape[0]
    features = 2 * pairs
    width = rows * features
    block = grid_index.shape[0] // cols
    parts = cols // rows
    unit = block // EIGHTHS
    me = row.astype(jnp.int32).reshape(1)
    my_part = (col % parts).astype(jnp.int32).reshape(1)
    owner = col // parts

    order = list(range(0, cols, 2)) + list(range(1, cols, 2))[::-1]
    ring_up = [(order[q], order[(q + 1) % cols]) for q in range(cols)]
    ring_down = [(b, a) for a, b in ring_up]
    my_place = jnp.asarray(np.argsort(np.array(order)), jnp.int32)[col]
    half = cols // 2
    offsets = [0]
    for t in range(1, half):
        offsets += [-t, t]
    offsets.append(half)
    sources = jnp.asarray(np.array(order), jnp.int32)[
        (my_place + jnp.asarray(np.array(offsets), jnp.int32)) % cols
    ]

    gap = energy_gaps(valence_energy, conduction_energy, band_pairs)
    scale = jnp.sqrt(-2.0 / (math.sqrt(pairs * rows * cols) * gap))

    shares = [share for _, share in CHUNKS]
    position = table_position(grid_index).reshape(rows, parts, EIGHTHS, unit)
    position = jnp.concatenate(
        [position[:, :, first : first + share].reshape(-1) for first, share in CHUNKS]
    )
    counts = [parts * share * unit for share in shares]
    sent = transform(valence, conduction, band_pairs, scale, position, me, counts, rows)

    def go_round(below, above):
        return [lax.ppermute(below, "col", ring_up), lax.ppermute(above, "col", ring_down)]

    slots = [[] for _ in range(half)]
    ahead = []
    for i in range(len(CHUNKS)):
        parcels = [after(sent[i][s], *ahead) if ahead else sent[i][s] for s in range(rows)]
        got = parcels[:1] + [
            lax.ppermute(parcels[s], "row", [(r, r ^ s) for r in range(rows)])
            for s in range(1, rows)
        ]
        own = assemble(got, me, features)
        slots[0].append([own])
        if i:
            own = after(own, *slots[1][i - 1])
            slots[1][i - 1] = [after(block, *got) for block in slots[1][i - 1]]
        slots[1].append(go_round(own, own))
        ahead = [own]
    for t in range(2, half):
        for i in range(len(CHUNKS)):
            slots[t].append(go_round(*slots[t - 1][i]))

    def send_column(kept):
        holders, step = [0], rows // 2
        while step:
            perm = [
                ((c // parts ^ h) * cols + c, (c // parts ^ h ^ step) * cols + c)
                for c in range(cols)
                for h in holders
            ]
            arrived = lax.ppermute(kept, ("row", "col"), perm)
            take = (row ^ owner) & step != 0
            if step > 1:
                kept = jnp.where(take, arrived, kept)
            holders += [h ^ step for h in holders]
            step //= 2
        return settle(take.astype(jnp.int32).reshape(1), kept, arrived, pairs)

    def gathered(times):
        return [sum([slots[t][k] for t in times], []) for k in range(len(CHUNKS))]

    def column(times, *before):
        group = gathered(times)
        if before:
            group[0] = [after(group[0][0], *before)] + group[0][1:]
        return send_column(flip(group, shares, my_part, unit))

    def contract_times(result, times, rights, row_units, column_units, first, steps, add):
        lefts = [
            [slot.reshape(parts, share * unit, width) for slot in chunk]
            for chunk, share in zip(gathered(times), shares)
        ]
        return contract(
            result, lefts, shares, rights, unit, row_units, column_units, first, steps, add
        )

    early, late = list(range(half // 2 + 1)), list(range(half // 2 + 1, half + 1))
    rights = [column([0, 1], *slots[half - 1][0])] + [column([t]) for t in early[2:]]
    results = [None]
    for first in range(4):
        results.append(contract_times(results[-1], early, rights, 2, 2, first, 1, False))

    slots.append([])
    for k in range(len(CHUNKS)):
        up, down = slots[half - 1][k][0], slots[half - 1][k][-1]
        if k == len(CHUNKS) - 1:
            up, down = after(up, results[1]), after(down, results[1])
        cut = up.shape[0] // 2
        slots[half].append([jnp.concatenate(go_round(up[:cut], down[cut:]), axis=0)])

    rights = [column([t], results[1 + i]) for i, t in enumerate(late)]
    result = contract_times(results[-1], late, rights, 1, 4, 0, 2, True)
    return result.reshape(2, parts * block, block)


def solution(mesh):
    return jax.shard_map(
        body,
        mesh=mesh,
        in_specs=(P(), P(), P(), P(), P(("row", "col"), None), P()),
        out_specs=P(None, "row", "col"),
        check_vma=False,
    )
```

```python
import math

import jax
import jax.numpy as jnp
import ml_dtypes
import numpy as np
from jax import lax
from jax.experimental import pallas as pl
from jax.experimental.pallas import tpu as pltpu
from jax.sharding import PartitionSpec as P

N1 = 32
N2 = 32
N3 = 32
NR = N1 * N2 * N3
LANES = 128
HI = N2 * N3 // LANES
LO = N2 // HI
ROWS = N1 * HI
VMEM_LIMIT = 58 * 1024 * 1024
CHUNKS = ((0, 4), (4, 4))
EIGHTHS = 8
GROUP = 4


def split_bf16(values):
    high = values.astype(ml_dtypes.bfloat16)
    low = (values - high.astype(np.float64)).astype(ml_dtypes.bfloat16)
    return high, low


def dft_tables():
    row = np.arange(ROWS)
    left = np.exp(
        -2j
        * np.pi
        * (
            (row[:, None] // HI) * (row[None, :] // HI) / N1
            + (row[:, None] % HI) * (row[None, :] % HI) / HI
        )
    )
    lane = np.arange(LANES)
    right = np.exp(
        -2j
        * np.pi
        * (
            (lane[:, None] // N3) * (lane[None, :] // N3) / LO
            + (lane[:, None] % N3) * (lane[None, :] % N3) / N3
        )
    )
    twiddle = np.exp(-2j * np.pi * (row[:, None] % HI) * (lane[None, :] // N3) / N2)
    twiddle = twiddle / math.sqrt(NR)
    left_full = np.block([[left.real, -left.imag], [left.imag, left.real]])
    right_full = np.block([[right.real, right.imag], [-right.imag, right.real]])
    left_high, left_low = split_bf16(left_full)
    right_high, right_low = split_bf16(right_full)
    twiddle = np.concatenate([twiddle] * GROUP, axis=1)
    return (
        np.concatenate([left_high, left_low, left_high], axis=1),
        np.concatenate([right_high, right_low], axis=1),
        np.stack([twiddle.real, twiddle.imag]).astype(np.float32),
    )


def table_position(grid_index):
    first = grid_index // (N2 * N3)
    second = grid_index // N3 % N2
    third = grid_index % N3
    return (first * HI + second % HI) * LANES + second // HI * N3 + third


def halves(value):
    high = value.astype(jnp.bfloat16)
    low = (value - high.astype(jnp.float32)).astype(jnp.bfloat16)
    return high, low


def dot(a, b):
    return jnp.dot(a, b, preferred_element_type=jnp.float32)


def select_rows(count, row_count, features, position_ref, me_ref, table, rows, outs):
    pack = LANES // features
    part = count // pack
    unroll = 32
    lane = lax.broadcasted_iota(jnp.int32, (part, LANES), 1)
    for s in range(row_count):
        base = (me_ref[0] ^ s) * count

        def some_rows(step, carry):
            first = step * unroll
            for j in range(unroll):
                index = position_ref[base + first + j]
                rows[pl.ds(first + j, 1), :] = table[pl.ds(index, 1), :]
            return carry

        lax.fori_loop(0, count // unroll, some_rows, 0)
        packed = rows[0:part, :]
        for k in range(1, pack):
            packed = jnp.where(lane >= k * features, rows[k * part : (k + 1) * part, :], packed)
        outs[s][...] = packed.astype(jnp.bfloat16)


def select_kernel(row_count, features, count, position_ref, me_ref, table_ref, *rest):
    select_rows(
        count, row_count, features, position_ref, me_ref, table_ref, rest[-1], rest[:row_count]
    )


def select(table, position, me, row_count, features):
    count = position.shape[0] // row_count
    shape = (count * features // LANES, LANES)
    return pl.pallas_call(
        lambda *refs: select_kernel(row_count, features, count, *refs),
        grid_spec=pltpu.PrefetchScalarGridSpec(
            num_scalar_prefetch=2,
            grid=(),
            in_specs=[pl.BlockSpec(memory_space=pltpu.VMEM)],
            out_specs=[pl.BlockSpec(memory_space=pltpu.VMEM)] * row_count,
            scratch_shapes=[pltpu.VMEM((count, LANES), jnp.float32)],
        ),
        out_shape=[jax.ShapeDtypeStruct(shape, jnp.bfloat16)] * row_count,
        compiler_params=pltpu.CompilerParams(vmem_limit_bytes=VMEM_LIMIT),
        cost_estimate=pl.CostEstimate(flops=0, bytes_accessed=50_000_000, transcendentals=0),
        name="select",
    )(position, me, table)


def transform_kernel(pairs, load_steps, step_rows, count, row_count, *refs):
    position_ref, me_ref, hot_c_ref, hot_v_ref, scale_ref, cond_ref, val_ref = refs[:7]
    left_ref, right_ref, twiddle_ref = refs[7:10]
    outs = refs[10 : 10 + row_count]
    table_ref, rho_r, rho_i, spec, table, middle, rows, sem = refs[10 + row_count :]
    step = pl.program_id(0)
    features = 2 * pairs

    cond = dot(hot_c_ref[...], cond_ref[...])
    val = dot(hot_v_ref[...], val_ref[...]) * scale_ref[...]
    cr, ci = cond[:pairs], cond[pairs:]
    vr, vi = val[:pairs], val[pairs:]
    real = vr * cr + vi * ci
    imag = vr * ci - vi * cr
    for a in range(step_rows):
        row = pl.multiple_of((step * step_rows + a) * pairs, pairs)
        rho_r[pl.ds(row, pairs), :] = real[:, a * LANES : (a + 1) * LANES]
        rho_i[pl.ds(row, pairs), :] = imag[:, a * LANES : (a + 1) * LANES]

    def left_half(group, slot):
        members = [GROUP * group + k for k in range(GROUP)]
        data = jnp.concatenate(
            [
                jnp.concatenate([ref[pl.ds(p, ROWS, stride=pairs), :] for p in members], axis=1)
                for ref in (rho_r, rho_i)
            ],
            axis=0,
        )
        high, low = halves(data)
        mixed = dot(left_ref[...], jnp.concatenate([high, high, low], axis=0))
        mid_r, mid_i = mixed[:ROWS], mixed[ROWS:]
        tr, ti = twiddle_ref[0], twiddle_ref[1]
        turn_r = mid_r * tr - mid_i * ti
        turn_i = mid_r * ti + mid_i * tr
        for k in range(GROUP):
            lanes = slice(k * LANES, (k + 1) * LANES)
            rows_k = slice(k * ROWS, (k + 1) * ROWS)
            for z, turned in enumerate((turn_r, turn_i)):
                high, low = halves(turned[:, lanes])
                middle[slot, rows_k, z * LANES : (z + 1) * LANES] = high
                middle[slot, rows_k, (2 + z) * LANES : (3 + z) * LANES] = low

    def right_half(group, slot):
        high = middle[slot, :, : 2 * LANES]
        low = middle[slot, :, 2 * LANES :]
        by_high = dot(high, right_ref[...])
        by_low = dot(low, right_ref[:, : 2 * LANES])
        out = by_high[:, : 2 * LANES] + (by_high[:, 2 * LANES :] + by_low)
        for k in range(GROUP):
            p = GROUP * group + k
            part = out[k * ROWS : (k + 1) * ROWS]
            spec[pl.ds(p, ROWS, stride=features), :] = part[:, :LANES]
            spec[pl.ds(pairs + p, ROWS, stride=features), :] = part[:, LANES:]

    @pl.when(step == load_steps - 1)
    def _():
        groups = pairs // GROUP
        left_half(0, 0)

        def two_groups(k, carry):
            right_half(2 * k, 0)
            left_half(2 * k + 1, 1)
            right_half(2 * k + 1, 1)
            left_half(jnp.minimum(2 * k + 2, groups - 1), 0)
            return carry

        lax.fori_loop(0, groups // 2, two_groups, 0)

        def one_row(k, carry):
            start = pl.multiple_of(k * features, features)
            tile = spec[pl.ds(start, features), :].astype(jnp.bfloat16)
            tile = jnp.concatenate([tile] * (LANES // features), axis=0)
            table[pl.ds(pl.multiple_of(k * LANES, LANES), LANES), :] = tile.T.astype(jnp.float32)
            return carry

        lax.fori_loop(0, ROWS, one_row, 0, unroll=8)
        keep = pltpu.make_async_copy(table, table_ref, sem)
        keep.start()
        select_rows(count, row_count, features, position_ref, me_ref, table, rows, outs)
        keep.wait()


def transform(valence, conduction, band_pairs, scale, position, me, row_count):
    count = position.shape[0] // row_count
    pairs = band_pairs.shape[0]
    features = 2 * pairs
    pack = LANES // features
    nvb, ncb = valence.shape[1], conduction.shape[1]
    load_steps = 8
    step_rows = ROWS // load_steps
    chunk = step_rows * LANES

    def hot(band, count):
        one = (band[:, None] == jnp.arange(count, dtype=jnp.int32)[None, :]).astype(jnp.bfloat16)
        none = jnp.zeros_like(one)
        return jnp.concatenate(
            [jnp.concatenate([one, none], axis=1), jnp.concatenate([none, one], axis=1)], axis=0
        )

    left, right, twiddle = dft_tables()
    whole = lambda shape: pl.BlockSpec(shape, lambda i, *_: (0,) * len(shape))
    loaded = lambda i, *_: (0, i)
    flops = 2 * pairs * (6 * ROWS * ROWS * 2 * LANES + 3 * ROWS * 4 * LANES * LANES)
    out_shapes = [(count // pack, LANES)] * row_count
    outs = pl.pallas_call(
        lambda *refs: transform_kernel(pairs, load_steps, step_rows, count, row_count, *refs),
        grid_spec=pltpu.PrefetchScalarGridSpec(
            num_scalar_prefetch=2,
            grid=(load_steps,),
            in_specs=[
                whole((2 * pairs, 2 * ncb)),
                whole((2 * pairs, 2 * nvb)),
                whole((2 * pairs, 1)),
                pl.BlockSpec((2 * ncb, chunk), loaded),
                pl.BlockSpec((2 * nvb, chunk), loaded),
                whole(left.shape),
                whole(right.shape),
                whole(twiddle.shape),
            ],
            out_specs=[whole(shape) for shape in out_shapes] + [pl.BlockSpec(memory_space=pl.ANY)],
            scratch_shapes=[
                pltpu.VMEM((ROWS * pairs, LANES), jnp.float32),
                pltpu.VMEM((ROWS * pairs, LANES), jnp.float32),
                pltpu.VMEM((ROWS * features, LANES), jnp.float32),
                pltpu.VMEM((NR, LANES), jnp.float32),
                pltpu.VMEM((2, GROUP * ROWS, 4 * LANES), jnp.bfloat16),
                pltpu.VMEM((count, LANES), jnp.float32),
                pltpu.SemaphoreType.DMA,
            ],
        ),
        out_shape=[jax.ShapeDtypeStruct(shape, jnp.bfloat16) for shape in out_shapes]
        + [jax.ShapeDtypeStruct((NR, LANES), jnp.float32)],
        compiler_params=pltpu.CompilerParams(vmem_limit_bytes=VMEM_LIMIT),
        cost_estimate=pl.CostEstimate(flops=flops, bytes_accessed=40_000_000, transcendentals=0),
        name="transform",
    )(
        position,
        me,
        hot(band_pairs[:, 1], ncb),
        hot(band_pairs[:, 0], nvb),
        jnp.concatenate([scale, scale])[:, None],
        conduction.reshape(2 * ncb, NR),
        valence.reshape(2 * nvb, NR),
        jnp.asarray(left),
        jnp.asarray(right),
        jnp.asarray(twiddle),
    )
    return outs[:row_count], outs[row_count]


def assemble_kernel(row_count, features, me_ref, *rest):
    parts, out_ref, held = rest[:row_count], rest[row_count], rest[row_count + 1]
    pack = LANES // features
    part = parts[0].shape[0]
    lane = lax.broadcasted_iota(jnp.int32, (part, LANES), 1)
    for s in range(row_count):
        held[s] = parts[s][...].astype(jnp.float32)
    for b in range(row_count // pack):
        for k in range(pack):
            block = None
            for q in range(pack):
                piece = held[(b * pack + q) ^ me_ref[0]]
                if q != k:
                    piece = pltpu.roll(piece, (q - k) * features % LANES, 1)
                block = piece if block is None else jnp.where(lane >= q * features, piece, block)
            out_ref[k * part : (k + 1) * part, b * LANES : (b + 1) * LANES] = block.astype(
                jnp.bfloat16
            )


def assemble(parts, me, features):
    row_count = len(parts)
    pack = LANES // features
    part = parts[0].shape[0]
    return pl.pallas_call(
        lambda *refs: assemble_kernel(row_count, features, *refs),
        grid_spec=pltpu.PrefetchScalarGridSpec(
            num_scalar_prefetch=1,
            grid=(),
            in_specs=[pl.BlockSpec(memory_space=pltpu.VMEM)] * row_count,
            out_specs=pl.BlockSpec(memory_space=pltpu.VMEM),
            scratch_shapes=[pltpu.VMEM((row_count, part, LANES), jnp.float32)],
        ),
        out_shape=jax.ShapeDtypeStruct((part * pack, row_count * features), jnp.bfloat16),
        compiler_params=pltpu.CompilerParams(vmem_limit_bytes=VMEM_LIMIT),
        cost_estimate=pl.CostEstimate(flops=0, bytes_accessed=2_000_000, transcendentals=0),
        name="assemble",
    )(me, *parts)


def flip_kernel(slot_count, part_ref, *refs):
    out_ref = refs[slot_count]
    for s in range(slot_count):
        width = refs[s].shape[1]
        out_ref[s * width : (s + 1) * width, :] = refs[s][...].T


def flip(slots, part, parts, unit):
    slot_count = len(slots)
    width = slots[0].shape[1]
    depth = slots[0].shape[0] // parts
    steps = depth // unit
    return pl.pallas_call(
        lambda *refs: flip_kernel(slot_count, *refs),
        grid_spec=pltpu.PrefetchScalarGridSpec(
            num_scalar_prefetch=1,
            grid=(steps,),
            in_specs=[
                pl.BlockSpec((unit, width), lambda t, part_ref: (part_ref[0] * steps + t, 0))
            ]
            * slot_count,
            out_specs=pl.BlockSpec((slot_count * width, unit), lambda t, part_ref: (0, t)),
        ),
        out_shape=jax.ShapeDtypeStruct((slot_count * width, depth), jnp.bfloat16),
        compiler_params=pltpu.CompilerParams(vmem_limit_bytes=VMEM_LIMIT),
        cost_estimate=pl.CostEstimate(
            flops=0, bytes_accessed=8 * slot_count * width * depth, transcendentals=0
        ),
        name="flip",
    )(part, *slots)


def settle_kernel(pairs, row_count, which_ref, *refs):
    out_ref = refs[row_count]
    for k in range(row_count):

        @pl.when(which_ref[0] == k)
        def _():
            values = refs[k][...].astype(jnp.float32)
            rows, across = values.shape
            out_ref[0] = (-values).astype(jnp.bfloat16)
            values = values.reshape(rows // (2 * pairs), 2, pairs, across)
            turned = jnp.stack([-values[:, 1], values[:, 0]], axis=1)
            out_ref[1] = turned.reshape(rows, across).astype(jnp.bfloat16)


def settle(which, copies, pairs):
    rows, across = copies[0].shape
    tile = math.gcd(rows, 256)
    row_count = len(copies)

    def pick(k):
        return lambda t, which_ref: (jnp.where(which_ref[0] == k, t, 0), 0)

    return pl.pallas_call(
        lambda *refs: settle_kernel(pairs, row_count, *refs),
        grid_spec=pltpu.PrefetchScalarGridSpec(
            num_scalar_prefetch=1,
            grid=(rows // tile,),
            in_specs=[pl.BlockSpec((tile, across), pick(k)) for k in range(row_count)],
            out_specs=pl.BlockSpec((2, tile, across), lambda t, _: (0, t, 0)),
        ),
        out_shape=jax.ShapeDtypeStruct((2, rows, across), jnp.bfloat16),
        compiler_params=pltpu.CompilerParams(vmem_limit_bytes=VMEM_LIMIT),
        cost_estimate=pl.CostEstimate(
            flops=0, bytes_accessed=8 * rows * across, transcendentals=0
        ),
        name="settle",
    )(which, *copies)


def contract_kernel(slot_count, shares, right_count, *refs):
    rights = refs[len(shares) * slot_count : len(shares) * slot_count + right_count]
    out_ref = refs[-1]
    row = pl.program_id(1)
    for k, share in enumerate(shares):
        start = sum(shares[:k])

        @pl.when((row >= start) & (row < start + share))
        def _():
            slots = refs[k * slot_count : (k + 1) * slot_count]
            parts, depth, width = slots[0].shape
            left = jnp.concatenate(
                [slot[...].reshape(parts * depth, width) for slot in slots], axis=1
            )
            for z in range(2):
                right = jnp.concatenate([ref[z] for ref in rights], axis=0)
                out_ref[z] = dot(left, right).reshape(out_ref.shape[1:])


def contract(result, lefts, rights, unit, row_first, wide, tile_first, steps, out_first):
    parts, _, width = lefts[0][0].shape
    slot_count = len(lefts[0])
    shares = [chunk[0].shape[1] // unit for chunk in lefts]
    depth = slot_count * width
    columns, side = wide * unit, EIGHTHS * unit
    alias = 0 if result is None else 1
    flops = 8 * parts * sum(shares) * unit * steps * columns * depth

    def place(start, share):
        return lambda c, r: (0, jnp.clip(r - start, 0, share - 1), 0)

    in_specs = [
        pl.BlockSpec((parts, unit, width), place(sum(shares[:k]), share))
        for k, share in enumerate(shares)
        for _ in range(slot_count)
    ]
    in_specs += [
        pl.BlockSpec((2, right.shape[1], columns), lambda c, r: (0, 0, tile_first + c))
        for right in rights
    ]
    if alias:
        in_specs.append(pl.BlockSpec(memory_space=pl.ANY))
    arrays = [slot for chunk in lefts for slot in chunk] + list(rights)
    return pl.pallas_call(
        lambda *refs: contract_kernel(slot_count, shares, len(rights), *refs),
        grid=(steps, sum(shares)),
        in_specs=in_specs,
        out_specs=pl.BlockSpec(
            (2, parts, unit, columns), lambda c, r: (0, 0, row_first + r, out_first + c)
        ),
        out_shape=jax.ShapeDtypeStruct((2, parts, side, side), jnp.float32),
        input_output_aliases={len(arrays): 0} if alias else {},
        compiler_params=pltpu.CompilerParams(vmem_limit_bytes=VMEM_LIMIT),
        cost_estimate=pl.CostEstimate(
            flops=flops, bytes_accessed=flops // depth, transcendentals=0
        ),
        name="contract",
    )(*arrays, *([result] if alias else []))


def energy_gaps(valence_energy, conduction_energy, band_pairs):
    valence_hot = (
        band_pairs[:, 0][:, None] == jnp.arange(valence_energy.shape[0], dtype=jnp.int32)[None, :]
    )
    conduction_hot = (
        band_pairs[:, 1][:, None]
        == jnp.arange(conduction_energy.shape[0], dtype=jnp.int32)[None, :]
    )
    return jnp.sum(jnp.where(valence_hot, valence_energy[None, :], 0.0), axis=1) - jnp.sum(
        jnp.where(conduction_hot, conduction_energy[None, :], 0.0), axis=1
    )


def after(value, *others):
    return lax.optimization_barrier((value,) + others)[0]


def body(valence, conduction, valence_energy, conduction_energy, band_pairs, grid_index):
    rows, cols = lax.axis_size("row"), lax.axis_size("col")
    row, col = lax.axis_index("row"), lax.axis_index("col")
    pairs = band_pairs.shape[0]
    features = 2 * pairs
    width = rows * features
    block = grid_index.shape[0] // cols
    parts = cols // rows
    unit = block // EIGHTHS
    me = row.astype(jnp.int32).reshape(1)
    my_part = (col % parts).astype(jnp.int32).reshape(1)
    owner = col // parts

    order = list(range(0, cols, 2)) + list(range(1, cols, 2))[::-1]
    ring_up = [(order[q], order[(q + 1) % cols]) for q in range(cols)]
    ring_down = [(b, a) for a, b in ring_up]
    my_place = jnp.asarray(np.argsort(np.array(order)), jnp.int32)[col]
    half = cols // 2
    offsets = [0]
    for t in range(1, half):
        offsets += [-t, t]
    offsets.append(half)
    sources = jnp.asarray(np.array(order), jnp.int32)[
        (my_place + jnp.asarray(np.array(offsets), jnp.int32)) % cols
    ]

    gap = energy_gaps(valence_energy, conduction_energy, band_pairs)
    scale = jnp.sqrt(-2.0 / (math.sqrt(pairs * rows * cols) * gap))

    position = table_position(grid_index).reshape(rows, parts, EIGHTHS, unit)
    positions = [
        position[:, :, first : first + share].reshape(-1) for first, share in CHUNKS
    ]
    sent, table = transform(valence, conduction, band_pairs, scale, positions[0], me, rows)

    def across_rows(parcels):
        return [parcels[0]] + [
            lax.ppermute(parcels[s], "row", [(r, r ^ s) for r in range(rows)])
            for s in range(1, rows)
        ]

    def go_round(below, above):
        return [lax.ppermute(below, "col", ring_up), lax.ppermute(above, "col", ring_down)]

    def last_round(below, above):
        cut = below.shape[0] // 2
        return [jnp.concatenate(go_round(below[:cut], above[cut:]), axis=0)]

    def column(slots, *before):
        slots = [after(slots[0], *before)] + slots[1:] if before else slots
        copies = [flip(slots, my_part, parts, unit)]
        for relation in range(1, rows):
            source = relation & (relation - 1)
            perm = [
                ((c // parts ^ source) * cols + c, (c // parts ^ relation) * cols + c)
                for c in range(cols)
            ]
            copies.append(lax.ppermute(copies[source], ("row", "col"), perm))
        return copies

    which = (row ^ owner).astype(jnp.int32).reshape(1)

    own = assemble(across_rows(sent), me, features)
    one = [[own], go_round(own, own)]
    sent = select(after(table, own), positions[1], me, rows, features)
    one[1] = [after(block, *sent) for block in one[1]]
    own = assemble(across_rows(sent), me, features)
    for t in range(2, half):
        one.append(go_round(*one[t - 1]))
    one.append(last_round(*one[half - 1]))
    copies = [column(sum(one[:2], [])), column(sum(one[2:half], [])), column(one[half])]
    rights = [settle(which, copies[0], pairs)]

    two = [[own], go_round(*[after(own, rights[0], *one[half - 1])] * 2)]
    two.append(go_round(*[after(block, copies[1][0]) for block in two[1]]))
    rights += [settle(which, some, pairs) for some in copies[1:]]

    def as_lefts(slots):
        return [slot.reshape(parts, -1, width) for slot in sum(slots, [])]

    lefts = as_lefts(one)
    wide = CHUNKS[0][1] // 2
    first = contract(None, [lefts], rights, unit, 0, wide, 0, 1, 0)
    two.append(go_round(*[after(block, first) for block in two[2]]))
    second = contract(first, [lefts], rights, unit, 0, wide, 1, 1, 1)
    for t in range(4, half):
        two.append(go_round(*two[t - 1]))
    middle = half // 2 + 1
    copies = [column(sum(two[:middle], []))]
    two.append(last_round(*[after(block, second, copies[0][0]) for block in two[half - 1]]))
    copies.append(column(sum(two[middle:], [])))
    share = CHUNKS[0][1]
    both = [lefts, as_lefts(two)]
    result = contract(second, both[1:], rights, unit, share, share, 0, 1, 0)
    rights = [settle(which, some, pairs) for some in copies]
    result = contract(result, both, rights, unit, 0, share, 0, 1, 1)
    return result.reshape(2, parts * block, block)


def solution(mesh):
    return jax.shard_map(
        body,
        mesh=mesh,
        in_specs=(P(), P(), P(), P(), P(("row", "col"), None), P()),
        out_specs=P(None, "row", "col"),
        check_vma=False,
    )
```

```python
import math

import jax
import jax.numpy as jnp
import ml_dtypes
import numpy as np
from jax import lax
from jax.experimental import pallas as pl
from jax.experimental.pallas import tpu as pltpu
from jax.sharding import PartitionSpec as P

N1 = 32
N2 = 32
N3 = 32
NR = N1 * N2 * N3
LANES = 128
HI = N2 * N3 // LANES
LO = N2 // HI
ROWS = N1 * HI
VMEM_LIMIT = 58 * 1024 * 1024
CHUNKS = ((0, 4), (4, 4))
EIGHTHS = 8
GROUP = 4


def split_bf16(values):
    high = values.astype(ml_dtypes.bfloat16)
    low = (values - high.astype(np.float64)).astype(ml_dtypes.bfloat16)
    return high, low


def dft_tables():
    row = np.arange(ROWS)
    left = np.exp(
        -2j
        * np.pi
        * (
            (row[:, None] // HI) * (row[None, :] // HI) / N1
            + (row[:, None] % HI) * (row[None, :] % HI) / HI
        )
    )
    lane = np.arange(LANES)
    right = np.exp(
        -2j
        * np.pi
        * (
            (lane[:, None] // N3) * (lane[None, :] // N3) / LO
            + (lane[:, None] % N3) * (lane[None, :] % N3) / N3
        )
    )
    twiddle = np.exp(-2j * np.pi * (row[:, None] % HI) * (lane[None, :] // N3) / N2)
    twiddle = twiddle / math.sqrt(NR)
    left_full = np.block([[left.real, -left.imag], [left.imag, left.real]])
    right_full = np.block([[right.real, right.imag], [-right.imag, right.real]])
    left_high, left_low = split_bf16(left_full)
    right_high, right_low = split_bf16(right_full)
    twiddle = np.concatenate([twiddle] * GROUP, axis=1)
    return (
        np.concatenate([left_high, left_low, left_high], axis=1),
        np.concatenate([right_high, right_low], axis=1),
        np.stack([twiddle.real, twiddle.imag]).astype(np.float32),
    )


def table_position(grid_index):
    first = grid_index // (N2 * N3)
    second = grid_index // N3 % N2
    third = grid_index % N3
    return (first * HI + second % HI) * LANES + second // HI * N3 + third


def halves(value):
    high = value.astype(jnp.bfloat16)
    low = (value - high.astype(jnp.float32)).astype(jnp.bfloat16)
    return high, low


def dot(a, b):
    return jnp.dot(a, b, preferred_element_type=jnp.float32)


def select_rows(count, row_count, features, position_ref, me_ref, table, rows, outs):
    pack = LANES // features
    part = count // pack
    unroll = 32
    lane = lax.broadcasted_iota(jnp.int32, (part, LANES), 1)
    for s in range(row_count):
        base = (me_ref[0] ^ s) * count

        def some_rows(step, carry):
            first = step * unroll
            for j in range(unroll):
                index = position_ref[base + first + j]
                rows[pl.ds(first + j, 1), :] = table[pl.ds(index, 1), :]
            return carry

        lax.fori_loop(0, count // unroll, some_rows, 0)
        packed = rows[0:part, :]
        for k in range(1, pack):
            packed = jnp.where(lane >= k * features, rows[k * part : (k + 1) * part, :], packed)
        outs[s][...] = packed.astype(jnp.bfloat16)


def select_kernel(row_count, features, count, position_ref, me_ref, table_ref, *rest):
    select_rows(
        count, row_count, features, position_ref, me_ref, table_ref, rest[-1], rest[:row_count]
    )


def select(table, position, me, row_count, features):
    count = position.shape[0] // row_count
    shape = (count * features // LANES, LANES)
    return pl.pallas_call(
        lambda *refs: select_kernel(row_count, features, count, *refs),
        grid_spec=pltpu.PrefetchScalarGridSpec(
            num_scalar_prefetch=2,
            grid=(),
            in_specs=[pl.BlockSpec(memory_space=pltpu.VMEM)],
            out_specs=[pl.BlockSpec(memory_space=pltpu.VMEM)] * row_count,
            scratch_shapes=[pltpu.VMEM((count, LANES), jnp.float32)],
        ),
        out_shape=[jax.ShapeDtypeStruct(shape, jnp.bfloat16)] * row_count,
        compiler_params=pltpu.CompilerParams(vmem_limit_bytes=VMEM_LIMIT),
        cost_estimate=pl.CostEstimate(flops=0, bytes_accessed=50_000_000, transcendentals=0),
        name="select",
    )(position, me, table)


def transform_kernel(pairs, load_steps, step_rows, count, row_count, *refs):
    position_ref, me_ref, hot_c_ref, hot_v_ref, scale_ref, cond_ref, val_ref = refs[:7]
    left_ref, right_ref, twiddle_ref = refs[7:10]
    outs = refs[10 : 10 + row_count]
    table_ref, rho_r, rho_i, spec, table, middle, rows, sem = refs[10 + row_count :]
    step = pl.program_id(0)
    features = 2 * pairs

    cond = dot(hot_c_ref[...], cond_ref[...])
    val = dot(hot_v_ref[...], val_ref[...]) * scale_ref[...]
    cr, ci = cond[:pairs], cond[pairs:]
    vr, vi = val[:pairs], val[pairs:]
    real = vr * cr + vi * ci
    imag = vr * ci - vi * cr
    for a in range(step_rows):
        row = pl.multiple_of((step * step_rows + a) * pairs, pairs)
        rho_r[pl.ds(row, pairs), :] = real[:, a * LANES : (a + 1) * LANES]
        rho_i[pl.ds(row, pairs), :] = imag[:, a * LANES : (a + 1) * LANES]

    def left_half(group, slot):
        members = [GROUP * group + k for k in range(GROUP)]
        data = jnp.concatenate(
            [
                jnp.concatenate([ref[pl.ds(p, ROWS, stride=pairs), :] for p in members], axis=1)
                for ref in (rho_r, rho_i)
            ],
            axis=0,
        )
        high, low = halves(data)
        mixed = dot(left_ref[...], jnp.concatenate([high, high, low], axis=0))
        mid_r, mid_i = mixed[:ROWS], mixed[ROWS:]
        tr, ti = twiddle_ref[0], twiddle_ref[1]
        turn_r = mid_r * tr - mid_i * ti
        turn_i = mid_r * ti + mid_i * tr
        for k in range(GROUP):
            lanes = slice(k * LANES, (k + 1) * LANES)
            rows_k = slice(k * ROWS, (k + 1) * ROWS)
            for z, turned in enumerate((turn_r, turn_i)):
                high, low = halves(turned[:, lanes])
                middle[slot, rows_k, z * LANES : (z + 1) * LANES] = high
                middle[slot, rows_k, (2 + z) * LANES : (3 + z) * LANES] = low

    def right_half(group, slot):
        high = middle[slot, :, : 2 * LANES]
        low = middle[slot, :, 2 * LANES :]
        by_high = dot(high, right_ref[...])
        by_low = dot(low, right_ref[:, : 2 * LANES])
        out = by_high[:, : 2 * LANES] + (by_high[:, 2 * LANES :] + by_low)
        for k in range(GROUP):
            p = GROUP * group + k
            part = out[k * ROWS : (k + 1) * ROWS]
            spec[pl.ds(p, ROWS, stride=features), :] = part[:, :LANES]
            spec[pl.ds(pairs + p, ROWS, stride=features), :] = part[:, LANES:]

    @pl.when(step == load_steps - 1)
    def _():
        groups = pairs // GROUP
        left_half(0, 0)

        def two_groups(k, carry):
            right_half(2 * k, 0)
            left_half(2 * k + 1, 1)
            right_half(2 * k + 1, 1)
            left_half(jnp.minimum(2 * k + 2, groups - 1), 0)
            return carry

        lax.fori_loop(0, groups // 2, two_groups, 0)

        def one_row(k, carry):
            start = pl.multiple_of(k * features, features)
            tile = spec[pl.ds(start, features), :].astype(jnp.bfloat16)
            tile = jnp.concatenate([tile] * (LANES // features), axis=0)
            table[pl.ds(pl.multiple_of(k * LANES, LANES), LANES), :] = tile.T.astype(jnp.float32)
            return carry

        lax.fori_loop(0, ROWS, one_row, 0, unroll=8)
        keep = pltpu.make_async_copy(table, table_ref, sem)
        keep.start()
        select_rows(count, row_count, features, position_ref, me_ref, table, rows, outs)
        keep.wait()


def transform(valence, conduction, band_pairs, scale, position, me, row_count):
    count = position.shape[0] // row_count
    pairs = band_pairs.shape[0]
    features = 2 * pairs
    pack = LANES // features
    nvb, ncb = valence.shape[1], conduction.shape[1]
    load_steps = 8
    step_rows = ROWS // load_steps
    chunk = step_rows * LANES

    def hot(band, count):
        one = (band[:, None] == jnp.arange(count, dtype=jnp.int32)[None, :]).astype(jnp.bfloat16)
        none = jnp.zeros_like(one)
        return jnp.concatenate(
            [jnp.concatenate([one, none], axis=1), jnp.concatenate([none, one], axis=1)], axis=0
        )

    left, right, twiddle = dft_tables()
    whole = lambda shape: pl.BlockSpec(shape, lambda i, *_: (0,) * len(shape))
    loaded = lambda i, *_: (0, i)
    flops = 2 * pairs * (6 * ROWS * ROWS * 2 * LANES + 3 * ROWS * 4 * LANES * LANES)
    out_shapes = [(count // pack, LANES)] * row_count
    outs = pl.pallas_call(
        lambda *refs: transform_kernel(pairs, load_steps, step_rows, count, row_count, *refs),
        grid_spec=pltpu.PrefetchScalarGridSpec(
            num_scalar_prefetch=2,
            grid=(load_steps,),
            in_specs=[
                whole((2 * pairs, 2 * ncb)),
                whole((2 * pairs, 2 * nvb)),
                whole((2 * pairs, 1)),
                pl.BlockSpec((2 * ncb, chunk), loaded),
                pl.BlockSpec((2 * nvb, chunk), loaded),
                whole(left.shape),
                whole(right.shape),
                whole(twiddle.shape),
            ],
            out_specs=[whole(shape) for shape in out_shapes] + [pl.BlockSpec(memory_space=pl.ANY)],
            scratch_shapes=[
                pltpu.VMEM((ROWS * pairs, LANES), jnp.float32),
                pltpu.VMEM((ROWS * pairs, LANES), jnp.float32),
                pltpu.VMEM((ROWS * features, LANES), jnp.float32),
                pltpu.VMEM((NR, LANES), jnp.float32),
                pltpu.VMEM((2, GROUP * ROWS, 4 * LANES), jnp.bfloat16),
                pltpu.VMEM((count, LANES), jnp.float32),
                pltpu.SemaphoreType.DMA,
            ],
        ),
        out_shape=[jax.ShapeDtypeStruct(shape, jnp.bfloat16) for shape in out_shapes]
        + [jax.ShapeDtypeStruct((NR, LANES), jnp.float32)],
        compiler_params=pltpu.CompilerParams(vmem_limit_bytes=VMEM_LIMIT),
        cost_estimate=pl.CostEstimate(flops=flops, bytes_accessed=40_000_000, transcendentals=0),
        name="transform",
    )(
        position,
        me,
        hot(band_pairs[:, 1], ncb),
        hot(band_pairs[:, 0], nvb),
        jnp.concatenate([scale, scale])[:, None],
        conduction.reshape(2 * ncb, NR),
        valence.reshape(2 * nvb, NR),
        jnp.asarray(left),
        jnp.asarray(right),
        jnp.asarray(twiddle),
    )
    return outs[:row_count], outs[row_count]


def assemble_kernel(row_count, features, me_ref, *rest):
    parts, out_ref, held = rest[:row_count], rest[row_count], rest[row_count + 1]
    pack = LANES // features
    part = parts[0].shape[0]
    lane = lax.broadcasted_iota(jnp.int32, (part, LANES), 1)
    for s in range(row_count):
        held[s] = parts[s][...].astype(jnp.float32)
    for b in range(row_count // pack):
        for k in range(pack):
            block = None
            for q in range(pack):
                piece = held[(b * pack + q) ^ me_ref[0]]
                if q != k:
                    piece = pltpu.roll(piece, (q - k) * features % LANES, 1)
                block = piece if block is None else jnp.where(lane >= q * features, piece, block)
            out_ref[k * part : (k + 1) * part, b * LANES : (b + 1) * LANES] = block.astype(
                jnp.bfloat16
            )


def assemble(parts, me, features):
    row_count = len(parts)
    pack = LANES // features
    part = parts[0].shape[0]
    return pl.pallas_call(
        lambda *refs: assemble_kernel(row_count, features, *refs),
        grid_spec=pltpu.PrefetchScalarGridSpec(
            num_scalar_prefetch=1,
            grid=(),
            in_specs=[pl.BlockSpec(memory_space=pltpu.VMEM)] * row_count,
            out_specs=pl.BlockSpec(memory_space=pltpu.VMEM),
            scratch_shapes=[pltpu.VMEM((row_count, part, LANES), jnp.float32)],
        ),
        out_shape=jax.ShapeDtypeStruct((part * pack, row_count * features), jnp.bfloat16),
        compiler_params=pltpu.CompilerParams(vmem_limit_bytes=VMEM_LIMIT),
        cost_estimate=pl.CostEstimate(flops=0, bytes_accessed=2_000_000, transcendentals=0),
        name="assemble",
    )(me, *parts)


def flip_kernel(slot_count, part_ref, *refs):
    out_ref = refs[slot_count]
    for s in range(slot_count):
        width = refs[s].shape[1]
        out_ref[s * width : (s + 1) * width, :] = refs[s][...].T


def flip(slots, part, parts, unit):
    slot_count = len(slots)
    width = slots[0].shape[1]
    depth = slots[0].shape[0] // parts
    steps = depth // unit
    return pl.pallas_call(
        lambda *refs: flip_kernel(slot_count, *refs),
        grid_spec=pltpu.PrefetchScalarGridSpec(
            num_scalar_prefetch=1,
            grid=(steps,),
            in_specs=[
                pl.BlockSpec((unit, width), lambda t, part_ref: (part_ref[0] * steps + t, 0))
            ]
            * slot_count,
            out_specs=pl.BlockSpec((slot_count * width, unit), lambda t, part_ref: (0, t)),
        ),
        out_shape=jax.ShapeDtypeStruct((slot_count * width, depth), jnp.bfloat16),
        compiler_params=pltpu.CompilerParams(vmem_limit_bytes=VMEM_LIMIT),
        cost_estimate=pl.CostEstimate(
            flops=0, bytes_accessed=8 * slot_count * width * depth, transcendentals=0
        ),
        name="flip",
    )(part, *slots)


def settle_kernel(pairs, row_count, which_ref, *refs):
    out_ref = refs[row_count]
    for k in range(row_count):

        @pl.when(which_ref[0] == k)
        def _():
            values = refs[k][...].astype(jnp.float32)
            rows, across = values.shape
            out_ref[0] = (-values).astype(jnp.bfloat16)
            values = values.reshape(rows // (2 * pairs), 2, pairs, across)
            turned = jnp.stack([-values[:, 1], values[:, 0]], axis=1)
            out_ref[1] = turned.reshape(rows, across).astype(jnp.bfloat16)


def settle(which, copies, pairs):
    rows, across = copies[0].shape
    tile = math.gcd(rows, 256)
    row_count = len(copies)

    def pick(k):
        return lambda t, which_ref: (jnp.where(which_ref[0] == k, t, 0), 0)

    return pl.pallas_call(
        lambda *refs: settle_kernel(pairs, row_count, *refs),
        grid_spec=pltpu.PrefetchScalarGridSpec(
            num_scalar_prefetch=1,
            grid=(rows // tile,),
            in_specs=[pl.BlockSpec((tile, across), pick(k)) for k in range(row_count)],
            out_specs=pl.BlockSpec((2, tile, across), lambda t, _: (0, t, 0)),
        ),
        out_shape=jax.ShapeDtypeStruct((2, rows, across), jnp.bfloat16),
        compiler_params=pltpu.CompilerParams(vmem_limit_bytes=VMEM_LIMIT),
        cost_estimate=pl.CostEstimate(
            flops=0, bytes_accessed=8 * rows * across, transcendentals=0
        ),
        name="settle",
    )(which, *copies)


def contract_kernel(slot_count, shares, right_count, *refs):
    rights = refs[len(shares) * slot_count : len(shares) * slot_count + right_count]
    out_ref = refs[-1]
    row = pl.program_id(1)
    for k, share in enumerate(shares):
        start = sum(shares[:k])

        @pl.when((row >= start) & (row < start + share))
        def _():
            slots = refs[k * slot_count : (k + 1) * slot_count]
            parts, depth, width = slots[0].shape
            left = jnp.concatenate(
                [slot[...].reshape(parts * depth, width) for slot in slots], axis=1
            )
            for z in range(2):
                right = jnp.concatenate([ref[z] for ref in rights], axis=0)
                out_ref[z] = dot(left, right).reshape(out_ref.shape[1:])


def contract(result, lefts, rights, unit, row_first, wide, tile_first, steps, out_first):
    parts, _, width = lefts[0][0].shape
    slot_count = len(lefts[0])
    shares = [chunk[0].shape[1] // unit for chunk in lefts]
    depth = slot_count * width
    columns, side = wide * unit, EIGHTHS * unit
    alias = 0 if result is None else 1
    flops = 8 * parts * sum(shares) * unit * steps * columns * depth

    def place(start, share):
        return lambda c, r: (0, jnp.clip(r - start, 0, share - 1), 0)

    in_specs = [
        pl.BlockSpec((parts, unit, width), place(sum(shares[:k]), share))
        for k, share in enumerate(shares)
        for _ in range(slot_count)
    ]
    in_specs += [
        pl.BlockSpec((2, right.shape[1], columns), lambda c, r: (0, 0, tile_first + c))
        for right in rights
    ]
    if alias:
        in_specs.append(pl.BlockSpec(memory_space=pl.ANY))
    arrays = [slot for chunk in lefts for slot in chunk] + list(rights)
    return pl.pallas_call(
        lambda *refs: contract_kernel(slot_count, shares, len(rights), *refs),
        grid=(steps, sum(shares)),
        in_specs=in_specs,
        out_specs=pl.BlockSpec(
            (2, parts, unit, columns), lambda c, r: (0, 0, row_first + r, out_first + c)
        ),
        out_shape=jax.ShapeDtypeStruct((2, parts, side, side), jnp.float32),
        input_output_aliases={len(arrays): 0} if alias else {},
        compiler_params=pltpu.CompilerParams(vmem_limit_bytes=VMEM_LIMIT),
        cost_estimate=pl.CostEstimate(
            flops=flops, bytes_accessed=flops // depth, transcendentals=0
        ),
        name="contract",
    )(*arrays, *([result] if alias else []))


def energy_gaps(valence_energy, conduction_energy, band_pairs):
    valence_hot = (
        band_pairs[:, 0][:, None] == jnp.arange(valence_energy.shape[0], dtype=jnp.int32)[None, :]
    )
    conduction_hot = (
        band_pairs[:, 1][:, None]
        == jnp.arange(conduction_energy.shape[0], dtype=jnp.int32)[None, :]
    )
    return jnp.sum(jnp.where(valence_hot, valence_energy[None, :], 0.0), axis=1) - jnp.sum(
        jnp.where(conduction_hot, conduction_energy[None, :], 0.0), axis=1
    )


def after(value, *others):
    return lax.optimization_barrier((value,) + others)[0]


def body(valence, conduction, valence_energy, conduction_energy, band_pairs, grid_index):
    rows, cols = lax.axis_size("row"), lax.axis_size("col")
    row, col = lax.axis_index("row"), lax.axis_index("col")
    pairs = band_pairs.shape[0]
    features = 2 * pairs
    width = rows * features
    block = grid_index.shape[0] // cols
    parts = cols // rows
    unit = block // EIGHTHS
    me = row.astype(jnp.int32).reshape(1)
    my_part = (col % parts).astype(jnp.int32).reshape(1)
    owner = col // parts

    order = list(range(0, cols, 2)) + list(range(1, cols, 2))[::-1]
    ring_up = [(order[q], order[(q + 1) % cols]) for q in range(cols)]
    ring_down = [(b, a) for a, b in ring_up]
    my_place = jnp.asarray(np.argsort(np.array(order)), jnp.int32)[col]
    half = cols // 2
    offsets = [0]
    for t in range(1, half):
        offsets += [-t, t]
    offsets.append(half)
    sources = jnp.asarray(np.array(order), jnp.int32)[
        (my_place + jnp.asarray(np.array(offsets), jnp.int32)) % cols
    ]

    gap = energy_gaps(valence_energy, conduction_energy, band_pairs)
    scale = jnp.sqrt(-2.0 / (math.sqrt(pairs * rows * cols) * gap))

    position = table_position(grid_index).reshape(rows, parts, EIGHTHS, unit)
    positions = [
        position[:, :, first : first + share].reshape(-1) for first, share in CHUNKS
    ]
    sent, table = transform(valence, conduction, band_pairs, scale, positions[0], me, rows)

    def across_rows(parcels):
        return [parcels[0]] + [
            lax.ppermute(parcels[s], "row", [(r, r ^ s) for r in range(rows)])
            for s in range(1, rows)
        ]

    def go_round(below, above):
        return [lax.ppermute(below, "col", ring_up), lax.ppermute(above, "col", ring_down)]

    def last_round(below, above):
        cut = below.shape[0] // 2
        return [jnp.concatenate(go_round(below[:cut], above[cut:]), axis=0)]

    def column(slots, before=(), behind=()):
        slots = [after(slots[0], *before)] + slots[1:] if before else slots
        copies = [flip(slots, my_part, parts, unit)]
        for relation in range(1, rows):
            source = relation & (relation - 1)
            hop = relation ^ source
            held = copies[source]
            if source and behind:
                held = after(held, *behind)
            if hop == 1:
                copies.append(lax.ppermute(held, "row", [(r, r ^ 1) for r in range(rows)]))
                continue
            perm = [
                ((c // parts ^ source) * cols + c, (c // parts ^ relation) * cols + c)
                for c in range(cols)
            ]
            copies.append(lax.ppermute(held, ("row", "col"), perm))
        return copies

    which = (row ^ owner).astype(jnp.int32).reshape(1)

    own = assemble(across_rows(sent), me, features)
    one = [[own], go_round(own, own)]
    sent = select(after(table, own), positions[1], me, rows, features)
    one[1] = [after(block, *sent) for block in one[1]]
    own = assemble(across_rows(sent), me, features)
    one.append(go_round(*one[1]))
    copies = [column(sum(one[:2], []))]
    one[2] = [after(block, own, copies[0][0]) for block in one[2]]
    for t in range(3, half):
        one.append(go_round(*one[t - 1]))
    copies.append(column(sum(one[2 : half - 1], [])))
    below, above = [after(block, copies[1][0]) for block in one[half - 1]]
    one.append(last_round(below, above))
    two = [[own], go_round(*[after(own, below)] * 2)]
    two.append(go_round(*two[1]))
    copies.append(column(sum(one[half - 1 :], []), two[1], two[2]))
    rights = [settle(which, some, pairs) for some in copies]
    for t in range(3, half):
        two.append(go_round(*two[t - 1]))

    def as_lefts(slots):
        return [slot.reshape(parts, -1, width) for slot in sum(slots, [])]

    lefts = as_lefts(one)
    wide = CHUNKS[0][1] // 2
    first = contract(None, [lefts], rights, unit, 0, wide, 0, 1, 0)
    second = contract(first, [lefts], rights, unit, 0, wide, 1, 1, 1)
    middle = half // 2 + 1
    copies = [column(sum(two[:middle], []), two[half - 1] + [first])]
    two.append(last_round(*[after(block, *rights) for block in two[half - 1]]))
    share = CHUNKS[0][1]
    both = [lefts, as_lefts(two)]
    result = contract(second, both[1:], rights, unit, share, share, 0, 1, 0)
    copies.append(column(sum(two[middle:], []), (), (result,)))
    rights = [settle(which, some, pairs) for some in copies]
    result = contract(result, both, rights, unit, 0, share, 0, 1, 1)
    return result.reshape(2, parts * block, block)


def solution(mesh):
    return jax.shard_map(
        body,
        mesh=mesh,
        in_specs=(P(), P(), P(), P(), P(("row", "col"), None), P()),
        out_specs=P(None, "row", "col"),
        check_vma=False,
    )
```

```python
import math

import jax
import jax.numpy as jnp
import ml_dtypes
import numpy as np
from jax import lax
from jax.experimental import pallas as pl
from jax.experimental.pallas import tpu as pltpu
from jax.sharding import PartitionSpec as P

N1 = 32
N2 = 32
N3 = 32
NR = N1 * N2 * N3
LANES = 128
HI = N2 * N3 // LANES
LO = N2 // HI
ROWS = N1 * HI
VMEM_LIMIT = 58 * 1024 * 1024
CHUNKS = ((0, 4), (4, 4))
EIGHTHS = 8
GROUP = 4


def split_bf16(values):
    high = values.astype(ml_dtypes.bfloat16)
    low = (values - high.astype(np.float64)).astype(ml_dtypes.bfloat16)
    return high, low


def dft_tables():
    row = np.arange(ROWS)
    left = np.exp(
        -2j
        * np.pi
        * (
            (row[:, None] // HI) * (row[None, :] // HI) / N1
            + (row[:, None] % HI) * (row[None, :] % HI) / HI
        )
    )
    lane = np.arange(LANES)
    right = np.exp(
        -2j
        * np.pi
        * (
            (lane[:, None] // N3) * (lane[None, :] // N3) / LO
            + (lane[:, None] % N3) * (lane[None, :] % N3) / N3
        )
    )
    twiddle = np.exp(-2j * np.pi * (row[:, None] % HI) * (lane[None, :] // N3) / N2)
    twiddle = twiddle / math.sqrt(NR)
    left_full = np.block([[left.real, -left.imag], [left.imag, left.real]])
    right_full = np.block([[right.real, right.imag], [-right.imag, right.real]])
    left_high, left_low = split_bf16(left_full)
    right_high, right_low = split_bf16(right_full)
    twiddle = np.concatenate([twiddle] * GROUP, axis=1)
    return (
        np.concatenate([left_high, left_low, left_high], axis=1),
        np.concatenate([right_high, right_low], axis=1),
        np.stack([twiddle.real, twiddle.imag]).astype(np.float32),
    )


def table_position(grid_index):
    first = grid_index // (N2 * N3)
    second = grid_index // N3 % N2
    third = grid_index % N3
    return (first * HI + second % HI) * LANES + second // HI * N3 + third


def halves(value):
    high = value.astype(jnp.bfloat16)
    low = (value - high.astype(jnp.float32)).astype(jnp.bfloat16)
    return high, low


def dot(a, b):
    return jnp.dot(a, b, preferred_element_type=jnp.float32)


def select_rows(count, row_count, features, position_ref, me_ref, table, rows, outs):
    pack = LANES // features
    part = count // pack
    unroll = 32
    lane = lax.broadcasted_iota(jnp.int32, (part, LANES), 1)
    for s in range(row_count):
        base = (me_ref[0] ^ s) * count

        def some_rows(step, carry):
            first = step * unroll
            for j in range(unroll):
                index = position_ref[base + first + j]
                rows[pl.ds(first + j, 1), :] = table[pl.ds(index, 1), :]
            return carry

        lax.fori_loop(0, count // unroll, some_rows, 0)
        packed = rows[0:part, :]
        for k in range(1, pack):
            packed = jnp.where(lane >= k * features, rows[k * part : (k + 1) * part, :], packed)
        outs[s][...] = packed.astype(jnp.bfloat16)


def select_kernel(row_count, features, count, position_ref, me_ref, table_ref, *rest):
    select_rows(
        count, row_count, features, position_ref, me_ref, table_ref, rest[-1], rest[:row_count]
    )


def select(table, position, me, row_count, features):
    count = position.shape[0] // row_count
    shape = (count * features // LANES, LANES)
    return pl.pallas_call(
        lambda *refs: select_kernel(row_count, features, count, *refs),
        grid_spec=pltpu.PrefetchScalarGridSpec(
            num_scalar_prefetch=2,
            grid=(),
            in_specs=[pl.BlockSpec(memory_space=pltpu.VMEM)],
            out_specs=[pl.BlockSpec(memory_space=pltpu.VMEM)] * row_count,
            scratch_shapes=[pltpu.VMEM((count, LANES), jnp.float32)],
        ),
        out_shape=[jax.ShapeDtypeStruct(shape, jnp.bfloat16)] * row_count,
        compiler_params=pltpu.CompilerParams(vmem_limit_bytes=VMEM_LIMIT),
        cost_estimate=pl.CostEstimate(flops=0, bytes_accessed=50_000_000, transcendentals=0),
        name="select",
    )(position, me, table)


def transform_kernel(pairs, load_steps, step_rows, count, row_count, *refs):
    position_ref, me_ref, hot_c_ref, hot_v_ref, scale_ref, cond_ref, val_ref = refs[:7]
    left_ref, right_ref, twiddle_ref = refs[7:10]
    outs = refs[10 : 10 + row_count]
    table_ref, rho_r, rho_i, spec, table, middle, rows, sem = refs[10 + row_count :]
    step = pl.program_id(0)
    features = 2 * pairs

    cond = dot(hot_c_ref[...], cond_ref[...])
    val = dot(hot_v_ref[...], val_ref[...]) * scale_ref[...]
    cr, ci = cond[:pairs], cond[pairs:]
    vr, vi = val[:pairs], val[pairs:]
    real = vr * cr + vi * ci
    imag = vr * ci - vi * cr
    for a in range(step_rows):
        row = pl.multiple_of((step * step_rows + a) * pairs, pairs)
        rho_r[pl.ds(row, pairs), :] = real[:, a * LANES : (a + 1) * LANES]
        rho_i[pl.ds(row, pairs), :] = imag[:, a * LANES : (a + 1) * LANES]

    def left_half(group, slot):
        members = [GROUP * group + k for k in range(GROUP)]
        data = jnp.concatenate(
            [
                jnp.concatenate([ref[pl.ds(p, ROWS, stride=pairs), :] for p in members], axis=1)
                for ref in (rho_r, rho_i)
            ],
            axis=0,
        )
        high, low = halves(data)
        mixed = dot(left_ref[...], jnp.concatenate([high, high, low], axis=0))
        mid_r, mid_i = mixed[:ROWS], mixed[ROWS:]
        tr, ti = twiddle_ref[0], twiddle_ref[1]
        turn_r = mid_r * tr - mid_i * ti
        turn_i = mid_r * ti + mid_i * tr
        for k in range(GROUP):
            lanes = slice(k * LANES, (k + 1) * LANES)
            rows_k = slice(k * ROWS, (k + 1) * ROWS)
            for z, turned in enumerate((turn_r, turn_i)):
                high, low = halves(turned[:, lanes])
                middle[slot, rows_k, z * LANES : (z + 1) * LANES] = high
                middle[slot, rows_k, (2 + z) * LANES : (3 + z) * LANES] = low

    def right_half(group, slot):
        high = middle[slot, :, : 2 * LANES]
        low = middle[slot, :, 2 * LANES :]
        by_high = dot(high, right_ref[...])
        by_low = dot(low, right_ref[:, : 2 * LANES])
        out = by_high[:, : 2 * LANES] + (by_high[:, 2 * LANES :] + by_low)
        for k in range(GROUP):
            p = GROUP * group + k
            part = out[k * ROWS : (k + 1) * ROWS]
            spec[pl.ds(p, ROWS, stride=features), :] = part[:, :LANES]
            spec[pl.ds(pairs + p, ROWS, stride=features), :] = part[:, LANES:]

    @pl.when(step == load_steps - 1)
    def _():
        groups = pairs // GROUP
        left_half(0, 0)

        def two_groups(k, carry):
            right_half(2 * k, 0)
            left_half(2 * k + 1, 1)
            right_half(2 * k + 1, 1)
            left_half(jnp.minimum(2 * k + 2, groups - 1), 0)
            return carry

        lax.fori_loop(0, groups // 2, two_groups, 0)

        def one_row(k, carry):
            start = pl.multiple_of(k * features, features)
            tile = spec[pl.ds(start, features), :].astype(jnp.bfloat16)
            tile = jnp.concatenate([tile] * (LANES // features), axis=0)
            table[pl.ds(pl.multiple_of(k * LANES, LANES), LANES), :] = tile.T.astype(jnp.float32)
            return carry

        lax.fori_loop(0, ROWS, one_row, 0, unroll=8)
        keep = pltpu.make_async_copy(table, table_ref, sem)
        keep.start()
        select_rows(count, row_count, features, position_ref, me_ref, table, rows, outs)
        keep.wait()


def transform(valence, conduction, band_pairs, scale, position, me, row_count):
    count = position.shape[0] // row_count
    pairs = band_pairs.shape[0]
    features = 2 * pairs
    pack = LANES // features
    nvb, ncb = valence.shape[1], conduction.shape[1]
    load_steps = 8
    step_rows = ROWS // load_steps
    chunk = step_rows * LANES

    def hot(band, count):
        one = (band[:, None] == jnp.arange(count, dtype=jnp.int32)[None, :]).astype(jnp.bfloat16)
        none = jnp.zeros_like(one)
        return jnp.concatenate(
            [jnp.concatenate([one, none], axis=1), jnp.concatenate([none, one], axis=1)], axis=0
        )

    left, right, twiddle = dft_tables()
    whole = lambda shape: pl.BlockSpec(shape, lambda i, *_: (0,) * len(shape))
    loaded = lambda i, *_: (0, i)
    flops = 2 * pairs * (6 * ROWS * ROWS * 2 * LANES + 3 * ROWS * 4 * LANES * LANES)
    out_shapes = [(count // pack, LANES)] * row_count
    outs = pl.pallas_call(
        lambda *refs: transform_kernel(pairs, load_steps, step_rows, count, row_count, *refs),
        grid_spec=pltpu.PrefetchScalarGridSpec(
            num_scalar_prefetch=2,
            grid=(load_steps,),
            in_specs=[
                whole((2 * pairs, 2 * ncb)),
                whole((2 * pairs, 2 * nvb)),
                whole((2 * pairs, 1)),
                pl.BlockSpec((2 * ncb, chunk), loaded),
                pl.BlockSpec((2 * nvb, chunk), loaded),
                whole(left.shape),
                whole(right.shape),
                whole(twiddle.shape),
            ],
            out_specs=[whole(shape) for shape in out_shapes] + [pl.BlockSpec(memory_space=pl.ANY)],
            scratch_shapes=[
                pltpu.VMEM((ROWS * pairs, LANES), jnp.float32),
                pltpu.VMEM((ROWS * pairs, LANES), jnp.float32),
                pltpu.VMEM((ROWS * features, LANES), jnp.float32),
                pltpu.VMEM((NR, LANES), jnp.float32),
                pltpu.VMEM((2, GROUP * ROWS, 4 * LANES), jnp.bfloat16),
                pltpu.VMEM((count, LANES), jnp.float32),
                pltpu.SemaphoreType.DMA,
            ],
        ),
        out_shape=[jax.ShapeDtypeStruct(shape, jnp.bfloat16) for shape in out_shapes]
        + [jax.ShapeDtypeStruct((NR, LANES), jnp.float32)],
        compiler_params=pltpu.CompilerParams(vmem_limit_bytes=VMEM_LIMIT),
        cost_estimate=pl.CostEstimate(flops=flops, bytes_accessed=40_000_000, transcendentals=0),
        name="transform",
    )(
        position,
        me,
        hot(band_pairs[:, 1], ncb),
        hot(band_pairs[:, 0], nvb),
        jnp.concatenate([scale, scale])[:, None],
        conduction.reshape(2 * ncb, NR),
        valence.reshape(2 * nvb, NR),
        jnp.asarray(left),
        jnp.asarray(right),
        jnp.asarray(twiddle),
    )
    return outs[:row_count], outs[row_count]


def assemble_kernel(row_count, features, me_ref, *rest):
    parts, out_ref, held = rest[:row_count], rest[row_count], rest[row_count + 1]
    pack = LANES // features
    part = parts[0].shape[0]
    lane = lax.broadcasted_iota(jnp.int32, (part, LANES), 1)
    for s in range(row_count):
        held[s] = parts[s][...].astype(jnp.float32)
    for b in range(row_count // pack):
        for k in range(pack):
            block = None
            for q in range(pack):
                piece = held[(b * pack + q) ^ me_ref[0]]
                if q != k:
                    piece = pltpu.roll(piece, (q - k) * features % LANES, 1)
                block = piece if block is None else jnp.where(lane >= q * features, piece, block)
            out_ref[k * part : (k + 1) * part, b * LANES : (b + 1) * LANES] = block.astype(
                jnp.bfloat16
            )


def assemble(parts, me, features):
    row_count = len(parts)
    pack = LANES // features
    part = parts[0].shape[0]
    return pl.pallas_call(
        lambda *refs: assemble_kernel(row_count, features, *refs),
        grid_spec=pltpu.PrefetchScalarGridSpec(
            num_scalar_prefetch=1,
            grid=(),
            in_specs=[pl.BlockSpec(memory_space=pltpu.VMEM)] * row_count,
            out_specs=pl.BlockSpec(memory_space=pltpu.VMEM),
            scratch_shapes=[pltpu.VMEM((row_count, part, LANES), jnp.float32)],
        ),
        out_shape=jax.ShapeDtypeStruct((part * pack, row_count * features), jnp.bfloat16),
        compiler_params=pltpu.CompilerParams(vmem_limit_bytes=VMEM_LIMIT),
        cost_estimate=pl.CostEstimate(flops=0, bytes_accessed=2_000_000, transcendentals=0),
        name="assemble",
    )(me, *parts)


def flip_kernel(slot_count, part_ref, *refs):
    out_ref = refs[slot_count]
    for s in range(slot_count):
        width = refs[s].shape[1]
        out_ref[s * width : (s + 1) * width, :] = refs[s][...].T


def flip(slots, part, parts, unit):
    slot_count = len(slots)
    width = slots[0].shape[1]
    depth = slots[0].shape[0] // parts
    steps = depth // unit
    return pl.pallas_call(
        lambda *refs: flip_kernel(slot_count, *refs),
        grid_spec=pltpu.PrefetchScalarGridSpec(
            num_scalar_prefetch=1,
            grid=(steps,),
            in_specs=[
                pl.BlockSpec((unit, width), lambda t, part_ref: (part_ref[0] * steps + t, 0))
            ]
            * slot_count,
            out_specs=pl.BlockSpec((slot_count * width, unit), lambda t, part_ref: (0, t)),
        ),
        out_shape=jax.ShapeDtypeStruct((slot_count * width, depth), jnp.bfloat16),
        compiler_params=pltpu.CompilerParams(vmem_limit_bytes=VMEM_LIMIT),
        cost_estimate=pl.CostEstimate(
            flops=0, bytes_accessed=8 * slot_count * width * depth, transcendentals=0
        ),
        name="flip",
    )(part, *slots)


def settle_kernel(pairs, row_count, which_ref, *refs):
    out_ref = refs[row_count]
    kind = jnp.float32 if pairs % 16 else jnp.bfloat16
    for k in range(row_count):

        @pl.when(which_ref[0] == k)
        def _():
            values = -refs[k][...].astype(kind)
            rows, across = values.shape
            out_ref[0] = values.astype(jnp.bfloat16)
            values = values.reshape(rows // (2 * pairs), 2, pairs, across)
            turned = jnp.stack([values[:, 1], -values[:, 0]], axis=1)
            out_ref[1] = turned.reshape(rows, across).astype(jnp.bfloat16)


def settle(which, copies, pairs):
    rows, across = copies[0].shape
    tile = math.gcd(rows, 256)
    row_count = len(copies)

    def pick(k):
        return lambda t, which_ref: (jnp.where(which_ref[0] == k, t, 0), 0)

    return pl.pallas_call(
        lambda *refs: settle_kernel(pairs, row_count, *refs),
        grid_spec=pltpu.PrefetchScalarGridSpec(
            num_scalar_prefetch=1,
            grid=(rows // tile,),
            in_specs=[pl.BlockSpec((tile, across), pick(k)) for k in range(row_count)],
            out_specs=pl.BlockSpec((2, tile, across), lambda t, _: (0, t, 0)),
        ),
        out_shape=jax.ShapeDtypeStruct((2, rows, across), jnp.bfloat16),
        compiler_params=pltpu.CompilerParams(vmem_limit_bytes=VMEM_LIMIT),
        cost_estimate=pl.CostEstimate(
            flops=0, bytes_accessed=8 * rows * across, transcendentals=0
        ),
        name="settle",
    )(which, *copies)


def contract_kernel(slot_count, shares, right_count, *refs):
    rights = refs[len(shares) * slot_count : len(shares) * slot_count + right_count]
    out_ref = refs[-1]
    row = pl.program_id(1)
    for k, share in enumerate(shares):
        start = sum(shares[:k])

        @pl.when((row >= start) & (row < start + share))
        def _():
            slots = refs[k * slot_count : (k + 1) * slot_count]
            parts, depth, width = slots[0].shape
            left = jnp.concatenate(
                [slot[...].reshape(parts * depth, width) for slot in slots], axis=1
            )
            for z in range(2):
                right = jnp.concatenate([ref[z] for ref in rights], axis=0)
                out_ref[z] = dot(left, right).reshape(out_ref.shape[1:])


def contract(result, lefts, rights, unit, row_first, wide, tile_first, steps, out_first):
    parts, _, width = lefts[0][0].shape
    slot_count = len(lefts[0])
    shares = [chunk[0].shape[1] // unit for chunk in lefts]
    depth = slot_count * width
    columns, side = wide * unit, EIGHTHS * unit
    alias = 0 if result is None else 1
    flops = 8 * parts * sum(shares) * unit * steps * columns * depth

    def place(start, share):
        return lambda c, r: (0, jnp.clip(r - start, 0, share - 1), 0)

    in_specs = [
        pl.BlockSpec((parts, unit, width), place(sum(shares[:k]), share))
        for k, share in enumerate(shares)
        for _ in range(slot_count)
    ]
    in_specs += [
        pl.BlockSpec((2, right.shape[1], columns), lambda c, r: (0, 0, tile_first + c))
        for right in rights
    ]
    if alias:
        in_specs.append(pl.BlockSpec(memory_space=pl.ANY))
    arrays = [slot for chunk in lefts for slot in chunk] + list(rights)
    return pl.pallas_call(
        lambda *refs: contract_kernel(slot_count, shares, len(rights), *refs),
        grid=(steps, sum(shares)),
        in_specs=in_specs,
        out_specs=pl.BlockSpec(
            (2, parts, unit, columns), lambda c, r: (0, 0, row_first + r, out_first + c)
        ),
        out_shape=jax.ShapeDtypeStruct((2, parts, side, side), jnp.float32),
        input_output_aliases={len(arrays): 0} if alias else {},
        compiler_params=pltpu.CompilerParams(vmem_limit_bytes=VMEM_LIMIT),
        cost_estimate=pl.CostEstimate(
            flops=flops, bytes_accessed=flops // depth, transcendentals=0
        ),
        name="contract",
    )(*arrays, *([result] if alias else []))


def energy_gaps(valence_energy, conduction_energy, band_pairs):
    valence_hot = (
        band_pairs[:, 0][:, None] == jnp.arange(valence_energy.shape[0], dtype=jnp.int32)[None, :]
    )
    conduction_hot = (
        band_pairs[:, 1][:, None]
        == jnp.arange(conduction_energy.shape[0], dtype=jnp.int32)[None, :]
    )
    return jnp.sum(jnp.where(valence_hot, valence_energy[None, :], 0.0), axis=1) - jnp.sum(
        jnp.where(conduction_hot, conduction_energy[None, :], 0.0), axis=1
    )


def after(value, *others):
    return lax.optimization_barrier((value,) + others)[0]


def body(valence, conduction, valence_energy, conduction_energy, band_pairs, grid_index):
    rows, cols = lax.axis_size("row"), lax.axis_size("col")
    row, col = lax.axis_index("row"), lax.axis_index("col")
    pairs = band_pairs.shape[0]
    features = 2 * pairs
    width = rows * features
    block = grid_index.shape[0] // cols
    parts = cols // rows
    unit = block // EIGHTHS
    me = row.astype(jnp.int32).reshape(1)
    my_part = (col % parts).astype(jnp.int32).reshape(1)
    owner = col // parts

    order = list(range(0, cols, 2)) + list(range(1, cols, 2))[::-1]
    ring_up = [(order[q], order[(q + 1) % cols]) for q in range(cols)]
    ring_down = [(b, a) for a, b in ring_up]
    my_place = jnp.asarray(np.argsort(np.array(order)), jnp.int32)[col]
    half = cols // 2
    offsets = [0]
    for t in range(1, half):
        offsets += [-t, t]
    offsets.append(half)
    sources = jnp.asarray(np.array(order), jnp.int32)[
        (my_place + jnp.asarray(np.array(offsets), jnp.int32)) % cols
    ]

    gap = energy_gaps(valence_energy, conduction_energy, band_pairs)
    scale = jnp.sqrt(-2.0 / (math.sqrt(pairs * rows * cols) * gap))

    position = table_position(grid_index).reshape(rows, parts, EIGHTHS, unit)
    positions = [
        position[:, :, first : first + share].reshape(-1) for first, share in CHUNKS
    ]
    sent, table = transform(valence, conduction, band_pairs, scale, positions[0], me, rows)

    def across_rows(parcels):
        return [parcels[0]] + [
            lax.ppermute(parcels[s], "row", [(r, r ^ s) for r in range(rows)])
            for s in range(1, rows)
        ]

    def go_round(below, above):
        return [lax.ppermute(below, "col", ring_up), lax.ppermute(above, "col", ring_down)]

    def last_round(below, above):
        cut = below.shape[0] // 2
        return [jnp.concatenate(go_round(below[:cut], above[cut:]), axis=0)]

    def column(slots, before=(), behind=()):
        slots = [after(slots[0], *before)] + slots[1:] if before else slots
        copies = [flip(slots, my_part, parts, unit)]
        for relation in range(1, rows):
            source = relation & (relation - 1)
            hop = relation ^ source
            held = copies[source]
            if source and behind:
                held = after(held, *behind)
            if hop == 1:
                copies.append(lax.ppermute(held, "row", [(r, r ^ 1) for r in range(rows)]))
                continue
            perm = [
                ((c // parts ^ source) * cols + c, (c // parts ^ relation) * cols + c)
                for c in range(cols)
            ]
            copies.append(lax.ppermute(held, ("row", "col"), perm))
        return copies

    which = (row ^ owner).astype(jnp.int32).reshape(1)

    own = assemble(across_rows(sent), me, features)
    one = [[own], go_round(own, own)]
    sent = select(after(table, own), positions[1], me, rows, features)
    one[1] = [after(block, *sent) for block in one[1]]
    own = assemble(across_rows([after(part, *one[1]) for part in sent]), me, features)
    one.append(go_round(*one[1]))
    copies = [column(sum(one[:2], []), (own,))]
    one[2] = [after(block, own, copies[0][0]) for block in one[2]]
    for t in range(3, half):
        one.append(go_round(*one[t - 1]))
    copies.append(column(sum(one[2 : half - 1], [])))
    below, above = [after(block, copies[1][0]) for block in one[half - 1]]
    copies.append(column(one[half - 1]))
    one.append(last_round(below, above))
    two = [[own], go_round(*[after(own, *one[half])] * 2)]
    copies.append(column(one[half], (), two[1]))
    rights = [settle(which, some, pairs) for some in copies]
    two.append(go_round(*[after(block, *rights[:2]) for block in two[1]]))

    def as_lefts(slots):
        return [slot.reshape(parts, -1, width) for slot in sum(slots, [])]

    lefts = as_lefts(one)
    wide = CHUNKS[0][1] // 2
    first = contract(None, [lefts], rights, unit, 0, wide, 0, 1, 0)
    second = contract(first, [lefts], rights, unit, 0, wide, 1, 1, 1)
    copies = [column(sum(two[:2], []), two[2])]
    two.append(go_round(*[after(block, first) for block in two[2]]))
    for t in range(4, half):
        two.append(go_round(*two[t - 1]))
    copies.append(column(sum(two[2:half], []), two[half - 1]))
    two.append(last_round(*[after(block, second, copies[0][0]) for block in two[half - 1]]))
    share = CHUNKS[0][1]
    both = [lefts, as_lefts(two)]
    result = contract(second, both[1:], rights, unit, share, share, 0, 1, 0)
    copies.append(column(two[half], (), (result,)))
    rights = [settle(which, some, pairs) for some in copies]
    result = contract(result, both, rights, unit, 0, share, 0, 1, 1)
    return result.reshape(2, parts * block, block)


def solution(mesh):
    return jax.shard_map(
        body,
        mesh=mesh,
        in_specs=(P(), P(), P(), P(), P(("row", "col"), None), P()),
        out_specs=P(None, "row", "col"),
        check_vma=False,
    )
```

```python
import math

import jax
import jax.numpy as jnp
import ml_dtypes
import numpy as np
from jax import lax
from jax.experimental import pallas as pl
from jax.experimental.pallas import tpu as pltpu
from jax.sharding import PartitionSpec as P

N1 = 32
N2 = 32
N3 = 32
NR = N1 * N2 * N3
LANES = 128
HI = N2 * N3 // LANES
LO = N2 // HI
ROWS = N1 * HI
VMEM_LIMIT = 58 * 1024 * 1024
CHUNKS = ((0, 4), (4, 4))
EIGHTHS = 8
GROUP = 4


def split_bf16(values):
    high = values.astype(ml_dtypes.bfloat16)
    low = (values - high.astype(np.float64)).astype(ml_dtypes.bfloat16)
    return high, low


def dft_tables():
    row = np.arange(ROWS)
    left = np.exp(
        -2j
        * np.pi
        * (
            (row[:, None] // HI) * (row[None, :] // HI) / N1
            + (row[:, None] % HI) * (row[None, :] % HI) / HI
        )
    )
    lane = np.arange(LANES)
    right = np.exp(
        -2j
        * np.pi
        * (
            (lane[:, None] // N3) * (lane[None, :] // N3) / LO
            + (lane[:, None] % N3) * (lane[None, :] % N3) / N3
        )
    )
    twiddle = np.exp(-2j * np.pi * (row[:, None] % HI) * (lane[None, :] // N3) / N2)
    twiddle = twiddle / math.sqrt(NR)
    left_full = np.block([[left.real, -left.imag], [left.imag, left.real]])
    right_full = np.block([[right.real, right.imag], [-right.imag, right.real]])
    left_high, left_low = split_bf16(left_full)
    right_high, right_low = split_bf16(right_full)
    twiddle = np.concatenate([twiddle] * GROUP, axis=1)
    return (
        np.concatenate([left_high, left_low, left_high], axis=1),
        np.concatenate([right_high, right_low], axis=1),
        np.stack([twiddle.real, twiddle.imag]).astype(np.float32),
    )


def table_position(grid_index):
    first = grid_index // (N2 * N3)
    second = grid_index // N3 % N2
    third = grid_index % N3
    return (first * HI + second % HI) * LANES + second // HI * N3 + third


def halves(value):
    high = value.astype(jnp.bfloat16)
    low = (value - high.astype(jnp.float32)).astype(jnp.bfloat16)
    return high, low


def dot(a, b):
    return jnp.dot(a, b, preferred_element_type=jnp.float32)


def select_rows(count, row_count, features, position_ref, me_ref, table, rows, outs):
    pack = LANES // features
    part = count // pack
    unroll = 32
    lane = lax.broadcasted_iota(jnp.int32, (part, LANES), 1)
    for s in range(row_count):
        base = (me_ref[0] ^ s) * count

        def some_rows(step, carry):
            first = step * unroll
            for j in range(unroll):
                index = position_ref[base + first + j]
                rows[pl.ds(first + j, 1), :] = table[pl.ds(index, 1), :]
            return carry

        lax.fori_loop(0, count // unroll, some_rows, 0)
        packed = rows[0:part, :]
        for k in range(1, pack):
            packed = jnp.where(lane >= k * features, rows[k * part : (k + 1) * part, :], packed)
        outs[s][...] = packed.astype(jnp.bfloat16)


def select_kernel(row_count, features, count, position_ref, me_ref, table_ref, *rest):
    select_rows(
        count, row_count, features, position_ref, me_ref, table_ref, rest[-1], rest[:row_count]
    )


def select(table, position, me, row_count, features):
    count = position.shape[0] // row_count
    shape = (count * features // LANES, LANES)
    return pl.pallas_call(
        lambda *refs: select_kernel(row_count, features, count, *refs),
        grid_spec=pltpu.PrefetchScalarGridSpec(
            num_scalar_prefetch=2,
            grid=(),
            in_specs=[pl.BlockSpec(memory_space=pltpu.VMEM)],
            out_specs=[pl.BlockSpec(memory_space=pltpu.VMEM)] * row_count,
            scratch_shapes=[pltpu.VMEM((count, LANES), jnp.float32)],
        ),
        out_shape=[jax.ShapeDtypeStruct(shape, jnp.bfloat16)] * row_count,
        compiler_params=pltpu.CompilerParams(vmem_limit_bytes=VMEM_LIMIT),
        cost_estimate=pl.CostEstimate(flops=0, bytes_accessed=50_000_000, transcendentals=0),
        name="select",
    )(position, me, table)


def transform_kernel(pairs, load_steps, step_rows, count, row_count, *refs):
    position_ref, me_ref, hot_c_ref, hot_v_ref, scale_ref, cond_ref, val_ref = refs[:7]
    left_ref, right_ref, twiddle_ref = refs[7:10]
    outs = refs[10 : 10 + row_count]
    table_ref, rho_r, rho_i, spec, table, middle, rows, sem = refs[10 + row_count :]
    step = pl.program_id(0)
    features = 2 * pairs

    cond = dot(hot_c_ref[...], cond_ref[...])
    val = dot(hot_v_ref[...], val_ref[...]) * scale_ref[...]
    cr, ci = cond[:pairs], cond[pairs:]
    vr, vi = val[:pairs], val[pairs:]
    real = vr * cr + vi * ci
    imag = vr * ci - vi * cr
    for a in range(step_rows):
        row = pl.multiple_of((step * step_rows + a) * pairs, pairs)
        rho_r[pl.ds(row, pairs), :] = real[:, a * LANES : (a + 1) * LANES]
        rho_i[pl.ds(row, pairs), :] = imag[:, a * LANES : (a + 1) * LANES]

    def left_half(group, slot):
        members = [GROUP * group + k for k in range(GROUP)]
        data = jnp.concatenate(
            [
                jnp.concatenate([ref[pl.ds(p, ROWS, stride=pairs), :] for p in members], axis=1)
                for ref in (rho_r, rho_i)
            ],
            axis=0,
        )
        high, low = halves(data)
        mixed = dot(left_ref[...], jnp.concatenate([high, high, low], axis=0))
        mid_r, mid_i = mixed[:ROWS], mixed[ROWS:]
        tr, ti = twiddle_ref[0], twiddle_ref[1]
        turn_r = mid_r * tr - mid_i * ti
        turn_i = mid_r * ti + mid_i * tr
        for k in range(GROUP):
            lanes = slice(k * LANES, (k + 1) * LANES)
            rows_k = slice(k * ROWS, (k + 1) * ROWS)
            for z, turned in enumerate((turn_r, turn_i)):
                high, low = halves(turned[:, lanes])
                middle[slot, rows_k, z * LANES : (z + 1) * LANES] = high
                middle[slot, rows_k, (2 + z) * LANES : (3 + z) * LANES] = low

    def right_half(group, slot):
        high = middle[slot, :, : 2 * LANES]
        low = middle[slot, :, 2 * LANES :]
        by_high = dot(high, right_ref[...])
        by_low = dot(low, right_ref[:, : 2 * LANES])
        out = by_high[:, : 2 * LANES] + (by_high[:, 2 * LANES :] + by_low)
        for k in range(GROUP):
            p = GROUP * group + k
            part = out[k * ROWS : (k + 1) * ROWS]
            spec[pl.ds(p, ROWS, stride=features), :] = part[:, :LANES]
            spec[pl.ds(pairs + p, ROWS, stride=features), :] = part[:, LANES:]

    @pl.when(step == load_steps - 1)
    def _():
        groups = pairs // GROUP
        left_half(0, 0)

        def two_groups(k, carry):
            right_half(2 * k, 0)
            left_half(2 * k + 1, 1)
            right_half(2 * k + 1, 1)
            left_half(jnp.minimum(2 * k + 2, groups - 1), 0)
            return carry

        lax.fori_loop(0, groups // 2, two_groups, 0)

        def one_row(k, carry):
            start = pl.multiple_of(k * features, features)
            tile = spec[pl.ds(start, features), :].astype(jnp.bfloat16)
            tile = jnp.concatenate([tile] * (LANES // features), axis=0)
            table[pl.ds(pl.multiple_of(k * LANES, LANES), LANES), :] = tile.T.astype(jnp.float32)
            return carry

        lax.fori_loop(0, ROWS, one_row, 0, unroll=8)
        keep = pltpu.make_async_copy(table, table_ref, sem)
        keep.start()
        select_rows(count, row_count, features, position_ref, me_ref, table, rows, outs)
        keep.wait()


def transform(valence, conduction, band_pairs, scale, position, me, row_count):
    count = position.shape[0] // row_count
    pairs = band_pairs.shape[0]
    features = 2 * pairs
    pack = LANES // features
    nvb, ncb = valence.shape[1], conduction.shape[1]
    load_steps = 8
    step_rows = ROWS // load_steps
    chunk = step_rows * LANES

    def hot(band, count):
        one = (band[:, None] == jnp.arange(count, dtype=jnp.int32)[None, :]).astype(jnp.bfloat16)
        none = jnp.zeros_like(one)
        return jnp.concatenate(
            [jnp.concatenate([one, none], axis=1), jnp.concatenate([none, one], axis=1)], axis=0
        )

    left, right, twiddle = dft_tables()
    whole = lambda shape: pl.BlockSpec(shape, lambda i, *_: (0,) * len(shape))
    loaded = lambda i, *_: (0, i)
    flops = 2 * pairs * (6 * ROWS * ROWS * 2 * LANES + 3 * ROWS * 4 * LANES * LANES)
    out_shapes = [(count // pack, LANES)] * row_count
    outs = pl.pallas_call(
        lambda *refs: transform_kernel(pairs, load_steps, step_rows, count, row_count, *refs),
        grid_spec=pltpu.PrefetchScalarGridSpec(
            num_scalar_prefetch=2,
            grid=(load_steps,),
            in_specs=[
                whole((2 * pairs, 2 * ncb)),
                whole((2 * pairs, 2 * nvb)),
                whole((2 * pairs, 1)),
                pl.BlockSpec((2 * ncb, chunk), loaded),
                pl.BlockSpec((2 * nvb, chunk), loaded),
                whole(left.shape),
                whole(right.shape),
                whole(twiddle.shape),
            ],
            out_specs=[whole(shape) for shape in out_shapes] + [pl.BlockSpec(memory_space=pl.ANY)],
            scratch_shapes=[
                pltpu.VMEM((ROWS * pairs, LANES), jnp.float32),
                pltpu.VMEM((ROWS * pairs, LANES), jnp.float32),
                pltpu.VMEM((ROWS * features, LANES), jnp.float32),
                pltpu.VMEM((NR, LANES), jnp.float32),
                pltpu.VMEM((2, GROUP * ROWS, 4 * LANES), jnp.bfloat16),
                pltpu.VMEM((count, LANES), jnp.float32),
                pltpu.SemaphoreType.DMA,
            ],
        ),
        out_shape=[jax.ShapeDtypeStruct(shape, jnp.bfloat16) for shape in out_shapes]
        + [jax.ShapeDtypeStruct((NR, LANES), jnp.float32)],
        compiler_params=pltpu.CompilerParams(vmem_limit_bytes=VMEM_LIMIT),
        cost_estimate=pl.CostEstimate(flops=flops, bytes_accessed=40_000_000, transcendentals=0),
        name="transform",
    )(
        position,
        me,
        hot(band_pairs[:, 1], ncb),
        hot(band_pairs[:, 0], nvb),
        jnp.concatenate([scale, scale])[:, None],
        conduction.reshape(2 * ncb, NR),
        valence.reshape(2 * nvb, NR),
        jnp.asarray(left),
        jnp.asarray(right),
        jnp.asarray(twiddle),
    )
    return outs[:row_count], outs[row_count]


def assemble_kernel(row_count, features, me_ref, *rest):
    parts, out_ref, held = rest[:row_count], rest[row_count], rest[row_count + 1]
    pack = LANES // features
    part = parts[0].shape[0]
    lane = lax.broadcasted_iota(jnp.int32, (part, LANES), 1)
    for s in range(row_count):
        held[s] = parts[s][...].astype(jnp.float32)
    for b in range(row_count // pack):
        for k in range(pack):
            block = None
            for q in range(pack):
                piece = held[(b * pack + q) ^ me_ref[0]]
                if q != k:
                    piece = pltpu.roll(piece, (q - k) * features % LANES, 1)
                block = piece if block is None else jnp.where(lane >= q * features, piece, block)
            out_ref[k * part : (k + 1) * part, b * LANES : (b + 1) * LANES] = block.astype(
                jnp.bfloat16
            )


def assemble(parts, me, features):
    row_count = len(parts)
    pack = LANES // features
    part = parts[0].shape[0]
    return pl.pallas_call(
        lambda *refs: assemble_kernel(row_count, features, *refs),
        grid_spec=pltpu.PrefetchScalarGridSpec(
            num_scalar_prefetch=1,
            grid=(),
            in_specs=[pl.BlockSpec(memory_space=pltpu.VMEM)] * row_count,
            out_specs=pl.BlockSpec(memory_space=pltpu.VMEM),
            scratch_shapes=[pltpu.VMEM((row_count, part, LANES), jnp.float32)],
        ),
        out_shape=jax.ShapeDtypeStruct((part * pack, row_count * features), jnp.bfloat16),
        compiler_params=pltpu.CompilerParams(vmem_limit_bytes=VMEM_LIMIT),
        cost_estimate=pl.CostEstimate(flops=0, bytes_accessed=2_000_000, transcendentals=0),
        name="assemble",
    )(me, *parts)


def flip_kernel(slot_count, part_ref, *refs):
    out_ref = refs[slot_count]
    for s in range(slot_count):
        width = refs[s].shape[1]
        out_ref[s * width : (s + 1) * width, :] = refs[s][...].T


def flip(slots, part, parts, unit):
    slot_count = len(slots)
    width = slots[0].shape[1]
    depth = slots[0].shape[0] // parts
    steps = depth // unit
    return pl.pallas_call(
        lambda *refs: flip_kernel(slot_count, *refs),
        grid_spec=pltpu.PrefetchScalarGridSpec(
            num_scalar_prefetch=1,
            grid=(steps,),
            in_specs=[
                pl.BlockSpec((unit, width), lambda t, part_ref: (part_ref[0] * steps + t, 0))
            ]
            * slot_count,
            out_specs=pl.BlockSpec((slot_count * width, unit), lambda t, part_ref: (0, t)),
        ),
        out_shape=jax.ShapeDtypeStruct((slot_count * width, depth), jnp.bfloat16),
        compiler_params=pltpu.CompilerParams(vmem_limit_bytes=VMEM_LIMIT),
        cost_estimate=pl.CostEstimate(
            flops=0, bytes_accessed=8 * slot_count * width * depth, transcendentals=0
        ),
        name="flip",
    )(part, *slots)


def settle_kernel(pairs, row_count, which_ref, *refs):
    out_ref = refs[row_count]
    kind = jnp.float32 if pairs % 16 else jnp.bfloat16
    for k in range(row_count):

        @pl.when(which_ref[0] == k)
        def _():
            values = -refs[k][...].astype(kind)
            rows, across = values.shape
            out_ref[0] = values.astype(jnp.bfloat16)
            values = values.reshape(rows // (2 * pairs), 2, pairs, across)
            turned = jnp.stack([values[:, 1], -values[:, 0]], axis=1)
            out_ref[1] = turned.reshape(rows, across).astype(jnp.bfloat16)


def settle(which, copies, pairs):
    rows, across = copies[0].shape
    tile = math.gcd(rows, 256)
    row_count = len(copies)

    def pick(k):
        return lambda t, which_ref: (jnp.where(which_ref[0] == k, t, 0), 0)

    return pl.pallas_call(
        lambda *refs: settle_kernel(pairs, row_count, *refs),
        grid_spec=pltpu.PrefetchScalarGridSpec(
            num_scalar_prefetch=1,
            grid=(rows // tile,),
            in_specs=[pl.BlockSpec((tile, across), pick(k)) for k in range(row_count)],
            out_specs=pl.BlockSpec((2, tile, across), lambda t, _: (0, t, 0)),
        ),
        out_shape=jax.ShapeDtypeStruct((2, rows, across), jnp.bfloat16),
        compiler_params=pltpu.CompilerParams(vmem_limit_bytes=VMEM_LIMIT),
        cost_estimate=pl.CostEstimate(
            flops=0, bytes_accessed=8 * rows * across, transcendentals=0
        ),
        name="settle",
    )(which, *copies)


def contract_kernel(slot_count, shares, right_count, *refs):
    rights = refs[len(shares) * slot_count : len(shares) * slot_count + right_count]
    out_ref = refs[-1]
    row = pl.program_id(1)
    for k, share in enumerate(shares):
        start = sum(shares[:k])

        @pl.when((row >= start) & (row < start + share))
        def _():
            slots = refs[k * slot_count : (k + 1) * slot_count]
            parts, depth, width = slots[0].shape
            left = jnp.concatenate(
                [slot[...].reshape(parts * depth, width) for slot in slots], axis=1
            )
            for z in range(2):
                right = jnp.concatenate([ref[z] for ref in rights], axis=0)
                out_ref[z] = dot(left, right).reshape(out_ref.shape[1:])


def contract(result, lefts, rights, unit, row_first, wide, tile_first, steps, out_first):
    parts, _, width = lefts[0][0].shape
    slot_count = len(lefts[0])
    shares = [chunk[0].shape[1] // unit for chunk in lefts]
    depth = slot_count * width
    columns, side = wide * unit, EIGHTHS * unit
    alias = 0 if result is None else 1
    flops = 8 * parts * sum(shares) * unit * steps * columns * depth

    def place(start, share):
        return lambda c, r: (0, jnp.clip(r - start, 0, share - 1), 0)

    in_specs = [
        pl.BlockSpec((parts, unit, width), place(sum(shares[:k]), share))
        for k, share in enumerate(shares)
        for _ in range(slot_count)
    ]
    in_specs += [
        pl.BlockSpec((2, right.shape[1], columns), lambda c, r: (0, 0, tile_first + c))
        for right in rights
    ]
    if alias:
        in_specs.append(pl.BlockSpec(memory_space=pl.ANY))
    arrays = [slot for chunk in lefts for slot in chunk] + list(rights)
    return pl.pallas_call(
        lambda *refs: contract_kernel(slot_count, shares, len(rights), *refs),
        grid=(steps, sum(shares)),
        in_specs=in_specs,
        out_specs=pl.BlockSpec(
            (2, parts, unit, columns), lambda c, r: (0, 0, row_first + r, out_first + c)
        ),
        out_shape=jax.ShapeDtypeStruct((2, parts, side, side), jnp.float32),
        input_output_aliases={len(arrays): 0} if alias else {},
        compiler_params=pltpu.CompilerParams(vmem_limit_bytes=VMEM_LIMIT),
        cost_estimate=pl.CostEstimate(
            flops=flops, bytes_accessed=flops // depth, transcendentals=0
        ),
        name="contract",
    )(*arrays, *([result] if alias else []))


def energy_gaps(valence_energy, conduction_energy, band_pairs):
    valence_hot = (
        band_pairs[:, 0][:, None] == jnp.arange(valence_energy.shape[0], dtype=jnp.int32)[None, :]
    )
    conduction_hot = (
        band_pairs[:, 1][:, None]
        == jnp.arange(conduction_energy.shape[0], dtype=jnp.int32)[None, :]
    )
    return jnp.sum(jnp.where(valence_hot, valence_energy[None, :], 0.0), axis=1) - jnp.sum(
        jnp.where(conduction_hot, conduction_energy[None, :], 0.0), axis=1
    )


def after(value, *others):
    return lax.optimization_barrier((value,) + others)[0]


def body(valence, conduction, valence_energy, conduction_energy, band_pairs, grid_index):
    rows, cols = lax.axis_size("row"), lax.axis_size("col")
    row, col = lax.axis_index("row"), lax.axis_index("col")
    pairs = band_pairs.shape[0]
    features = 2 * pairs
    width = rows * features
    block = grid_index.shape[0] // cols
    parts = cols // rows
    unit = block // EIGHTHS
    me = row.astype(jnp.int32).reshape(1)
    my_part = (col % parts).astype(jnp.int32).reshape(1)
    owner = col // parts

    order = list(range(0, cols, 2)) + list(range(1, cols, 2))[::-1]
    ring_up = [(order[q], order[(q + 1) % cols]) for q in range(cols)]
    ring_down = [(b, a) for a, b in ring_up]
    my_place = jnp.asarray(np.argsort(np.array(order)), jnp.int32)[col]
    half = cols // 2
    offsets = [0]
    for t in range(1, half):
        offsets += [-t, t]
    offsets.append(half)
    sources = jnp.asarray(np.array(order), jnp.int32)[
        (my_place + jnp.asarray(np.array(offsets), jnp.int32)) % cols
    ]

    gap = energy_gaps(valence_energy, conduction_energy, band_pairs)
    scale = jnp.sqrt(-2.0 / (math.sqrt(pairs * rows * cols) * gap))

    position = table_position(grid_index).reshape(rows, parts, EIGHTHS, unit)
    positions = [
        position[:, :, first : first + share].reshape(-1) for first, share in CHUNKS
    ]
    sent, table = transform(valence, conduction, band_pairs, scale, positions[0], me, rows)

    def across_rows(parcels):
        return [parcels[0]] + [
            lax.ppermute(parcels[s], "row", [(r, r ^ s) for r in range(rows)])
            for s in range(1, rows)
        ]

    def go_round(below, above):
        return [lax.ppermute(below, "col", ring_up), lax.ppermute(above, "col", ring_down)]

    def last_round(below, above):
        cut = below.shape[0] // 2
        return [jnp.concatenate(go_round(below[:cut], above[cut:]), axis=0)]

    def column(slots, before=(), behind=()):
        slots = [after(slots[0], *before)] + slots[1:] if before else slots
        copies = [flip(slots, my_part, parts, unit)]
        for relation in range(1, rows):
            source = relation & (relation - 1)
            hop = relation ^ source
            held = copies[source]
            if source and behind:
                held = after(held, *behind)
            perm = []
            for c in range(cols):
                for r in range(rows):
                    moves = hop == 1 or (r ^ c // parts) in (source, relation)
                    perm.append((r * cols + c, (r ^ hop if moves else r) * cols + c))
            copies.append(lax.ppermute(held, ("row", "col"), perm))
        return copies

    which = (row ^ owner).astype(jnp.int32).reshape(1)

    own = assemble(across_rows(sent), me, features)
    one = [[own], go_round(own, own)]
    sent = select(after(table, own), positions[1], me, rows, features)
    one[1] = [after(block, *sent) for block in one[1]]
    own = assemble(across_rows([after(part, *one[1]) for part in sent]), me, features)
    one.append(go_round(*one[1]))
    copies = [column(sum(one[:2], []), (own,))]
    one[2] = [after(block, own, copies[0][0]) for block in one[2]]
    for t in range(3, half):
        one.append(go_round(*one[t - 1]))
    copies.append(column(sum(one[2 : half - 1], [])))
    two = [[own], go_round(*[after(own, copies[1][0])] * 2)]
    below, above = one[half - 1]
    copies.append(column(one[half - 1]))
    one.append(last_round(below, above))
    rights = [settle(which, some, pairs) for some in copies[:2]]
    copies.append(column(one[half], rights))
    rights += [settle(which, some, pairs) for some in copies[2:]]
    two.append(go_round(*two[1]))

    def as_lefts(slots):
        return [slot.reshape(parts, -1, width) for slot in sum(slots, [])]

    lefts = as_lefts(one)
    wide = CHUNKS[0][1] // 2
    first = contract(None, [lefts], rights, unit, 0, wide, 0, 1, 0)
    for t in range(3, half):
        two.append(go_round(*two[t - 1]))
    copies = [column(sum(two[:2], []), two[2] + [first])]
    lefts = [after(lefts[0], copies[0][0], *two[half - 1])] + lefts[1:]
    second = contract(first, [lefts], rights, unit, 0, wide, 1, 1, 1)
    copies.append(column(sum(two[2:half], []), two[half - 1]))
    two.append(last_round(*[after(block, first) for block in two[half - 1]]))
    share = CHUNKS[0][1]
    both = [lefts, as_lefts(two)]
    result = contract(second, both[1:], rights, unit, share, share, 0, 1, 0)
    copies.append(column(two[half], (), (result,)))
    rights = [settle(which, some, pairs) for some in copies]
    result = contract(result, both, rights, unit, 0, share, 0, 1, 1)
    return result.reshape(2, parts * block, block)


def solution(mesh):
    return jax.shard_map(
        body,
        mesh=mesh,
        in_specs=(P(), P(), P(), P(), P(("row", "col"), None), P()),
        out_specs=P(None, "row", "col"),
        check_vma=False,
    )
```

```python
import math

import jax
import jax.numpy as jnp
import ml_dtypes
import numpy as np
from jax import lax
from jax.experimental import pallas as pl
from jax.experimental.pallas import tpu as pltpu
from jax.sharding import PartitionSpec as P

N1 = 32
N2 = 32
N3 = 32
NR = N1 * N2 * N3
LANES = 128
HI = N2 * N3 // LANES
LO = N2 // HI
ROWS = N1 * HI
VMEM_LIMIT = 58 * 1024 * 1024
CHUNKS = ((0, 4), (4, 4))
EIGHTHS = 8
GROUP = 4


def split_bf16(values):
    high = values.astype(ml_dtypes.bfloat16)
    low = (values - high.astype(np.float64)).astype(ml_dtypes.bfloat16)
    return high, low


def dft_tables():
    row = np.arange(ROWS)
    left = np.exp(
        -2j
        * np.pi
        * (
            (row[:, None] // HI) * (row[None, :] // HI) / N1
            + (row[:, None] % HI) * (row[None, :] % HI) / HI
        )
    )
    lane = np.arange(LANES)
    right = np.exp(
        -2j
        * np.pi
        * (
            (lane[:, None] // N3) * (lane[None, :] // N3) / LO
            + (lane[:, None] % N3) * (lane[None, :] % N3) / N3
        )
    )
    twiddle = np.exp(-2j * np.pi * (row[:, None] % HI) * (lane[None, :] // N3) / N2)
    twiddle = twiddle / math.sqrt(NR)
    left_full = np.block([[left.real, -left.imag], [left.imag, left.real]])
    right_full = np.block([[right.real, right.imag], [-right.imag, right.real]])
    left_high, left_low = split_bf16(left_full)
    right_high, right_low = split_bf16(right_full)
    twiddle = np.concatenate([twiddle] * GROUP, axis=1)
    return (
        np.concatenate([left_high, left_low, left_high], axis=1),
        np.concatenate([right_high, right_low], axis=1),
        np.stack([twiddle.real, twiddle.imag]).astype(np.float32),
    )


def table_position(grid_index):
    first = grid_index // (N2 * N3)
    second = grid_index // N3 % N2
    third = grid_index % N3
    return (first * HI + second % HI) * LANES + second // HI * N3 + third


def halves(value):
    high = value.astype(jnp.bfloat16)
    low = (value - high.astype(jnp.float32)).astype(jnp.bfloat16)
    return high, low


def dot(a, b):
    return jnp.dot(a, b, preferred_element_type=jnp.float32)


def select_rows(count, row_count, features, position_ref, me_ref, table, rows, outs):
    pack = LANES // features
    part = count // pack
    unroll = 32
    lane = lax.broadcasted_iota(jnp.int32, (part, LANES), 1)
    for s in range(row_count):
        base = (me_ref[0] ^ s) * count

        def some_rows(step, carry):
            first = step * unroll
            for j in range(unroll):
                index = position_ref[base + first + j]
                rows[pl.ds(first + j, 1), :] = table[pl.ds(index, 1), :]
            return carry

        lax.fori_loop(0, count // unroll, some_rows, 0)
        packed = rows[0:part, :]
        for k in range(1, pack):
            packed = jnp.where(lane >= k * features, rows[k * part : (k + 1) * part, :], packed)
        outs[s][...] = packed.astype(jnp.bfloat16)


def select_kernel(row_count, features, count, position_ref, me_ref, table_ref, *rest):
    select_rows(
        count, row_count, features, position_ref, me_ref, table_ref, rest[-1], rest[:row_count]
    )


def select(table, position, me, row_count, features):
    count = position.shape[0] // row_count
    shape = (count * features // LANES, LANES)
    return pl.pallas_call(
        lambda *refs: select_kernel(row_count, features, count, *refs),
        grid_spec=pltpu.PrefetchScalarGridSpec(
            num_scalar_prefetch=2,
            grid=(),
            in_specs=[pl.BlockSpec(memory_space=pltpu.VMEM)],
            out_specs=[pl.BlockSpec(memory_space=pltpu.VMEM)] * row_count,
            scratch_shapes=[pltpu.VMEM((count, LANES), jnp.float32)],
        ),
        out_shape=[jax.ShapeDtypeStruct(shape, jnp.bfloat16)] * row_count,
        compiler_params=pltpu.CompilerParams(vmem_limit_bytes=VMEM_LIMIT),
        cost_estimate=pl.CostEstimate(flops=0, bytes_accessed=50_000_000, transcendentals=0),
        name="select",
    )(position, me, table)


def transform_kernel(pairs, load_steps, step_rows, count, row_count, *refs):
    position_ref, me_ref, hot_c_ref, hot_v_ref, scale_ref, cond_ref, val_ref = refs[:7]
    left_ref, right_ref, twiddle_ref = refs[7:10]
    outs = refs[10 : 10 + row_count]
    table_ref, rho_r, rho_i, spec, table, middle, rows, sem = refs[10 + row_count :]
    step = pl.program_id(0)
    features = 2 * pairs

    cond = dot(hot_c_ref[...], cond_ref[...])
    val = dot(hot_v_ref[...], val_ref[...]) * scale_ref[...]
    cr, ci = cond[:pairs], cond[pairs:]
    vr, vi = val[:pairs], val[pairs:]
    real = vr * cr + vi * ci
    imag = vr * ci - vi * cr
    for a in range(step_rows):
        row = pl.multiple_of((step * step_rows + a) * pairs, pairs)
        rho_r[pl.ds(row, pairs), :] = real[:, a * LANES : (a + 1) * LANES]
        rho_i[pl.ds(row, pairs), :] = imag[:, a * LANES : (a + 1) * LANES]

    def left_half(group, slot):
        members = [GROUP * group + k for k in range(GROUP)]
        data = jnp.concatenate(
            [
                jnp.concatenate([ref[pl.ds(p, ROWS, stride=pairs), :] for p in members], axis=1)
                for ref in (rho_r, rho_i)
            ],
            axis=0,
        )
        high, low = halves(data)
        mixed = dot(left_ref[...], jnp.concatenate([high, high, low], axis=0))
        mid_r, mid_i = mixed[:ROWS], mixed[ROWS:]
        tr, ti = twiddle_ref[0], twiddle_ref[1]
        turn_r = mid_r * tr - mid_i * ti
        turn_i = mid_r * ti + mid_i * tr
        for k in range(GROUP):
            lanes = slice(k * LANES, (k + 1) * LANES)
            rows_k = slice(k * ROWS, (k + 1) * ROWS)
            for z, turned in enumerate((turn_r, turn_i)):
                high, low = halves(turned[:, lanes])
                middle[slot, rows_k, z * LANES : (z + 1) * LANES] = high
                middle[slot, rows_k, (2 + z) * LANES : (3 + z) * LANES] = low

    def right_half(group, slot):
        high = middle[slot, :, : 2 * LANES]
        low = middle[slot, :, 2 * LANES :]
        by_high = dot(high, right_ref[...])
        by_low = dot(low, right_ref[:, : 2 * LANES])
        out = by_high[:, : 2 * LANES] + (by_high[:, 2 * LANES :] + by_low)
        for k in range(GROUP):
            p = GROUP * group + k
            part = out[k * ROWS : (k + 1) * ROWS]
            spec[pl.ds(p, ROWS, stride=features), :] = part[:, :LANES]
            spec[pl.ds(pairs + p, ROWS, stride=features), :] = part[:, LANES:]

    @pl.when(step == load_steps - 1)
    def _():
        groups = pairs // GROUP
        left_half(0, 0)

        def two_groups(k, carry):
            right_half(2 * k, 0)
            left_half(2 * k + 1, 1)
            right_half(2 * k + 1, 1)
            left_half(jnp.minimum(2 * k + 2, groups - 1), 0)
            return carry

        lax.fori_loop(0, groups // 2, two_groups, 0)

        def one_row(k, carry):
            start = pl.multiple_of(k * features, features)
            tile = spec[pl.ds(start, features), :].astype(jnp.bfloat16)
            tile = jnp.concatenate([tile] * (LANES // features), axis=0)
            table[pl.ds(pl.multiple_of(k * LANES, LANES), LANES), :] = tile.T.astype(jnp.float32)
            return carry

        lax.fori_loop(0, ROWS, one_row, 0, unroll=8)
        keep = pltpu.make_async_copy(table, table_ref, sem)
        keep.start()
        select_rows(count, row_count, features, position_ref, me_ref, table, rows, outs)
        keep.wait()


def transform(valence, conduction, band_pairs, scale, position, me, row_count):
    count = position.shape[0] // row_count
    pairs = band_pairs.shape[0]
    features = 2 * pairs
    pack = LANES // features
    nvb, ncb = valence.shape[1], conduction.shape[1]
    load_steps = 8
    step_rows = ROWS // load_steps
    chunk = step_rows * LANES

    def hot(band, count):
        one = (band[:, None] == jnp.arange(count, dtype=jnp.int32)[None, :]).astype(jnp.bfloat16)
        none = jnp.zeros_like(one)
        return jnp.concatenate(
            [jnp.concatenate([one, none], axis=1), jnp.concatenate([none, one], axis=1)], axis=0
        )

    left, right, twiddle = dft_tables()
    whole = lambda shape: pl.BlockSpec(shape, lambda i, *_: (0,) * len(shape))
    loaded = lambda i, *_: (0, i)
    flops = 2 * pairs * (6 * ROWS * ROWS * 2 * LANES + 3 * ROWS * 4 * LANES * LANES)
    out_shapes = [(count // pack, LANES)] * row_count
    outs = pl.pallas_call(
        lambda *refs: transform_kernel(pairs, load_steps, step_rows, count, row_count, *refs),
        grid_spec=pltpu.PrefetchScalarGridSpec(
            num_scalar_prefetch=2,
            grid=(load_steps,),
            in_specs=[
                whole((2 * pairs, 2 * ncb)),
                whole((2 * pairs, 2 * nvb)),
                whole((2 * pairs, 1)),
                pl.BlockSpec((2 * ncb, chunk), loaded),
                pl.BlockSpec((2 * nvb, chunk), loaded),
                whole(left.shape),
                whole(right.shape),
                whole(twiddle.shape),
            ],
            out_specs=[whole(shape) for shape in out_shapes] + [pl.BlockSpec(memory_space=pl.ANY)],
            scratch_shapes=[
                pltpu.VMEM((ROWS * pairs, LANES), jnp.float32),
                pltpu.VMEM((ROWS * pairs, LANES), jnp.float32),
                pltpu.VMEM((ROWS * features, LANES), jnp.float32),
                pltpu.VMEM((NR, LANES), jnp.float32),
                pltpu.VMEM((2, GROUP * ROWS, 4 * LANES), jnp.bfloat16),
                pltpu.VMEM((count, LANES), jnp.float32),
                pltpu.SemaphoreType.DMA,
            ],
        ),
        out_shape=[jax.ShapeDtypeStruct(shape, jnp.bfloat16) for shape in out_shapes]
        + [jax.ShapeDtypeStruct((NR, LANES), jnp.float32)],
        compiler_params=pltpu.CompilerParams(vmem_limit_bytes=VMEM_LIMIT),
        cost_estimate=pl.CostEstimate(flops=flops, bytes_accessed=40_000_000, transcendentals=0),
        name="transform",
    )(
        position,
        me,
        hot(band_pairs[:, 1], ncb),
        hot(band_pairs[:, 0], nvb),
        jnp.concatenate([scale, scale])[:, None],
        conduction.reshape(2 * ncb, NR),
        valence.reshape(2 * nvb, NR),
        jnp.asarray(left),
        jnp.asarray(right),
        jnp.asarray(twiddle),
    )
    return outs[:row_count], outs[row_count]


def assemble_kernel(row_count, features, me_ref, *rest):
    parts, out_ref, held = rest[:row_count], rest[row_count], rest[row_count + 1]
    pack = LANES // features
    part = parts[0].shape[0]
    lane = lax.broadcasted_iota(jnp.int32, (part, LANES), 1)
    for s in range(row_count):
        held[s] = parts[s][...].astype(jnp.float32)
    for b in range(row_count // pack):
        for k in range(pack):
            block = None
            for q in range(pack):
                piece = held[(b * pack + q) ^ me_ref[0]]
                if q != k:
                    piece = pltpu.roll(piece, (q - k) * features % LANES, 1)
                block = piece if block is None else jnp.where(lane >= q * features, piece, block)
            out_ref[k * part : (k + 1) * part, b * LANES : (b + 1) * LANES] = block.astype(
                jnp.bfloat16
            )


def assemble(parts, me, features):
    row_count = len(parts)
    pack = LANES // features
    part = parts[0].shape[0]
    return pl.pallas_call(
        lambda *refs: assemble_kernel(row_count, features, *refs),
        grid_spec=pltpu.PrefetchScalarGridSpec(
            num_scalar_prefetch=1,
            grid=(),
            in_specs=[pl.BlockSpec(memory_space=pltpu.VMEM)] * row_count,
            out_specs=pl.BlockSpec(memory_space=pltpu.VMEM),
            scratch_shapes=[pltpu.VMEM((row_count, part, LANES), jnp.float32)],
        ),
        out_shape=jax.ShapeDtypeStruct((part * pack, row_count * features), jnp.bfloat16),
        compiler_params=pltpu.CompilerParams(vmem_limit_bytes=VMEM_LIMIT),
        cost_estimate=pl.CostEstimate(flops=0, bytes_accessed=2_000_000, transcendentals=0),
        name="assemble",
    )(me, *parts)


def flip_kernel(slot_count, part_ref, *refs):
    out_ref = refs[slot_count]
    for s in range(slot_count):
        width = refs[s].shape[1]
        out_ref[s * width : (s + 1) * width, :] = refs[s][...].T


def flip(slots, part, parts, unit):
    slot_count = len(slots)
    width = slots[0].shape[1]
    depth = slots[0].shape[0] // parts
    steps = depth // unit
    return pl.pallas_call(
        lambda *refs: flip_kernel(slot_count, *refs),
        grid_spec=pltpu.PrefetchScalarGridSpec(
            num_scalar_prefetch=1,
            grid=(steps,),
            in_specs=[
                pl.BlockSpec((unit, width), lambda t, part_ref: (part_ref[0] * steps + t, 0))
            ]
            * slot_count,
            out_specs=pl.BlockSpec((slot_count * width, unit), lambda t, part_ref: (0, t)),
        ),
        out_shape=jax.ShapeDtypeStruct((slot_count * width, depth), jnp.bfloat16),
        compiler_params=pltpu.CompilerParams(vmem_limit_bytes=VMEM_LIMIT),
        cost_estimate=pl.CostEstimate(
            flops=0, bytes_accessed=8 * slot_count * width * depth, transcendentals=0
        ),
        name="flip",
    )(part, *slots)


def settle_kernel(pairs, row_count, which_ref, *refs):
    out_ref = refs[row_count]
    kind = jnp.float32 if pairs % 16 else jnp.bfloat16
    for k in range(row_count):

        @pl.when(which_ref[0] == k)
        def _():
            values = -refs[k][...].astype(kind)
            rows, across = values.shape
            out_ref[0] = values.astype(jnp.bfloat16)
            values = values.reshape(rows // (2 * pairs), 2, pairs, across)
            turned = jnp.stack([values[:, 1], -values[:, 0]], axis=1)
            out_ref[1] = turned.reshape(rows, across).astype(jnp.bfloat16)


def settle(which, copies, pairs):
    rows, across = copies[0].shape
    tile = math.gcd(rows, 256)
    row_count = len(copies)

    def pick(k):
        return lambda t, which_ref: (jnp.where(which_ref[0] == k, t, 0), 0)

    return pl.pallas_call(
        lambda *refs: settle_kernel(pairs, row_count, *refs),
        grid_spec=pltpu.PrefetchScalarGridSpec(
            num_scalar_prefetch=1,
            grid=(rows // tile,),
            in_specs=[pl.BlockSpec((tile, across), pick(k)) for k in range(row_count)],
            out_specs=pl.BlockSpec((2, tile, across), lambda t, _: (0, t, 0)),
        ),
        out_shape=jax.ShapeDtypeStruct((2, rows, across), jnp.bfloat16),
        compiler_params=pltpu.CompilerParams(vmem_limit_bytes=VMEM_LIMIT),
        cost_estimate=pl.CostEstimate(
            flops=0, bytes_accessed=8 * rows * across, transcendentals=0
        ),
        name="settle",
    )(which, *copies)


def contract_kernel(slot_count, shares, right_count, *refs):
    rights = refs[len(shares) * slot_count : len(shares) * slot_count + right_count]
    out_ref = refs[-1]
    row = pl.program_id(1)
    for k, share in enumerate(shares):
        start = sum(shares[:k])

        @pl.when((row >= start) & (row < start + share))
        def _():
            slots = refs[k * slot_count : (k + 1) * slot_count]
            parts, depth, width = slots[0].shape
            left = jnp.concatenate(
                [slot[...].reshape(parts * depth, width) for slot in slots], axis=1
            )
            for z in range(2):
                right = jnp.concatenate([ref[z] for ref in rights], axis=0)
                out_ref[z] = dot(left, right).reshape(out_ref.shape[1:])


def contract(result, lefts, rights, unit, row_first, wide, tile_first, steps, out_first):
    parts, _, width = lefts[0][0].shape
    slot_count = len(lefts[0])
    shares = [chunk[0].shape[1] // unit for chunk in lefts]
    depth = slot_count * width
    columns, side = wide * unit, EIGHTHS * unit
    alias = 0 if result is None else 1
    flops = 8 * parts * sum(shares) * unit * steps * columns * depth

    def place(start, share):
        return lambda c, r: (0, jnp.clip(r - start, 0, share - 1), 0)

    in_specs = [
        pl.BlockSpec((parts, unit, width), place(sum(shares[:k]), share))
        for k, share in enumerate(shares)
        for _ in range(slot_count)
    ]
    in_specs += [
        pl.BlockSpec((2, right.shape[1], columns), lambda c, r: (0, 0, tile_first + c))
        for right in rights
    ]
    if alias:
        in_specs.append(pl.BlockSpec(memory_space=pl.ANY))
    arrays = [slot for chunk in lefts for slot in chunk] + list(rights)
    return pl.pallas_call(
        lambda *refs: contract_kernel(slot_count, shares, len(rights), *refs),
        grid=(steps, sum(shares)),
        in_specs=in_specs,
        out_specs=pl.BlockSpec(
            (2, parts, unit, columns), lambda c, r: (0, 0, row_first + r, out_first + c)
        ),
        out_shape=jax.ShapeDtypeStruct((2, parts, side, side), jnp.float32),
        input_output_aliases={len(arrays): 0} if alias else {},
        compiler_params=pltpu.CompilerParams(vmem_limit_bytes=VMEM_LIMIT),
        cost_estimate=pl.CostEstimate(
            flops=flops, bytes_accessed=flops // depth, transcendentals=0
        ),
        name="contract",
    )(*arrays, *([result] if alias else []))


def energy_gaps(valence_energy, conduction_energy, band_pairs):
    valence_hot = (
        band_pairs[:, 0][:, None] == jnp.arange(valence_energy.shape[0], dtype=jnp.int32)[None, :]
    )
    conduction_hot = (
        band_pairs[:, 1][:, None]
        == jnp.arange(conduction_energy.shape[0], dtype=jnp.int32)[None, :]
    )
    return jnp.sum(jnp.where(valence_hot, valence_energy[None, :], 0.0), axis=1) - jnp.sum(
        jnp.where(conduction_hot, conduction_energy[None, :], 0.0), axis=1
    )


def after(value, *others):
    return lax.optimization_barrier((value,) + others)[0]


def body(valence, conduction, valence_energy, conduction_energy, band_pairs, grid_index):
    rows, cols = lax.axis_size("row"), lax.axis_size("col")
    row, col = lax.axis_index("row"), lax.axis_index("col")
    pairs = band_pairs.shape[0]
    features = 2 * pairs
    width = rows * features
    block = grid_index.shape[0] // cols
    parts = cols // rows
    unit = block // EIGHTHS
    me = row.astype(jnp.int32).reshape(1)
    my_part = (col % parts).astype(jnp.int32).reshape(1)
    owner = col // parts

    order = list(range(0, cols, 2)) + list(range(1, cols, 2))[::-1]
    ring_up = [(order[q], order[(q + 1) % cols]) for q in range(cols)]
    ring_down = [(b, a) for a, b in ring_up]
    my_place = jnp.asarray(np.argsort(np.array(order)), jnp.int32)[col]
    half = cols // 2
    offsets = [0]
    for t in range(1, half):
        offsets += [-t, t]
    offsets.append(half)
    sources = jnp.asarray(np.array(order), jnp.int32)[
        (my_place + jnp.asarray(np.array(offsets), jnp.int32)) % cols
    ]

    gap = energy_gaps(valence_energy, conduction_energy, band_pairs)
    scale = jnp.sqrt(-2.0 / (math.sqrt(pairs * rows * cols) * gap))

    position = table_position(grid_index).reshape(rows, parts, EIGHTHS, unit)
    positions = [
        position[:, :, first : first + share].reshape(-1) for first, share in CHUNKS
    ]
    sent, table = transform(valence, conduction, band_pairs, scale, positions[0], me, rows)

    def across_rows(parcels):
        return [parcels[0]] + [
            lax.ppermute(parcels[s], "row", [(r, r ^ s) for r in range(rows)])
            for s in range(1, rows)
        ]

    def go_round(below, above):
        return [lax.ppermute(below, "col", ring_up), lax.ppermute(above, "col", ring_down)]

    def last_round(below, above):
        cut = below.shape[0] // 2
        return [jnp.concatenate(go_round(below[:cut], above[cut:]), axis=0)]

    def column(slots, before=(), behind=(), flipped=None):
        slots = [after(slots[0], *before)] + slots[1:] if before else slots
        copies = [flip(slots, my_part, parts, unit) if flipped is None else flipped]
        for relation in range(1, rows):
            source = relation & (relation - 1)
            hop = relation ^ source
            held = copies[source]
            if source and behind:
                held = after(held, *behind)
            if hop == 1:
                copies.append(lax.ppermute(held, "row", [(r, r ^ 1) for r in range(rows)]))
                continue
            perm = [
                ((c // parts ^ source) * cols + c, (c // parts ^ relation) * cols + c)
                for c in range(cols)
            ]
            copies.append(lax.ppermute(held, ("row", "col"), perm))
        return copies

    which = (row ^ owner).astype(jnp.int32).reshape(1)

    own = assemble(across_rows(sent), me, features)
    one = [[own], go_round(own, own)]
    sent = select(after(table, own), positions[1], me, rows, features)
    one[1] = [after(block, *sent) for block in one[1]]
    own = assemble(across_rows([after(part, *one[1]) for part in sent]), me, features)
    one.append(go_round(*one[1]))
    one[2] = [after(block, own) for block in one[2]]
    for t in range(3, half):
        one.append(go_round(*one[t - 1]))
    copies = [column(sum(one[:2], []), one[half - 1])]
    copies.append(column(sum(one[2 : half - 1], []), one[half - 1]))
    two = [[own], go_round(*[after(own, *one[half - 2])] * 2)]
    below, above = one[half - 1]
    copies.append(column(one[half - 1]))
    one.append(last_round(below, above))
    rights = [settle(which, some, pairs) for some in copies[:2]]
    copies.append(column(one[half], rights))
    rights += [settle(which, some, pairs) for some in copies[2:]]
    two.append(go_round(*two[1]))

    def as_lefts(slots):
        return [slot.reshape(parts, -1, width) for slot in sum(slots, [])]

    lefts = as_lefts(one)
    wide = CHUNKS[0][1] // 2
    copies = [column(sum(two[:2], []), two[2])]
    lefts = [after(lefts[0], copies[0][0])] + lefts[1:]
    first = contract(None, [lefts], rights, unit, 0, wide, 0, 1, 0)
    for t in range(3, half):
        two.append(go_round(*two[t - 1]))
    second = contract(first, [lefts], rights, unit, 0, wide, 1, 1, 1)
    two.append(last_round(*[after(block, first) for block in two[half - 1]]))
    share = CHUNKS[0][1]
    flipped = flip(two[half], my_part, parts, unit)
    both = [lefts, as_lefts(two)]
    both[1][0] = after(both[1][0], flipped)
    result = contract(second, both[1:], rights, unit, share, share, 0, 1, 0)
    copies.append(column(sum(two[2:half], []), two[half - 1] + [first], (result,)))
    copies.append(column(two[half], (), (result,), flipped))
    rights = [settle(which, some, pairs) for some in copies]
    result = contract(result, both, rights, unit, 0, share, 0, 1, 1)
    return result.reshape(2, parts * block, block)


def solution(mesh):
    return jax.shard_map(
        body,
        mesh=mesh,
        in_specs=(P(), P(), P(), P(), P(("row", "col"), None), P()),
        out_specs=P(None, "row", "col"),
        check_vma=False,
    )
```

```python
import math

import jax
import jax.numpy as jnp
import ml_dtypes
import numpy as np
from jax import lax
from jax.experimental import pallas as pl
from jax.experimental.pallas import tpu as pltpu
from jax.sharding import PartitionSpec as P

N1 = 32
N2 = 32
N3 = 32
NR = N1 * N2 * N3
LANES = 128
HI = N2 * N3 // LANES
LO = N2 // HI
ROWS = N1 * HI
VMEM_LIMIT = 58 * 1024 * 1024
CHUNKS = ((0, 4), (4, 4))
EIGHTHS = 8
GROUP = 4


def split_bf16(values):
    high = values.astype(ml_dtypes.bfloat16)
    low = (values - high.astype(np.float64)).astype(ml_dtypes.bfloat16)
    return high, low


def dft_tables():
    row = np.arange(ROWS)
    left = np.exp(
        -2j
        * np.pi
        * (
            (row[:, None] // HI) * (row[None, :] // HI) / N1
            + (row[:, None] % HI) * (row[None, :] % HI) / HI
        )
    )
    lane = np.arange(LANES)
    right = np.exp(
        -2j
        * np.pi
        * (
            (lane[:, None] // N3) * (lane[None, :] // N3) / LO
            + (lane[:, None] % N3) * (lane[None, :] % N3) / N3
        )
    )
    twiddle = np.exp(-2j * np.pi * (row[:, None] % HI) * (lane[None, :] // N3) / N2)
    twiddle = twiddle / math.sqrt(NR)
    left_full = np.block([[left.real, -left.imag], [left.imag, left.real]])
    right_full = np.block([[right.real, right.imag], [-right.imag, right.real]])
    left_high, left_low = split_bf16(left_full)
    right_high, right_low = split_bf16(right_full)
    twiddle = np.concatenate([twiddle] * GROUP, axis=1)
    return (
        np.concatenate([left_high, left_low, left_high], axis=1),
        np.concatenate([right_high, right_low], axis=1),
        np.stack([twiddle.real, twiddle.imag]).astype(np.float32),
    )


def table_position(grid_index):
    first = grid_index // (N2 * N3)
    second = grid_index // N3 % N2
    third = grid_index % N3
    return (first * HI + second % HI) * LANES + second // HI * N3 + third


def halves(value):
    high = value.astype(jnp.bfloat16)
    low = (value - high.astype(jnp.float32)).astype(jnp.bfloat16)
    return high, low


def dot(a, b):
    return jnp.dot(a, b, preferred_element_type=jnp.float32)


def select_rows(count, row_count, features, position_ref, me_ref, table, rows, outs):
    pack = LANES // features
    part = count // pack
    unroll = 32
    lane = lax.broadcasted_iota(jnp.int32, (part, LANES), 1)
    for s in range(row_count):
        base = (me_ref[0] ^ s) * count

        def some_rows(step, carry):
            first = step * unroll
            for j in range(unroll):
                index = position_ref[base + first + j]
                rows[pl.ds(first + j, 1), :] = table[pl.ds(index, 1), :]
            return carry

        lax.fori_loop(0, count // unroll, some_rows, 0)
        packed = rows[0:part, :]
        for k in range(1, pack):
            packed = jnp.where(lane >= k * features, rows[k * part : (k + 1) * part, :], packed)
        outs[s][...] = packed.astype(jnp.bfloat16)


def select_kernel(row_count, features, count, position_ref, me_ref, table_ref, *rest):
    select_rows(
        count, row_count, features, position_ref, me_ref, table_ref, rest[-1], rest[:row_count]
    )


def select(table, position, me, row_count, features):
    count = position.shape[0] // row_count
    shape = (count * features // LANES, LANES)
    return pl.pallas_call(
        lambda *refs: select_kernel(row_count, features, count, *refs),
        grid_spec=pltpu.PrefetchScalarGridSpec(
            num_scalar_prefetch=2,
            grid=(),
            in_specs=[pl.BlockSpec(memory_space=pltpu.VMEM)],
            out_specs=[pl.BlockSpec(memory_space=pltpu.VMEM)] * row_count,
            scratch_shapes=[pltpu.VMEM((count, LANES), jnp.float32)],
        ),
        out_shape=[jax.ShapeDtypeStruct(shape, jnp.bfloat16)] * row_count,
        compiler_params=pltpu.CompilerParams(vmem_limit_bytes=VMEM_LIMIT),
        cost_estimate=pl.CostEstimate(flops=0, bytes_accessed=50_000_000, transcendentals=0),
        name="select",
    )(position, me, table)


def transform_kernel(pairs, load_steps, step_rows, count, row_count, *refs):
    position_ref, me_ref, hot_c_ref, hot_v_ref, scale_ref, cond_ref, val_ref = refs[:7]
    left_ref, right_ref, twiddle_ref = refs[7:10]
    outs = refs[10 : 10 + row_count]
    table_ref, rho_r, rho_i, spec, table, middle, rows, sem = refs[10 + row_count :]
    step = pl.program_id(0)
    features = 2 * pairs

    cond = dot(hot_c_ref[...], cond_ref[...])
    val = dot(hot_v_ref[...], val_ref[...]) * scale_ref[...]
    cr, ci = cond[:pairs], cond[pairs:]
    vr, vi = val[:pairs], val[pairs:]
    real = vr * cr + vi * ci
    imag = vr * ci - vi * cr
    for a in range(step_rows):
        row = pl.multiple_of((step * step_rows + a) * pairs, pairs)
        rho_r[pl.ds(row, pairs), :] = real[:, a * LANES : (a + 1) * LANES]
        rho_i[pl.ds(row, pairs), :] = imag[:, a * LANES : (a + 1) * LANES]

    def left_half(group, slot):
        members = [GROUP * group + k for k in range(GROUP)]
        data = jnp.concatenate(
            [
                jnp.concatenate([ref[pl.ds(p, ROWS, stride=pairs), :] for p in members], axis=1)
                for ref in (rho_r, rho_i)
            ],
            axis=0,
        )
        high, low = halves(data)
        mixed = dot(left_ref[...], jnp.concatenate([high, high, low], axis=0))
        mid_r, mid_i = mixed[:ROWS], mixed[ROWS:]
        tr, ti = twiddle_ref[0], twiddle_ref[1]
        turn_r = mid_r * tr - mid_i * ti
        turn_i = mid_r * ti + mid_i * tr
        for k in range(GROUP):
            lanes = slice(k * LANES, (k + 1) * LANES)
            rows_k = slice(k * ROWS, (k + 1) * ROWS)
            for z, turned in enumerate((turn_r, turn_i)):
                high, low = halves(turned[:, lanes])
                middle[slot, rows_k, z * LANES : (z + 1) * LANES] = high
                middle[slot, rows_k, (2 + z) * LANES : (3 + z) * LANES] = low

    def right_half(group, slot):
        high = middle[slot, :, : 2 * LANES]
        low = middle[slot, :, 2 * LANES :]
        by_high = dot(high, right_ref[...])
        by_low = dot(low, right_ref[:, : 2 * LANES])
        out = by_high[:, : 2 * LANES] + (by_high[:, 2 * LANES :] + by_low)
        for k in range(GROUP):
            p = GROUP * group + k
            part = out[k * ROWS : (k + 1) * ROWS]
            spec[pl.ds(p, ROWS, stride=features), :] = part[:, :LANES]
            spec[pl.ds(pairs + p, ROWS, stride=features), :] = part[:, LANES:]

    @pl.when(step == load_steps - 1)
    def _():
        groups = pairs // GROUP
        left_half(0, 0)

        def two_groups(k, carry):
            right_half(2 * k, 0)
            left_half(2 * k + 1, 1)
            right_half(2 * k + 1, 1)
            left_half(jnp.minimum(2 * k + 2, groups - 1), 0)
            return carry

        lax.fori_loop(0, groups // 2, two_groups, 0)

        def one_row(k, carry):
            start = pl.multiple_of(k * features, features)
            tile = spec[pl.ds(start, features), :].astype(jnp.bfloat16)
            tile = jnp.concatenate([tile] * (LANES // features), axis=0)
            table[pl.ds(pl.multiple_of(k * LANES, LANES), LANES), :] = tile.T.astype(jnp.float32)
            return carry

        lax.fori_loop(0, ROWS, one_row, 0, unroll=8)
        keep = pltpu.make_async_copy(table, table_ref, sem)
        keep.start()
        select_rows(count, row_count, features, position_ref, me_ref, table, rows, outs)
        keep.wait()


def transform(valence, conduction, band_pairs, scale, position, me, row_count):
    count = position.shape[0] // row_count
    pairs = band_pairs.shape[0]
    features = 2 * pairs
    pack = LANES // features
    nvb, ncb = valence.shape[1], conduction.shape[1]
    load_steps = 8
    step_rows = ROWS // load_steps
    chunk = step_rows * LANES

    def hot(band, count):
        one = (band[:, None] == jnp.arange(count, dtype=jnp.int32)[None, :]).astype(jnp.bfloat16)
        none = jnp.zeros_like(one)
        return jnp.concatenate(
            [jnp.concatenate([one, none], axis=1), jnp.concatenate([none, one], axis=1)], axis=0
        )

    left, right, twiddle = dft_tables()
    whole = lambda shape: pl.BlockSpec(shape, lambda i, *_: (0,) * len(shape))
    loaded = lambda i, *_: (0, i)
    flops = 2 * pairs * (6 * ROWS * ROWS * 2 * LANES + 3 * ROWS * 4 * LANES * LANES)
    out_shapes = [(count // pack, LANES)] * row_count
    outs = pl.pallas_call(
        lambda *refs: transform_kernel(pairs, load_steps, step_rows, count, row_count, *refs),
        grid_spec=pltpu.PrefetchScalarGridSpec(
            num_scalar_prefetch=2,
            grid=(load_steps,),
            in_specs=[
                whole((2 * pairs, 2 * ncb)),
                whole((2 * pairs, 2 * nvb)),
                whole((2 * pairs, 1)),
                pl.BlockSpec((2 * ncb, chunk), loaded),
                pl.BlockSpec((2 * nvb, chunk), loaded),
                whole(left.shape),
                whole(right.shape),
                whole(twiddle.shape),
            ],
            out_specs=[whole(shape) for shape in out_shapes] + [pl.BlockSpec(memory_space=pl.ANY)],
            scratch_shapes=[
                pltpu.VMEM((ROWS * pairs, LANES), jnp.float32),
                pltpu.VMEM((ROWS * pairs, LANES), jnp.float32),
                pltpu.VMEM((ROWS * features, LANES), jnp.float32),
                pltpu.VMEM((NR, LANES), jnp.float32),
                pltpu.VMEM((2, GROUP * ROWS, 4 * LANES), jnp.bfloat16),
                pltpu.VMEM((count, LANES), jnp.float32),
                pltpu.SemaphoreType.DMA,
            ],
        ),
        out_shape=[jax.ShapeDtypeStruct(shape, jnp.bfloat16) for shape in out_shapes]
        + [jax.ShapeDtypeStruct((NR, LANES), jnp.float32)],
        compiler_params=pltpu.CompilerParams(vmem_limit_bytes=VMEM_LIMIT),
        cost_estimate=pl.CostEstimate(flops=flops, bytes_accessed=40_000_000, transcendentals=0),
        name="transform",
    )(
        position,
        me,
        hot(band_pairs[:, 1], ncb),
        hot(band_pairs[:, 0], nvb),
        jnp.concatenate([scale, scale])[:, None],
        conduction.reshape(2 * ncb, NR),
        valence.reshape(2 * nvb, NR),
        jnp.asarray(left),
        jnp.asarray(right),
        jnp.asarray(twiddle),
    )
    return outs[:row_count], outs[row_count]


def assemble_kernel(row_count, features, me_ref, *rest):
    parts, out_ref, held = rest[:row_count], rest[row_count], rest[row_count + 1]
    pack = LANES // features
    part = parts[0].shape[0]
    lane = lax.broadcasted_iota(jnp.int32, (part, LANES), 1)
    for s in range(row_count):
        held[s] = parts[s][...].astype(jnp.float32)
    for b in range(row_count // pack):
        for k in range(pack):
            block = None
            for q in range(pack):
                piece = held[(b * pack + q) ^ me_ref[0]]
                if q != k:
                    piece = pltpu.roll(piece, (q - k) * features % LANES, 1)
                block = piece if block is None else jnp.where(lane >= q * features, piece, block)
            out_ref[k * part : (k + 1) * part, b * LANES : (b + 1) * LANES] = block.astype(
                jnp.bfloat16
            )


def assemble(parts, me, features):
    row_count = len(parts)
    pack = LANES // features
    part = parts[0].shape[0]
    return pl.pallas_call(
        lambda *refs: assemble_kernel(row_count, features, *refs),
        grid_spec=pltpu.PrefetchScalarGridSpec(
            num_scalar_prefetch=1,
            grid=(),
            in_specs=[pl.BlockSpec(memory_space=pltpu.VMEM)] * row_count,
            out_specs=pl.BlockSpec(memory_space=pltpu.VMEM),
            scratch_shapes=[pltpu.VMEM((row_count, part, LANES), jnp.float32)],
        ),
        out_shape=jax.ShapeDtypeStruct((part * pack, row_count * features), jnp.bfloat16),
        compiler_params=pltpu.CompilerParams(vmem_limit_bytes=VMEM_LIMIT),
        cost_estimate=pl.CostEstimate(flops=0, bytes_accessed=2_000_000, transcendentals=0),
        name="assemble",
    )(me, *parts)


def flip_kernel(slot_count, part_ref, *refs):
    out_ref = refs[slot_count]
    for s in range(slot_count):
        width = refs[s].shape[1]
        out_ref[s * width : (s + 1) * width, :] = refs[s][...].T


def flip(slots, part, parts, unit):
    slot_count = len(slots)
    width = slots[0].shape[1]
    depth = slots[0].shape[0] // parts
    steps = depth // unit
    return pl.pallas_call(
        lambda *refs: flip_kernel(slot_count, *refs),
        grid_spec=pltpu.PrefetchScalarGridSpec(
            num_scalar_prefetch=1,
            grid=(steps,),
            in_specs=[
                pl.BlockSpec((unit, width), lambda t, part_ref: (part_ref[0] * steps + t, 0))
            ]
            * slot_count,
            out_specs=pl.BlockSpec((slot_count * width, unit), lambda t, part_ref: (0, t)),
        ),
        out_shape=jax.ShapeDtypeStruct((slot_count * width, depth), jnp.bfloat16),
        compiler_params=pltpu.CompilerParams(vmem_limit_bytes=VMEM_LIMIT),
        cost_estimate=pl.CostEstimate(
            flops=0, bytes_accessed=8 * slot_count * width * depth, transcendentals=0
        ),
        name="flip",
    )(part, *slots)


def settle_kernel(pairs, row_count, which_ref, *refs):
    out_ref = refs[row_count]
    kind = jnp.float32 if pairs % 16 else jnp.bfloat16
    for k in range(row_count):

        @pl.when(which_ref[0] == k)
        def _():
            values = -refs[k][...].astype(kind)
            rows, across = values.shape
            out_ref[0] = values.astype(jnp.bfloat16)
            values = values.reshape(rows // (2 * pairs), 2, pairs, across)
            turned = jnp.stack([values[:, 1], -values[:, 0]], axis=1)
            out_ref[1] = turned.reshape(rows, across).astype(jnp.bfloat16)


def settle(which, copies, pairs):
    rows, across = copies[0].shape
    tile = math.gcd(rows, 256)
    row_count = len(copies)

    def pick(k):
        return lambda t, which_ref: (jnp.where(which_ref[0] == k, t, 0), 0)

    return pl.pallas_call(
        lambda *refs: settle_kernel(pairs, row_count, *refs),
        grid_spec=pltpu.PrefetchScalarGridSpec(
            num_scalar_prefetch=1,
            grid=(rows // tile,),
            in_specs=[pl.BlockSpec((tile, across), pick(k)) for k in range(row_count)],
            out_specs=pl.BlockSpec((2, tile, across), lambda t, _: (0, t, 0)),
        ),
        out_shape=jax.ShapeDtypeStruct((2, rows, across), jnp.bfloat16),
        compiler_params=pltpu.CompilerParams(vmem_limit_bytes=VMEM_LIMIT),
        cost_estimate=pl.CostEstimate(
            flops=0, bytes_accessed=8 * rows * across, transcendentals=0
        ),
        name="settle",
    )(which, *copies)


def contract_kernel(slot_count, shares, right_count, *refs):
    rights = refs[len(shares) * slot_count : len(shares) * slot_count + right_count]
    out_ref = refs[-1]
    row = pl.program_id(1)
    for k, share in enumerate(shares):
        start = sum(shares[:k])

        @pl.when((row >= start) & (row < start + share))
        def _():
            slots = refs[k * slot_count : (k + 1) * slot_count]
            parts, depth, width = slots[0].shape
            left = jnp.concatenate(
                [slot[...].reshape(parts * depth, width) for slot in slots], axis=1
            )
            for z in range(2):
                right = jnp.concatenate([ref[z] for ref in rights], axis=0)
                out_ref[z] = dot(left, right).reshape(out_ref.shape[1:])


def contract(result, lefts, rights, unit, row_first, wide, tile_first, steps, out_first):
    parts, _, width = lefts[0][0].shape
    slot_count = len(lefts[0])
    shares = [chunk[0].shape[1] // unit for chunk in lefts]
    depth = slot_count * width
    columns, side = wide * unit, EIGHTHS * unit
    alias = 0 if result is None else 1
    flops = 8 * parts * sum(shares) * unit * steps * columns * depth

    def place(start, share):
        return lambda c, r: (0, jnp.clip(r - start, 0, share - 1), 0)

    in_specs = [
        pl.BlockSpec((parts, unit, width), place(sum(shares[:k]), share))
        for k, share in enumerate(shares)
        for _ in range(slot_count)
    ]
    in_specs += [
        pl.BlockSpec((2, right.shape[1], columns), lambda c, r: (0, 0, tile_first + c))
        for right in rights
    ]
    if alias:
        in_specs.append(pl.BlockSpec(memory_space=pl.ANY))
    arrays = [slot for chunk in lefts for slot in chunk] + list(rights)
    return pl.pallas_call(
        lambda *refs: contract_kernel(slot_count, shares, len(rights), *refs),
        grid=(steps, sum(shares)),
        in_specs=in_specs,
        out_specs=pl.BlockSpec(
            (2, parts, unit, columns), lambda c, r: (0, 0, row_first + r, out_first + c)
        ),
        out_shape=jax.ShapeDtypeStruct((2, parts, side, side), jnp.float32),
        input_output_aliases={len(arrays): 0} if alias else {},
        compiler_params=pltpu.CompilerParams(vmem_limit_bytes=VMEM_LIMIT),
        cost_estimate=pl.CostEstimate(
            flops=flops, bytes_accessed=flops // depth, transcendentals=0
        ),
        name="contract",
    )(*arrays, *([result] if alias else []))


def energy_gaps(valence_energy, conduction_energy, band_pairs):
    valence_hot = (
        band_pairs[:, 0][:, None] == jnp.arange(valence_energy.shape[0], dtype=jnp.int32)[None, :]
    )
    conduction_hot = (
        band_pairs[:, 1][:, None]
        == jnp.arange(conduction_energy.shape[0], dtype=jnp.int32)[None, :]
    )
    return jnp.sum(jnp.where(valence_hot, valence_energy[None, :], 0.0), axis=1) - jnp.sum(
        jnp.where(conduction_hot, conduction_energy[None, :], 0.0), axis=1
    )


def after(value, *others):
    return lax.optimization_barrier((value,) + others)[0]


def body(valence, conduction, valence_energy, conduction_energy, band_pairs, grid_index):
    rows, cols = lax.axis_size("row"), lax.axis_size("col")
    row, col = lax.axis_index("row"), lax.axis_index("col")
    pairs = band_pairs.shape[0]
    features = 2 * pairs
    width = rows * features
    block = grid_index.shape[0] // cols
    parts = cols // rows
    unit = block // EIGHTHS
    me = row.astype(jnp.int32).reshape(1)
    my_part = (col % parts).astype(jnp.int32).reshape(1)
    owner = col // parts

    order = list(range(0, cols, 2)) + list(range(1, cols, 2))[::-1]
    ring_up = [(order[q], order[(q + 1) % cols]) for q in range(cols)]
    ring_down = [(b, a) for a, b in ring_up]
    my_place = jnp.asarray(np.argsort(np.array(order)), jnp.int32)[col]
    half = cols // 2
    offsets = [0]
    for t in range(1, half):
        offsets += [-t, t]
    offsets.append(half)
    sources = jnp.asarray(np.array(order), jnp.int32)[
        (my_place + jnp.asarray(np.array(offsets), jnp.int32)) % cols
    ]

    gap = energy_gaps(valence_energy, conduction_energy, band_pairs)
    scale = jnp.sqrt(-2.0 / (math.sqrt(pairs * rows * cols) * gap))

    position = table_position(grid_index).reshape(rows, parts, EIGHTHS, unit)
    positions = [
        position[:, :, first : first + share].reshape(-1) for first, share in CHUNKS
    ]
    sent, table = transform(valence, conduction, band_pairs, scale, positions[0], me, rows)

    def across_rows(parcels):
        return [parcels[0]] + [
            lax.ppermute(parcels[s], "row", [(r, r ^ s) for r in range(rows)])
            for s in range(1, rows)
        ]

    def go_round(below, above):
        return [lax.ppermute(below, "col", ring_up), lax.ppermute(above, "col", ring_down)]

    def last_round(below, above):
        cut = below.shape[0] // 2
        return [jnp.concatenate(go_round(below[:cut], above[cut:]), axis=0)]

    def column(slots, before=(), behind=(), flipped=None):
        slots = [after(slots[0], *before)] + slots[1:] if before else slots
        copies = [flip(slots, my_part, parts, unit) if flipped is None else flipped]
        for relation in range(1, rows):
            source = relation & (relation - 1)
            hop = relation ^ source
            held = copies[source]
            if source and behind:
                held = after(held, *behind)
            if hop == 1:
                copies.append(lax.ppermute(held, "row", [(r, r ^ 1) for r in range(rows)]))
                continue
            perm = [
                ((c // parts ^ source) * cols + c, (c // parts ^ relation) * cols + c)
                for c in range(cols)
            ]
            copies.append(lax.ppermute(held, ("row", "col"), perm))
        return copies

    which = (row ^ owner).astype(jnp.int32).reshape(1)

    own = assemble(across_rows(sent), me, features)
    one = [[own], go_round(own, own)]
    sent = select(after(table, own), positions[1], me, rows, features)
    one[1] = [after(block, *sent) for block in one[1]]
    own = assemble(across_rows([after(part, *one[1]) for part in sent]), me, features)
    one.append(go_round(*one[1]))
    copies = [column(sum(one[:2], []), (own,))]
    one[2] = [after(block, own, copies[0][0]) for block in one[2]]
    for t in range(3, half):
        one.append(go_round(*one[t - 1]))
    copies.append(column(sum(one[2 : half - 1], [])))
    below, above = [after(block, copies[1][0]) for block in one[half - 1]]
    copies.append(column(one[half - 1]))
    one.append(last_round(below, above))
    two = [[own], go_round(*[after(own, *one[half])] * 2)]
    copies.append(column(one[half], (), two[1]))
    rights = [settle(which, some, pairs) for some in copies]
    two.append(go_round(*[after(block, *rights[:2]) for block in two[1]]))

    def as_lefts(slots):
        return [slot.reshape(parts, -1, width) for slot in sum(slots, [])]

    lefts = as_lefts(one)
    wide = CHUNKS[0][1] // 2
    first = contract(None, [lefts], rights, unit, 0, wide, 0, 1, 0)
    two.append(go_round(*[after(block, first) for block in two[2]]))
    for t in range(4, half):
        two.append(go_round(*two[t - 1]))
    copies = [column(sum(two[:2], []), two[2] + [first])]
    lefts = [after(lefts[0], copies[0][0])] + lefts[1:]
    second = contract(first, [lefts], rights, unit, 0, wide, 1, 1, 1)
    two.append(last_round(*[after(block, second) for block in two[half - 1]]))
    share = CHUNKS[0][1]
    flipped = flip(two[half], my_part, parts, unit)
    both = [lefts, as_lefts(two)]
    both[1][0] = after(both[1][0], flipped)
    result = contract(second, both[1:], rights, unit, share, share, 0, 1, 0)
    copies.append(column(sum(two[2:half], []), two[half - 1] + [second], (result,)))
    copies.append(column(two[half], (), (result,), flipped))
    rights = [settle(which, some, pairs) for some in copies]
    result = contract(result, both, rights, unit, 0, share, 0, 1, 1)
    return result.reshape(2, parts * block, block)


def solution(mesh):
    return jax.shard_map(
        body,
        mesh=mesh,
        in_specs=(P(), P(), P(), P(), P(("row", "col"), None), P()),
        out_specs=P(None, "row", "col"),
        check_vma=False,
    )
```

```python
import math

import jax
import jax.numpy as jnp
import ml_dtypes
import numpy as np
from jax import lax
from jax.experimental import pallas as pl
from jax.experimental.pallas import tpu as pltpu
from jax.sharding import PartitionSpec as P

N1 = 32
N2 = 32
N3 = 32
NR = N1 * N2 * N3
LANES = 128
HI = N2 * N3 // LANES
LO = N2 // HI
ROWS = N1 * HI
VMEM_LIMIT = 58 * 1024 * 1024
CHUNKS = ((0, 4), (4, 4))
EIGHTHS = 8
GROUP = 4


def split_bf16(values):
    high = values.astype(ml_dtypes.bfloat16)
    low = (values - high.astype(np.float64)).astype(ml_dtypes.bfloat16)
    return high, low


def dft_tables():
    row = np.arange(ROWS)
    left = np.exp(
        -2j
        * np.pi
        * (
            (row[:, None] // HI) * (row[None, :] // HI) / N1
            + (row[:, None] % HI) * (row[None, :] % HI) / HI
        )
    )
    lane = np.arange(LANES)
    right = np.exp(
        -2j
        * np.pi
        * (
            (lane[:, None] // N3) * (lane[None, :] // N3) / LO
            + (lane[:, None] % N3) * (lane[None, :] % N3) / N3
        )
    )
    twiddle = np.exp(-2j * np.pi * (row[:, None] % HI) * (lane[None, :] // N3) / N2)
    twiddle = twiddle / math.sqrt(NR)
    left_full = np.block([[left.real, -left.imag], [left.imag, left.real]])
    right_full = np.block([[right.real, right.imag], [-right.imag, right.real]])
    left_high, left_low = split_bf16(left_full)
    right_high, right_low = split_bf16(right_full)
    twiddle = np.concatenate([twiddle] * GROUP, axis=1)
    return (
        np.concatenate([left_high, left_low, left_high], axis=1),
        np.concatenate([right_high, right_low], axis=1),
        np.stack([twiddle.real, twiddle.imag]).astype(np.float32),
    )


def table_position(grid_index):
    first = grid_index // (N2 * N3)
    second = grid_index // N3 % N2
    third = grid_index % N3
    return (first * HI + second % HI) * LANES + second // HI * N3 + third


def halves(value):
    high = value.astype(jnp.bfloat16)
    low = (value - high.astype(jnp.float32)).astype(jnp.bfloat16)
    return high, low


def dot(a, b):
    return jnp.dot(a, b, preferred_element_type=jnp.float32)


def select_rows(count, row_count, features, position_ref, me_ref, table, rows, outs):
    pack = LANES // features
    part = count // pack
    unroll = 32
    lane = lax.broadcasted_iota(jnp.int32, (part, LANES), 1)
    for s in range(row_count):
        base = (me_ref[0] ^ s) * count

        def some_rows(step, carry):
            first = step * unroll
            for j in range(unroll):
                index = position_ref[base + first + j]
                rows[pl.ds(first + j, 1), :] = table[pl.ds(index, 1), :]
            return carry

        lax.fori_loop(0, count // unroll, some_rows, 0)
        packed = rows[0:part, :]
        for k in range(1, pack):
            packed = jnp.where(lane >= k * features, rows[k * part : (k + 1) * part, :], packed)
        outs[s][...] = packed.astype(jnp.bfloat16)


def select_kernel(row_count, features, count, position_ref, me_ref, table_ref, *rest):
    select_rows(
        count, row_count, features, position_ref, me_ref, table_ref, rest[-1], rest[:row_count]
    )


def select(table, position, me, row_count, features):
    count = position.shape[0] // row_count
    shape = (count * features // LANES, LANES)
    return pl.pallas_call(
        lambda *refs: select_kernel(row_count, features, count, *refs),
        grid_spec=pltpu.PrefetchScalarGridSpec(
            num_scalar_prefetch=2,
            grid=(),
            in_specs=[pl.BlockSpec(memory_space=pltpu.VMEM)],
            out_specs=[pl.BlockSpec(memory_space=pltpu.VMEM)] * row_count,
            scratch_shapes=[pltpu.VMEM((count, LANES), jnp.float32)],
        ),
        out_shape=[jax.ShapeDtypeStruct(shape, jnp.bfloat16)] * row_count,
        compiler_params=pltpu.CompilerParams(vmem_limit_bytes=VMEM_LIMIT),
        cost_estimate=pl.CostEstimate(flops=0, bytes_accessed=50_000_000, transcendentals=0),
        name="select",
    )(position, me, table)


def transform_kernel(pairs, load_steps, step_rows, count, row_count, *refs):
    position_ref, me_ref, hot_c_ref, hot_v_ref, scale_ref, cond_ref, val_ref = refs[:7]
    left_ref, right_ref, twiddle_ref = refs[7:10]
    outs = refs[10 : 10 + row_count]
    table_ref, rho_r, rho_i, spec, table, middle, rows, sem = refs[10 + row_count :]
    step = pl.program_id(0)
    features = 2 * pairs

    cond = dot(hot_c_ref[...], cond_ref[...])
    val = dot(hot_v_ref[...], val_ref[...]) * scale_ref[...]
    cr, ci = cond[:pairs], cond[pairs:]
    vr, vi = val[:pairs], val[pairs:]
    real = vr * cr + vi * ci
    imag = vr * ci - vi * cr
    for a in range(step_rows):
        row = pl.multiple_of((step * step_rows + a) * pairs, pairs)
        rho_r[pl.ds(row, pairs), :] = real[:, a * LANES : (a + 1) * LANES]
        rho_i[pl.ds(row, pairs), :] = imag[:, a * LANES : (a + 1) * LANES]

    def left_half(group, slot):
        members = [GROUP * group + k for k in range(GROUP)]
        data = jnp.concatenate(
            [
                jnp.concatenate([ref[pl.ds(p, ROWS, stride=pairs), :] for p in members], axis=1)
                for ref in (rho_r, rho_i)
            ],
            axis=0,
        )
        high, low = halves(data)
        mixed = dot(left_ref[...], jnp.concatenate([high, high, low], axis=0))
        mid_r, mid_i = mixed[:ROWS], mixed[ROWS:]
        tr, ti = twiddle_ref[0], twiddle_ref[1]
        turn_r = mid_r * tr - mid_i * ti
        turn_i = mid_r * ti + mid_i * tr
        for k in range(GROUP):
            lanes = slice(k * LANES, (k + 1) * LANES)
            rows_k = slice(k * ROWS, (k + 1) * ROWS)
            for z, turned in enumerate((turn_r, turn_i)):
                high, low = halves(turned[:, lanes])
                middle[slot, rows_k, z * LANES : (z + 1) * LANES] = high
                middle[slot, rows_k, (2 + z) * LANES : (3 + z) * LANES] = low

    def right_half(group, slot):
        high = middle[slot, :, : 2 * LANES]
        low = middle[slot, :, 2 * LANES :]
        by_high = dot(high, right_ref[...])
        by_low = dot(low, right_ref[:, : 2 * LANES])
        out = by_high[:, : 2 * LANES] + (by_high[:, 2 * LANES :] + by_low)
        for k in range(GROUP):
            p = GROUP * group + k
            part = out[k * ROWS : (k + 1) * ROWS]
            spec[pl.ds(p, ROWS, stride=features), :] = part[:, :LANES]
            spec[pl.ds(pairs + p, ROWS, stride=features), :] = part[:, LANES:]

    @pl.when(step == load_steps - 1)
    def _():
        groups = pairs // GROUP
        left_half(0, 0)

        def two_groups(k, carry):
            right_half(2 * k, 0)
            left_half(2 * k + 1, 1)
            right_half(2 * k + 1, 1)
            left_half(jnp.minimum(2 * k + 2, groups - 1), 0)
            return carry

        lax.fori_loop(0, groups // 2, two_groups, 0)

        def one_row(k, carry):
            start = pl.multiple_of(k * features, features)
            tile = spec[pl.ds(start, features), :].astype(jnp.bfloat16)
            tile = jnp.concatenate([tile] * (LANES // features), axis=0)
            table[pl.ds(pl.multiple_of(k * LANES, LANES), LANES), :] = tile.T.astype(jnp.float32)
            return carry

        lax.fori_loop(0, ROWS, one_row, 0, unroll=8)
        keep = pltpu.make_async_copy(table, table_ref, sem)
        keep.start()
        select_rows(count, row_count, features, position_ref, me_ref, table, rows, outs)
        keep.wait()


def transform(valence, conduction, band_pairs, scale, position, me, row_count):
    count = position.shape[0] // row_count
    pairs = band_pairs.shape[0]
    features = 2 * pairs
    pack = LANES // features
    nvb, ncb = valence.shape[1], conduction.shape[1]
    load_steps = 8
    step_rows = ROWS // load_steps
    chunk = step_rows * LANES

    def hot(band, count):
        one = (band[:, None] == jnp.arange(count, dtype=jnp.int32)[None, :]).astype(jnp.bfloat16)
        none = jnp.zeros_like(one)
        return jnp.concatenate(
            [jnp.concatenate([one, none], axis=1), jnp.concatenate([none, one], axis=1)], axis=0
        )

    left, right, twiddle = dft_tables()
    whole = lambda shape: pl.BlockSpec(shape, lambda i, *_: (0,) * len(shape))
    loaded = lambda i, *_: (0, i)
    flops = 2 * pairs * (6 * ROWS * ROWS * 2 * LANES + 3 * ROWS * 4 * LANES * LANES)
    out_shapes = [(count // pack, LANES)] * row_count
    outs = pl.pallas_call(
        lambda *refs: transform_kernel(pairs, load_steps, step_rows, count, row_count, *refs),
        grid_spec=pltpu.PrefetchScalarGridSpec(
            num_scalar_prefetch=2,
            grid=(load_steps,),
            in_specs=[
                whole((2 * pairs, 2 * ncb)),
                whole((2 * pairs, 2 * nvb)),
                whole((2 * pairs, 1)),
                pl.BlockSpec((2 * ncb, chunk), loaded),
                pl.BlockSpec((2 * nvb, chunk), loaded),
                whole(left.shape),
                whole(right.shape),
                whole(twiddle.shape),
            ],
            out_specs=[whole(shape) for shape in out_shapes] + [pl.BlockSpec(memory_space=pl.ANY)],
            scratch_shapes=[
                pltpu.VMEM((ROWS * pairs, LANES), jnp.float32),
                pltpu.VMEM((ROWS * pairs, LANES), jnp.float32),
                pltpu.VMEM((ROWS * features, LANES), jnp.float32),
                pltpu.VMEM((NR, LANES), jnp.float32),
                pltpu.VMEM((2, GROUP * ROWS, 4 * LANES), jnp.bfloat16),
                pltpu.VMEM((count, LANES), jnp.float32),
                pltpu.SemaphoreType.DMA,
            ],
        ),
        out_shape=[jax.ShapeDtypeStruct(shape, jnp.bfloat16) for shape in out_shapes]
        + [jax.ShapeDtypeStruct((NR, LANES), jnp.float32)],
        compiler_params=pltpu.CompilerParams(vmem_limit_bytes=VMEM_LIMIT),
        cost_estimate=pl.CostEstimate(flops=flops, bytes_accessed=40_000_000, transcendentals=0),
        name="transform",
    )(
        position,
        me,
        hot(band_pairs[:, 1], ncb),
        hot(band_pairs[:, 0], nvb),
        jnp.concatenate([scale, scale])[:, None],
        conduction.reshape(2 * ncb, NR),
        valence.reshape(2 * nvb, NR),
        jnp.asarray(left),
        jnp.asarray(right),
        jnp.asarray(twiddle),
    )
    return outs[:row_count], outs[row_count]


def assemble_kernel(row_count, features, me_ref, *rest):
    parts, out_ref, held = rest[:row_count], rest[row_count], rest[row_count + 1]
    pack = LANES // features
    part = parts[0].shape[0]
    lane = lax.broadcasted_iota(jnp.int32, (part, LANES), 1)
    for s in range(row_count):
        held[s] = parts[s][...].astype(jnp.float32)
    for b in range(row_count // pack):
        for k in range(pack):
            block = None
            for q in range(pack):
                piece = held[(b * pack + q) ^ me_ref[0]]
                if q != k:
                    piece = pltpu.roll(piece, (q - k) * features % LANES, 1)
                block = piece if block is None else jnp.where(lane >= q * features, piece, block)
            out_ref[k * part : (k + 1) * part, b * LANES : (b + 1) * LANES] = block.astype(
                jnp.bfloat16
            )


def assemble(parts, me, features):
    row_count = len(parts)
    pack = LANES // features
    part = parts[0].shape[0]
    return pl.pallas_call(
        lambda *refs: assemble_kernel(row_count, features, *refs),
        grid_spec=pltpu.PrefetchScalarGridSpec(
            num_scalar_prefetch=1,
            grid=(),
            in_specs=[pl.BlockSpec(memory_space=pltpu.VMEM)] * row_count,
            out_specs=pl.BlockSpec(memory_space=pltpu.VMEM),
            scratch_shapes=[pltpu.VMEM((row_count, part, LANES), jnp.float32)],
        ),
        out_shape=jax.ShapeDtypeStruct((part * pack, row_count * features), jnp.bfloat16),
        compiler_params=pltpu.CompilerParams(vmem_limit_bytes=VMEM_LIMIT),
        cost_estimate=pl.CostEstimate(flops=0, bytes_accessed=2_000_000, transcendentals=0),
        name="assemble",
    )(me, *parts)


def flip_kernel(slot_count, part_ref, *refs):
    out_ref = refs[slot_count]
    for s in range(slot_count):
        width = refs[s].shape[1]
        out_ref[s * width : (s + 1) * width, :] = refs[s][...].T


def flip(slots, part, parts, unit):
    slot_count = len(slots)
    width = slots[0].shape[1]
    depth = slots[0].shape[0] // parts
    steps = depth // unit
    return pl.pallas_call(
        lambda *refs: flip_kernel(slot_count, *refs),
        grid_spec=pltpu.PrefetchScalarGridSpec(
            num_scalar_prefetch=1,
            grid=(steps,),
            in_specs=[
                pl.BlockSpec((unit, width), lambda t, part_ref: (part_ref[0] * steps + t, 0))
            ]
            * slot_count,
            out_specs=pl.BlockSpec((slot_count * width, unit), lambda t, part_ref: (0, t)),
        ),
        out_shape=jax.ShapeDtypeStruct((slot_count * width, depth), jnp.bfloat16),
        compiler_params=pltpu.CompilerParams(vmem_limit_bytes=VMEM_LIMIT),
        cost_estimate=pl.CostEstimate(
            flops=0, bytes_accessed=8 * slot_count * width * depth, transcendentals=0
        ),
        name="flip",
    )(part, *slots)


def settle_kernel(pairs, row_count, which_ref, *refs):
    out_ref = refs[row_count]
    kind = jnp.float32 if pairs % 16 else jnp.bfloat16
    for k in range(row_count):

        @pl.when(which_ref[0] == k)
        def _():
            values = -refs[k][...].astype(kind)
            rows, across = values.shape
            out_ref[0] = values.astype(jnp.bfloat16)
            values = values.reshape(rows // (2 * pairs), 2, pairs, across)
            turned = jnp.stack([values[:, 1], -values[:, 0]], axis=1)
            out_ref[1] = turned.reshape(rows, across).astype(jnp.bfloat16)


def settle(which, copies, pairs):
    rows, across = copies[0].shape
    tile = math.gcd(rows, 256)
    row_count = len(copies)

    def pick(k):
        return lambda t, which_ref: (jnp.where(which_ref[0] == k, t, 0), 0)

    return pl.pallas_call(
        lambda *refs: settle_kernel(pairs, row_count, *refs),
        grid_spec=pltpu.PrefetchScalarGridSpec(
            num_scalar_prefetch=1,
            grid=(rows // tile,),
            in_specs=[pl.BlockSpec((tile, across), pick(k)) for k in range(row_count)],
            out_specs=pl.BlockSpec((2, tile, across), lambda t, _: (0, t, 0)),
        ),
        out_shape=jax.ShapeDtypeStruct((2, rows, across), jnp.bfloat16),
        compiler_params=pltpu.CompilerParams(vmem_limit_bytes=VMEM_LIMIT),
        cost_estimate=pl.CostEstimate(
            flops=0, bytes_accessed=8 * rows * across, transcendentals=0
        ),
        name="settle",
    )(which, *copies)


def contract_kernel(slot_count, shares, right_count, *refs):
    rights = refs[len(shares) * slot_count : len(shares) * slot_count + right_count]
    out_ref = refs[-1]
    row = pl.program_id(1)
    for k, share in enumerate(shares):
        start = sum(shares[:k])

        @pl.when((row >= start) & (row < start + share))
        def _():
            slots = refs[k * slot_count : (k + 1) * slot_count]
            parts, depth, width = slots[0].shape
            left = jnp.concatenate(
                [slot[...].reshape(parts * depth, width) for slot in slots], axis=1
            )
            for z in range(2):
                right = jnp.concatenate([ref[z] for ref in rights], axis=0)
                out_ref[z] = dot(left, right).reshape(out_ref.shape[1:])


def contract(result, lefts, rights, unit, row_first, wide, tile_first, steps, out_first):
    parts, _, width = lefts[0][0].shape
    slot_count = len(lefts[0])
    shares = [chunk[0].shape[1] // unit for chunk in lefts]
    depth = slot_count * width
    columns, side = wide * unit, EIGHTHS * unit
    alias = 0 if result is None else 1
    flops = 8 * parts * sum(shares) * unit * steps * columns * depth

    def place(start, share):
        return lambda c, r: (0, jnp.clip(r - start, 0, share - 1), 0)

    in_specs = [
        pl.BlockSpec((parts, unit, width), place(sum(shares[:k]), share))
        for k, share in enumerate(shares)
        for _ in range(slot_count)
    ]
    in_specs += [
        pl.BlockSpec((2, right.shape[1], columns), lambda c, r: (0, 0, tile_first + c))
        for right in rights
    ]
    if alias:
        in_specs.append(pl.BlockSpec(memory_space=pl.ANY))
    arrays = [slot for chunk in lefts for slot in chunk] + list(rights)
    return pl.pallas_call(
        lambda *refs: contract_kernel(slot_count, shares, len(rights), *refs),
        grid=(steps, sum(shares)),
        in_specs=in_specs,
        out_specs=pl.BlockSpec(
            (2, parts, unit, columns), lambda c, r: (0, 0, row_first + r, out_first + c)
        ),
        out_shape=jax.ShapeDtypeStruct((2, parts, side, side), jnp.float32),
        input_output_aliases={len(arrays): 0} if alias else {},
        compiler_params=pltpu.CompilerParams(vmem_limit_bytes=VMEM_LIMIT),
        cost_estimate=pl.CostEstimate(
            flops=flops, bytes_accessed=flops // depth, transcendentals=0
        ),
        name="contract",
    )(*arrays, *([result] if alias else []))


def energy_gaps(valence_energy, conduction_energy, band_pairs):
    valence_hot = (
        band_pairs[:, 0][:, None] == jnp.arange(valence_energy.shape[0], dtype=jnp.int32)[None, :]
    )
    conduction_hot = (
        band_pairs[:, 1][:, None]
        == jnp.arange(conduction_energy.shape[0], dtype=jnp.int32)[None, :]
    )
    return jnp.sum(jnp.where(valence_hot, valence_energy[None, :], 0.0), axis=1) - jnp.sum(
        jnp.where(conduction_hot, conduction_energy[None, :], 0.0), axis=1
    )


def after(value, *others):
    return lax.optimization_barrier((value,) + others)[0]


def body(valence, conduction, valence_energy, conduction_energy, band_pairs, grid_index):
    rows, cols = lax.axis_size("row"), lax.axis_size("col")
    row, col = lax.axis_index("row"), lax.axis_index("col")
    pairs = band_pairs.shape[0]
    features = 2 * pairs
    width = rows * features
    block = grid_index.shape[0] // cols
    parts = cols // rows
    unit = block // EIGHTHS
    me = row.astype(jnp.int32).reshape(1)
    my_part = (col % parts).astype(jnp.int32).reshape(1)
    owner = col // parts

    order = list(range(0, cols, 2)) + list(range(1, cols, 2))[::-1]
    ring_up = [(order[q], order[(q + 1) % cols]) for q in range(cols)]
    ring_down = [(b, a) for a, b in ring_up]
    my_place = jnp.asarray(np.argsort(np.array(order)), jnp.int32)[col]
    half = cols // 2
    offsets = [0]
    for t in range(1, half):
        offsets += [-t, t]
    offsets.append(half)
    sources = jnp.asarray(np.array(order), jnp.int32)[
        (my_place + jnp.asarray(np.array(offsets), jnp.int32)) % cols
    ]

    gap = energy_gaps(valence_energy, conduction_energy, band_pairs)
    scale = jnp.sqrt(-2.0 / (math.sqrt(pairs * rows * cols) * gap))

    position = table_position(grid_index).reshape(rows, parts, EIGHTHS, unit)
    positions = [
        position[:, :, first : first + share].reshape(-1) for first, share in CHUNKS
    ]
    sent, table = transform(valence, conduction, band_pairs, scale, positions[0], me, rows)

    def across_rows(parcels):
        return [parcels[0]] + [
            lax.ppermute(parcels[s], "row", [(r, r ^ s) for r in range(rows)])
            for s in range(1, rows)
        ]

    def go_round(below, above):
        return [lax.ppermute(below, "col", ring_up), lax.ppermute(above, "col", ring_down)]

    def last_round(below, above):
        cut = below.shape[0] // 2
        return [jnp.concatenate(go_round(below[:cut], above[cut:]), axis=0)]

    def column(slots, before=(), behind=(), flipped=None):
        slots = [after(slots[0], *before)] + slots[1:] if before else slots
        copies = [flip(slots, my_part, parts, unit) if flipped is None else flipped]
        for relation in range(1, rows):
            source = relation & (relation - 1)
            hop = relation ^ source
            held = copies[source]
            if source and behind:
                held = after(held, *behind)
            if hop == 1:
                copies.append(lax.ppermute(held, "row", [(r, r ^ 1) for r in range(rows)]))
                continue
            perm = [
                ((c // parts ^ source) * cols + c, (c // parts ^ relation) * cols + c)
                for c in range(cols)
            ]
            copies.append(lax.ppermute(held, ("row", "col"), perm))
        return copies

    which = (row ^ owner).astype(jnp.int32).reshape(1)

    own = assemble(across_rows(sent), me, features)
    one = [[own], go_round(own, own)]
    sent = select(after(table, own), positions[1], me, rows, features)
    one[1] = [after(block, *sent) for block in one[1]]
    own = assemble(across_rows([after(part, *one[1]) for part in sent]), me, features)
    one.append(go_round(*one[1]))
    copies = [column(sum(one[:2], []), (own,))]
    one[2] = [after(block, own, copies[0][0]) for block in one[2]]
    for t in range(3, half):
        one.append(go_round(*one[t - 1]))
    copies.append(column(sum(one[2 : half - 1], [])))
    below, above = [after(block, copies[1][0]) for block in one[half - 1]]
    copies.append(column(one[half - 1]))
    one.append(last_round(below, above))
    two = [[own], go_round(*[after(own, *one[half])] * 2)]
    copies.append(column(one[half], (), two[1]))
    rights = [settle(which, some, pairs) for some in copies]
    two.append(go_round(*[after(block, *rights[:2]) for block in two[1]]))

    def as_lefts(slots):
        return [slot.reshape(parts, -1, width) for slot in sum(slots, [])]

    lefts = as_lefts(one)
    wide = CHUNKS[0][1] // 2
    first = contract(None, [lefts], rights, unit, 0, wide, 0, 1, 0)
    two.append(go_round(*[after(block, first) for block in two[2]]))
    for t in range(4, half):
        two.append(go_round(*two[t - 1]))
    copies = [column(sum(two[:2], []), two[2] + [first])]
    lefts = [after(lefts[0], copies[0][0])] + lefts[1:]
    second = contract(first, [lefts], rights, unit, 0, wide, 1, 1, 1)
    two.append(last_round(*[after(block, second) for block in two[half - 1]]))
    share = CHUNKS[0][1]
    flipped = flip(two[half], my_part, parts, unit)
    both = [lefts, as_lefts(two)]
    both[1][0] = after(both[1][0], flipped)
    result = contract(second, both[1:], rights, unit, share, share, 0, 1, 0)
    copies.append(column(sum(two[2:half], []), two[half - 1] + [second], (result,)))
    rights = [settle(which, some, pairs) for some in copies]
    copies.append(column(two[half], (), (result, *rights), flipped))
    rights.append(settle(which, copies[-1], pairs))
    result = contract(result, both, rights, unit, 0, share, 0, 1, 1)
    return result.reshape(2, parts * block, block)


def solution(mesh):
    return jax.shard_map(
        body,
        mesh=mesh,
        in_specs=(P(), P(), P(), P(), P(("row", "col"), None), P()),
        out_specs=P(None, "row", "col"),
        check_vma=False,
    )
```
